32 devices in a mesh: lon: 8 (over z, x), lat: 4 (over y, core).
Axes of the slice: x: 2, y: 2, z: 4, core: 2. Of those that a mesh axis runs over, the one named last changes fastest.
Arguments:
- inputs: bfloat16 [64, 128, 1024], P(None, 'lon', 'lat'), may hold values from -6 to 6
- weights: bfloat16 [2, 3, 3, 64, 64], replicated, may hold values from -0.25 to 0.25
- biases: float32 [2, 64], replicated, may hold values from -0.5 to 0.5
- cotangent: bfloat16 [64, 128, 1024], P(None, 'lon', 'lat'), may hold values from -6 to 6
Outputs:
- features_out: bfloat16 [64, 128, 1024], P(None, 'lon', 'lat')
- grad_input: bfloat16 [64, 128, 1024], P(None, 'lon', 'lat')
- weight_grads: float32 [2, 3, 3, 64, 64], replicated
- bias_grads: float32 [2, 64], replicated
The draws below stay inside these ranges and needn't reach their ends.
All inputs are finite; a program needn't handle non-finite values.
Results may differ from the reference program's by a relative error of at most 0.012.
Values may be sent and summed in bfloat16 or wider, within the bound.
No kernel may reach another device: no remote copies, remote signals or barrier semaphores. Data moves between devices by JAX's collectives and lax.ppermute only.
A program may use at most 64 MiB of HBM per device.

```python
import math
import jax
import jax.numpy as jnp
from jax import lax

CH = 64
LAYERS = 2
LON_DEV = 16
NLON = 128
NLAT = 1024


def level_of(key, extent, cuts, smallest, top_value):
    level = 1.0
    for axis_at, shards_of in cuts:
        steps = jax.random.uniform(jax.random.fold_in(jax.random.fold_in(key, 6), axis_at), (shards_of,), jnp.float32, smallest / len(cuts), top_value / len(cuts))
        level = level * jnp.repeat(jnp.exp(steps), extent[axis_at] // shards_of).reshape((-1,) + (1,) * (len(extent) - 1 - axis_at))
    return level


def gaussian(key, dims, spread, reach, shards=(), kind=jnp.bfloat16):
    array = jax.random.normal(key, dims, jnp.float32) * spread
    if len(shards) > 0:
        array = level_of(key, dims, shards, -0.22, 0.18) * array
    return jnp.clip(array, min=-reach, max=reach).astype(kind)


def setup_inputs(seed: int = 0) -> dict:
    seeds = jax.random.split(jax.random.key(seed), 5)
    return {
        "inputs": gaussian(seeds[0], (CH, NLON, NLAT), 1.0, 6.0, ((1, 8), (2, 4))),
        "weights": gaussian(seeds[1], (LAYERS, 3, 3, CH, CH), (9 * CH) ** -0.5, 0.25),
        "biases": jnp.clip(jax.random.uniform(seeds[2], (LAYERS, CH), jnp.float32, -0.5, 0.5), -0.5, 0.5),
        "cotangent": gaussian(seeds[3], (CH, NLON, NLAT), 1.0, 6.0, ((1, 8), (2, 4))),
    }


def shifted(field, lon_off, lat_off):
    rolled = jnp.roll(field, -lon_off, axis=1)
    if lat_off > 0:
        zeros = jnp.zeros(rolled.shape[:2] + (lat_off,), rolled.dtype)
        return jnp.concatenate([rolled[:, :, lat_off:], zeros], axis=2)
    if lat_off < 0:
        zeros = jnp.zeros(rolled.shape[:2] + (-lat_off,), rolled.dtype)
        return jnp.concatenate([zeros, rolled[:, :, :lat_off]], axis=2)
    return rolled

def convolve(field, kernels, dilation, sign, transpose_kernel):
    channels = field.shape[0]
    total = jnp.zeros((channels, field.shape[1] * field.shape[2]), jnp.float32)
    for outer_tap in range(3):
        for inner_tap in range(3):
            piece = shifted(field, sign * (outer_tap - 1) * dilation, sign * (inner_tap - 1) * dilation)
            kernel = kernels[outer_tap, inner_tap]
            if transpose_kernel:
                kernel = kernel.T
            total = total + jnp.dot(kernel, piece.reshape(channels, -1), preferred_element_type=jnp.float32)
    return total.reshape(field.shape)

def slope_of(pre):
    sigma = jax.nn.sigmoid(pre)
    return sigma * (1.0 + pre * (1.0 - sigma))

def reference(inputs, weights, biases, cotangent):
    channels = inputs.shape[0]
    scale = 1.0 / math.sqrt(NLON * NLAT)
    layer_count = weights.shape[0]
    states = [inputs]
    pres = []
    current = inputs
    for layer_idx in range(layer_count):
        dilation = LON_DEV * 2 ** layer_idx
        pre = convolve(current, weights[layer_idx], dilation, 1, False) + biases[layer_idx][:, None, None]
        pres.append(pre)
        current = jax.nn.silu(pre).astype(jnp.bfloat16)
        states.append(current)
    upstream = cotangent
    weight_list = [None] * layer_count
    bias_list = [None] * layer_count
    for layer_idx in reversed(range(layer_count)):
        dilation = LON_DEV * 2 ** layer_idx
        gated = (upstream.astype(jnp.float32) * slope_of(pres[layer_idx])).astype(jnp.bfloat16)
        flat = gated.reshape(channels, -1)
        rows_w = []
        for outer_tap in range(3):
            row_taps = []
            for inner_tap in range(3):
                piece = shifted(states[layer_idx], (outer_tap - 1) * dilation, (inner_tap - 1) * dilation)
                term = lax.dot_general(flat, piece.reshape(channels, -1), (((1,), (1,)), ((), ())), preferred_element_type=jnp.float32)
                row_taps.append(term * scale)
            rows_w.append(jnp.stack(row_taps))
        weight_list[layer_idx] = jnp.stack(rows_w)
        bias_list[layer_idx] = lax.optimization_barrier(jnp.sum(flat.astype(jnp.float32), axis=1)) * scale
        upstream = convolve(gated, weights[layer_idx], dilation, -1, True).astype(jnp.bfloat16)
    return (current, upstream, jnp.stack(weight_list), jnp.stack(bias_list))
```

```python
import functools
import math

import jax
import jax.numpy as jnp
import numpy as np
from jax import lax
from jax.experimental import pallas as pl
from jax.experimental.pallas import tpu as pltpu
from jax.sharding import PartitionSpec as P


AXES = ("lon", "lat")
LANES = 128
PARAMS = pltpu.CompilerParams(vmem_limit_bytes=48 * 2**20)


def lane_order(cols, lat_rows, share):
    steps = lat_rows // cols
    place = np.arange(lat_rows)
    group, rest = place // (steps * share), place % (steps * share)
    source = (rest // share) * cols + group * share + rest % share
    matrix = np.zeros((lat_rows, lat_rows), np.float32)
    matrix[source, place] = 1.0
    return matrix


def pack_kernel(field_ref, order_ref, out_ref, rows_ref):
    channels, cols, lat_rows = field_ref.shape
    devices, _, width = out_ref.shape
    groups = devices // cols
    rows = field_ref[...].reshape(channels * cols, lat_rows)
    rows = jnp.dot(rows, order_ref[...], preferred_element_type=jnp.float32)
    halves = lat_rows // LANES
    for half in range(halves):
        rows_ref[half] = rows[:, half * LANES : (half + 1) * LANES]
    for col in range(cols):
        column = jnp.concatenate(
            [rows_ref[half, pl.ds(col, channels, stride=cols), :] for half in range(halves)], axis=1
        ).astype(out_ref.dtype)
        for group in range(groups):
            out_ref[col * groups + group] = column[:, group * width : (group + 1) * width]


def unpack_kernel(parts_ref, order_ref, out_ref, rows_ref):
    channels, cols, lat_rows = out_ref.shape
    devices, _, width = parts_ref.shape
    groups = devices // cols
    for col in range(cols):
        column = jnp.concatenate([parts_ref[col * groups + g] for g in range(groups)], axis=1)
        column = jnp.dot(column, order_ref[...], preferred_element_type=jnp.float32)
        for half in range(lat_rows // LANES):
            rows_ref[half, pl.ds(col, channels, stride=cols), :] = column[
                :, half * LANES : (half + 1) * LANES
            ]
    for half in range(lat_rows // LANES):
        out_ref[:, :, half * LANES : (half + 1) * LANES] = (
            rows_ref[half].astype(out_ref.dtype).reshape(channels, cols, LANES)
        )


def taps(row, shift):
    edge = jnp.zeros((row.shape[0], shift), row.dtype)
    before = jnp.concatenate([edge, row[:, :-shift]], axis=1)
    after = jnp.concatenate([row[:, shift:], edge], axis=1)
    return before, row, after


def line_of(ref, idx):
    blocks = ref.shape[1]
    return jnp.concatenate([ref[idx, k] for k in range(blocks)], axis=1)


def forward_kernel(share, x_ref, w_ref, b_ref, feat_ref, h_ref, s0_ref, s1_ref, y_ref):
    count, blocks, channels, width = x_ref.shape
    for layer in range(2):
        hops = 2**layer
        kernel = jnp.concatenate(
            [
                jnp.concatenate([w_ref[layer, a, b] for b in range(3)], axis=1)
                for a in range(3)
            ],
            axis=0,
        )
        for i in range(count):
            line = line_of(x_ref, i) if layer == 0 else h_ref[i]
            stack = jnp.concatenate(taps(line, hops * share), axis=0)
            y_ref[i] = jnp.dot(kernel, stack, preferred_element_type=jnp.float32)
        bias = b_ref[layer]
        for i in range(count):
            pre = bias + y_ref[i, channels : 2 * channels]
            pre = pre + y_ref[(i - hops) % count, :channels]
            pre = pre + y_ref[(i + hops) % count, 2 * channels :]
            sigma = 1.0 / (1.0 + jnp.exp(-pre))
            state = pre * sigma
            slope = sigma * (1.0 + pre * (1.0 - sigma))
            if layer == 0:
                h_ref[i] = state.astype(h_ref.dtype)
                s0_ref[i] = slope
            else:
                s1_ref[i] = slope
                state = state.astype(feat_ref.dtype)
                for k in range(blocks):
                    feat_ref[i, k] = state[:, k * width : (k + 1) * width]


def backward_kernel(
    share, cot_ref, x_ref, h_ref, s0_ref, s1_ref, w_ref, grad_ref, sums_ref, bias_ref, y_ref, g_ref
):
    count, blocks, channels, width = x_ref.shape
    for layer in (1, 0):
        hops = 2**layer
        kernel = jnp.concatenate(
            [
                jnp.concatenate([w_ref[layer, a, b].astype(jnp.float32).T for b in range(3)], axis=1)
                for a in range(3)
            ],
            axis=0,
        ).astype(jnp.bfloat16)
        total = jnp.zeros((3 * channels, 3 * channels), jnp.float32)
        bias = jnp.zeros((channels, 1), jnp.float32)
        for i in range(count):
            if layer == 1:
                gated = (line_of(cot_ref, i).astype(jnp.float32) * s1_ref[i]).astype(jnp.bfloat16)
            else:
                gated = g_ref[i]
            bias = bias + jnp.sum(gated.astype(jnp.float32), axis=1, keepdims=True)
            before, here, after = taps(gated, hops * share)
            stack = jnp.concatenate([after, here, before], axis=0)
            y_ref[i] = jnp.dot(kernel, stack, preferred_element_type=jnp.float32)
            around = [(i + (a - 1) * hops) % count for a in range(3)]
            lines = jnp.concatenate(
                [line_of(x_ref, j) if layer == 0 else h_ref[j] for j in around], axis=0
            )
            total = total + lax.dot_general(
                stack, lines, (((1,), (1,)), ((), ())), preferred_element_type=jnp.float32
            )
        sums_ref[layer] = total
        bias_ref[layer] = bias
        for i in range(count):
            g = y_ref[i, channels : 2 * channels]
            g = g + y_ref[(i + hops) % count, :channels]
            g = g + y_ref[(i - hops) % count, 2 * channels :]
            g = g.astype(jnp.bfloat16)
            if layer == 1:
                g_ref[i] = (g.astype(jnp.float32) * s0_ref[i]).astype(jnp.bfloat16)
            else:
                for k in range(blocks):
                    grad_ref[i, k] = g[:, k * width : (k + 1) * width]


def to_owner(packed):
    return lax.all_to_all(packed, AXES, 0, 0, tiled=True)


def local(inputs, weights, biases, cotangent):
    channels, cols, lat_rows = inputs.shape
    lons, lats = lax.axis_size("lon"), lax.axis_size("lat")
    devices = lons * lats
    share = cols * cols // devices
    steps = lat_rows // cols
    width = steps * share
    scale = 1.0 / math.sqrt(cols * lons * lat_rows * lats)
    order = lane_order(cols, lat_rows, share)
    into = jnp.asarray(order, jnp.bfloat16)
    back = jnp.asarray(order.T, jnp.bfloat16)
    bf16, f32 = jnp.bfloat16, jnp.float32
    blocks, chunk = (lats, width) if width % LANES == 0 else (1, lats * width)

    def pack(field):
        return pl.pallas_call(
            pack_kernel,
            out_shape=jax.ShapeDtypeStruct((devices, channels, width), bf16),
            scratch_shapes=[pltpu.VMEM((lat_rows // LANES, channels * cols, LANES), f32)],
            compiler_params=PARAMS,
        )(field, into)

    def unpack(parts):
        return pl.pallas_call(
            unpack_kernel,
            out_shape=jax.ShapeDtypeStruct((channels, cols, lat_rows), bf16),
            scratch_shapes=[pltpu.VMEM((lat_rows // LANES, channels * cols, LANES), f32)],
            compiler_params=PARAMS,
        )(parts, back)

    def arrived(parts):
        parts = parts.reshape(lons, lats, channels, width)
        if blocks == 1:
            parts = parts.transpose(0, 2, 1, 3).reshape(lons, 1, channels, chunk)
        return parts

    def leaving(parts):
        if blocks == 1:
            parts = parts.reshape(lons, channels, lats, width).transpose(0, 2, 1, 3)
        return parts.reshape(devices, channels, width)

    cells = (lons, channels, lats * width)
    x = arrived(to_owner(pack(inputs)))
    cot = arrived(to_owner(pack(cotangent)))
    features, hidden, slope0, slope1 = pl.pallas_call(
        functools.partial(forward_kernel, share),
        out_shape=[
            jax.ShapeDtypeStruct(x.shape, bf16),
            jax.ShapeDtypeStruct(cells, bf16),
            jax.ShapeDtypeStruct(cells, f32),
            jax.ShapeDtypeStruct(cells, f32),
        ],
        scratch_shapes=[pltpu.VMEM((lons, 3 * channels, lats * width), f32)],
        compiler_params=PARAMS,
    )(x, weights, biases[:, :, None])
    features_out = unpack(to_owner(leaving(features)))
    grads, sums, bias_sums = pl.pallas_call(
        functools.partial(backward_kernel, share),
        out_shape=[
            jax.ShapeDtypeStruct(x.shape, bf16),
            jax.ShapeDtypeStruct((2, 3 * channels, 3 * channels), f32),
            jax.ShapeDtypeStruct((2, channels, 1), f32),
        ],
        scratch_shapes=[
            pltpu.VMEM((lons, 3 * channels, lats * width), f32),
            pltpu.VMEM(cells, bf16),
        ],
        compiler_params=PARAMS,
    )(cot, x, hidden, slope0, slope1, weights)
    grad_input = unpack(to_owner(leaving(grads)))

    entries = jnp.concatenate([sums.reshape(-1), jnp.zeros((-sums.size) % devices, f32)])
    pieces = entries.reshape(devices, -1)
    bias_row = jnp.broadcast_to(bias_sums.reshape(1, -1), (devices, 2 * channels))
    got = to_owner(jnp.concatenate([pieces, bias_row], axis=1))
    got = jnp.sum(got, axis=0) * scale
    bias_grads = got[pieces.shape[1] :].reshape(2, channels)
    mine = got[: pieces.shape[1]]
    full = to_owner(jnp.broadcast_to(mine[None], pieces.shape)).reshape(-1)[: sums.size]
    weight_grads = full.reshape(2, 3, channels, 3, channels).transpose(0, 3, 1, 2, 4)
    return features_out, grad_input, weight_grads, bias_grads


def solution(mesh):
    in_specs = (P(None, "lon", "lat"), P(), P(), P(None, "lon", "lat"))
    out_specs = (P(None, "lon", "lat"), P(None, "lon", "lat"), P(), P())
    return jax.shard_map(local, mesh=mesh, in_specs=in_specs, out_specs=out_specs, check_vma=False)
```

```python
import functools
import math

import jax
import jax.numpy as jnp
import numpy as np
from jax import lax
from jax.experimental import pallas as pl
from jax.experimental.pallas import tpu as pltpu
from jax.sharding import PartitionSpec as P


AXES = ("lon", "lat")
LANES = 128
BF16, F32 = jnp.bfloat16, jnp.float32
PARAMS = pltpu.CompilerParams(vmem_limit_bytes=48 * 2**20)


def lane_order(cols, lat_rows, share):
    steps = lat_rows // cols
    place = np.arange(lat_rows)
    group, rest = place // (steps * share), place % (steps * share)
    source = (rest // share) * cols + group * share + rest % share
    matrix = np.zeros((lat_rows, lat_rows), np.float32)
    matrix[source, place] = 1.0
    return matrix


def pack_kernel(x_ref, cot_ref, order_ref, out_ref, x_buf, cot_buf, rows_ref, sems):
    channels, cols, lat_rows = x_ref.shape
    devices, _, width = out_ref.shape
    groups = devices // cols
    halves = lat_rows // LANES
    copies = [
        pltpu.make_async_copy(ref, buf, sems.at[at])
        for at, (ref, buf) in enumerate(((x_ref, x_buf), (cot_ref, cot_buf)))
    ]
    for copy in copies:
        copy.start()
    for at, buf in enumerate((x_buf, cot_buf)):
        copies[at].wait()
        rows = buf[...].reshape(channels * cols, lat_rows)
        rows = jnp.dot(rows, order_ref[...], preferred_element_type=F32)
        for half in range(halves):
            rows_ref[half] = rows[:, half * LANES : (half + 1) * LANES]
        for col in range(cols):
            column = jnp.concatenate(
                [rows_ref[half, pl.ds(col, channels, stride=cols), :] for half in range(halves)],
                axis=1,
            ).astype(BF16)
            for group in range(groups):
                out_ref[col * groups + group, at * channels : (at + 1) * channels, :] = column[
                    :, group * width : (group + 1) * width
                ]


def unpack_kernel(parts_ref, order_ref, feat_ref, grad_ref, rows_ref):
    channels, cols, lat_rows = feat_ref.shape
    devices, _, width = parts_ref.shape
    groups = devices // cols
    halves = lat_rows // LANES
    for at, out_ref in enumerate((feat_ref, grad_ref)):
        for col in range(cols):
            column = jnp.concatenate(
                [
                    parts_ref[col * groups + g, at * channels : (at + 1) * channels, :]
                    for g in range(groups)
                ],
                axis=1,
            )
            column = jnp.dot(column, order_ref[...], preferred_element_type=F32)
            for half in range(halves):
                rows_ref[half, pl.ds(col, channels, stride=cols), :] = column[
                    :, half * LANES : (half + 1) * LANES
                ]
        for half in range(halves):
            out_ref[:, :, half * LANES : (half + 1) * LANES] = (
                rows_ref[half].astype(BF16).reshape(channels, cols, LANES)
            )


def taps(row, shift):
    edge = jnp.zeros((row.shape[0], shift), row.dtype)
    before = jnp.concatenate([edge, row[:, :-shift]], axis=1)
    after = jnp.concatenate([row[:, shift:], edge], axis=1)
    return before, row, after


def stack_kernel(share, merged, parts_ref, w_ref, b_ref, *refs):
    if merged:
        out_ref, s0_ref, s1_ref, h_ref, y_ref, g_ref, sums_ref = refs
        first = 2 * w_ref.shape[-1]
        pieces_ref = out_ref
    else:
        out_ref, pieces_ref, s0_ref, s1_ref, h_ref, y_ref, g_ref, sums_ref = refs
        first = 0
    count = h_ref.shape[0]
    channels = w_ref.shape[-1]
    devices, _, width = parts_ref.shape
    blocks = devices // count

    def line_of(field, i):
        rows = slice(field * channels, (field + 1) * channels)
        return jnp.concatenate([parts_ref[i * blocks + k, rows, :] for k in range(blocks)], axis=1)

    def put(field, i, line):
        rows = slice(field * channels, (field + 1) * channels)
        for k in range(blocks):
            out_ref[i * blocks + k, rows, :] = line[:, k * width : (k + 1) * width]

    for layer in range(2):
        hops = 2**layer
        kernel = jnp.concatenate(
            [
                jnp.concatenate([w_ref[layer, a, b] for b in range(3)], axis=1)
                for a in range(3)
            ],
            axis=0,
        )
        for i in range(count):
            line = line_of(0, i) if layer == 0 else h_ref[i]
            stack = jnp.concatenate(taps(line, hops * share), axis=0)
            y_ref[i] = jnp.dot(kernel, stack, preferred_element_type=F32)
        bias = b_ref[layer]
        for i in range(count):
            pre = bias + y_ref[i, channels : 2 * channels]
            pre = pre + y_ref[(i - hops) % count, :channels]
            pre = pre + y_ref[(i + hops) % count, 2 * channels :]
            sigma = 1.0 / (1.0 + jnp.exp(-pre))
            state = (pre * sigma).astype(BF16)
            slope = sigma * (1.0 + pre * (1.0 - sigma))
            if layer == 0:
                h_ref[i] = state
                s0_ref[i] = slope
            else:
                s1_ref[i] = slope
                put(0, i, state)

    ones = jnp.ones((16, blocks * width), BF16)
    bias_rows = [None, None]
    for layer in (1, 0):
        hops = 2**layer
        kernel = jnp.concatenate(
            [
                jnp.concatenate([w_ref[layer, a, b].astype(F32).T for b in range(3)], axis=1)
                for a in range(3)
            ],
            axis=0,
        ).astype(BF16)
        total = jnp.zeros((3 * channels, 3 * channels), F32)
        bias = jnp.zeros((16, channels), F32)
        for i in range(count):
            if layer == 1:
                gated = (line_of(1, i).astype(F32) * s1_ref[i]).astype(BF16)
            else:
                gated = g_ref[i]
            bias = bias + lax.dot_general(
                ones, gated, (((1,), (1,)), ((), ())), preferred_element_type=F32
            )
            before, here, after = taps(gated, hops * share)
            stack = jnp.concatenate([after, here, before], axis=0)
            y_ref[i] = jnp.dot(kernel, stack, preferred_element_type=F32)
            around = [(i + (a - 1) * hops) % count for a in range(3)]
            lines = jnp.concatenate(
                [line_of(0, j) if layer == 0 else h_ref[j] for j in around], axis=0
            )
            total = total + lax.dot_general(
                stack, lines, (((1,), (1,)), ((), ())), preferred_element_type=F32
            )
        high = 3 * channels
        sums_ref[layer * high : (layer + 1) * high, :] = total[:, : 2 * channels]
        sums_ref[2 * high : 3 * high, layer * channels : (layer + 1) * channels] = total[
            :, 2 * channels :
        ]
        bias_rows[layer] = bias[:1]
        for i in range(count):
            g = y_ref[i, channels : 2 * channels]
            g = g + y_ref[(i + hops) % count, :channels]
            g = g + y_ref[(i - hops) % count, 2 * channels :]
            g = g.astype(BF16)
            if layer == 1:
                g_ref[i] = (g.astype(F32) * s0_ref[i]).astype(BF16)
            else:
                put(1, i, g)

    used = -(-9 * channels // devices)
    held = sums_ref.shape[0] - 9 * channels
    sums_ref[9 * channels :, :] = jnp.zeros((held, 2 * channels), F32)
    size = pieces_ref.shape[1] - first
    bias = jnp.concatenate(bias_rows, axis=1)
    high = bias.astype(BF16).astype(F32)
    low = bias - high
    row = lax.broadcasted_iota(jnp.int32, (size, 2 * channels), 0)
    for p in range(devices):
        piece = sums_ref[used * p : used * p + size, :]
        piece = jnp.where(row < used, piece, jnp.where(row == used, high, low))
        pieces_ref[p, first:, :] = piece.astype(BF16)


def reduce_kernel(scale, used, first, got_ref, mine_ref, bias_ref):
    devices, size, lanes = mine_ref.shape
    total = got_ref[0, first:, :].astype(F32)
    for p in range(1, devices):
        total = total + got_ref[p, first:, :].astype(F32)
    total = total * scale
    bias = total[used : used + 1] + total[used + 1 : used + 2]
    bias_ref[0:1, :] = bias[:, : lanes // 2]
    bias_ref[1:2, :] = bias[:, lanes // 2 :]
    total = total.astype(BF16)
    for p in range(devices):
        mine_ref[p] = total


def assemble_kernel(used, parts_ref, out_ref, rows_ref):
    devices = parts_ref.shape[0]
    channels = out_ref.shape[-1]
    for p in range(devices):
        rows_ref[used * p : used * (p + 1), :] = parts_ref[p].astype(F32)[:used]
    high = 3 * channels
    for layer in range(2):
        for b in range(3):
            pair = rows_ref[layer * high + b * channels : layer * high + (b + 1) * channels, :]
            out_ref[layer, 0, b] = pair[:, :channels]
            out_ref[layer, 1, b] = pair[:, channels:]
            third = rows_ref[2 * high + b * channels : 2 * high + (b + 1) * channels, :]
            out_ref[layer, 2, b] = third[:, layer * channels : (layer + 1) * channels]


def exchanged(parts):
    return lax.all_to_all(parts, AXES, 0, 0, tiled=True)


def local(inputs, weights, biases, cotangent):
    channels, cols, lat_rows = inputs.shape
    lons, lats = lax.axis_size("lon"), lax.axis_size("lat")
    devices = lons * lats
    share = cols * cols // devices
    width = lat_rows // cols * share
    span = lats * width
    scale = 1.0 / math.sqrt(cols * lons * lat_rows * lats)
    order = lane_order(cols, lat_rows, share)
    into = jnp.asarray(order, BF16)
    back = jnp.asarray(order.T, BF16)
    merged = width == LANES
    used = -(-9 * channels // devices)
    size = -(-(used + 2) // 8) * 8
    shape = jax.ShapeDtypeStruct
    rows = pltpu.VMEM((lat_rows // LANES, channels * cols, LANES), F32)

    packed = pl.pallas_call(
        pack_kernel,
        out_shape=shape((devices, 2 * channels, width), BF16),
        in_specs=[
            pl.BlockSpec(memory_space=pl.ANY),
            pl.BlockSpec(memory_space=pl.ANY),
            pl.BlockSpec(memory_space=pltpu.VMEM),
        ],
        scratch_shapes=[
            pltpu.VMEM(inputs.shape, BF16),
            pltpu.VMEM(inputs.shape, BF16),
            rows,
            pltpu.SemaphoreType.DMA((2,)),
        ],
        compiler_params=PARAMS,
    )(inputs, cotangent, into)
    parts = exchanged(packed)
    if not merged:
        parts = parts.reshape(lons, lats, 2 * channels, width).transpose(0, 2, 1, 3)
        parts = parts.reshape(lons, 2 * channels, span)

    cells = (lons, channels, span)
    pieces_shape = (devices, size, 2 * channels)
    if merged:
        out_shape = [shape((devices, 2 * channels + size, width), BF16)]
    else:
        out_shape = [shape(parts.shape, BF16), shape(pieces_shape, BF16)]
    results = pl.pallas_call(
        functools.partial(stack_kernel, share, merged),
        out_shape=out_shape,
        scratch_shapes=[
            pltpu.VMEM(cells, F32),
            pltpu.VMEM(cells, F32),
            pltpu.VMEM(cells, BF16),
            pltpu.VMEM((lons, 3 * channels, span), F32),
            pltpu.VMEM(cells, BF16),
            pltpu.VMEM((used * devices + size, 2 * channels), F32),
        ],
        compiler_params=PARAMS,
    )(parts, weights, biases[:, :, None])
    if merged:
        home = exchanged(results[0])
        got, first = home, 2 * channels
    else:
        home = results[0].reshape(lons, 2 * channels, lats, width).transpose(0, 2, 1, 3)
        home = exchanged(home.reshape(devices, 2 * channels, width))
        got, first = exchanged(results[1]), 0

    mine, bias_grads = pl.pallas_call(
        functools.partial(reduce_kernel, scale, used, first),
        out_shape=[shape(pieces_shape, BF16), shape(biases.shape, F32)],
        compiler_params=PARAMS,
    )(got)
    home, mine = lax.optimization_barrier((home, mine))
    full = exchanged(mine)
    features_out, grad_input = pl.pallas_call(
        unpack_kernel,
        out_shape=[shape(inputs.shape, BF16), shape(inputs.shape, BF16)],
        scratch_shapes=[rows],
        compiler_params=PARAMS,
        cost_estimate=pl.CostEstimate(
            flops=4 * inputs.size * lat_rows, bytes_accessed=8 * inputs.size, transcendentals=0
        ),
    )(home, back)
    weight_grads = pl.pallas_call(
        functools.partial(assemble_kernel, used),
        out_shape=shape(weights.shape, F32),
        scratch_shapes=[pltpu.VMEM((used * devices, 2 * channels), F32)],
        compiler_params=PARAMS,
    )(full)
    return features_out, grad_input, weight_grads, bias_grads


def solution(mesh):
    in_specs = (P(None, "lon", "lat"), P(), P(), P(None, "lon", "lat"))
    out_specs = (P(None, "lon", "lat"), P(None, "lon", "lat"), P(), P())
    return jax.shard_map(local, mesh=mesh, in_specs=in_specs, out_specs=out_specs, check_vma=False)
```

```python
import functools
import math

import jax
import jax.numpy as jnp
from jax import lax
from jax.experimental import pallas as pl
from jax.experimental.pallas import tpu as pltpu
from jax.sharding import PartitionSpec as P


AXES = ("lon", "lat")
LANES = 128
BF16, F32 = jnp.bfloat16, jnp.float32
PARAMS = pltpu.CompilerParams(vmem_limit_bytes=48 * 2**20)


def lane_order(cols, lat_rows, share, inverse):
    steps = lat_rows // cols
    place = lax.broadcasted_iota(jnp.int32, (lat_rows, lat_rows), 0 if inverse else 1)
    source = lax.broadcasted_iota(jnp.int32, (lat_rows, lat_rows), 1 if inverse else 0)
    group = lax.div(source & (cols - 1), share)
    wanted = (group * steps + lax.div(source, cols)) * share + (source & (share - 1))
    return (place == wanted).astype(F32).astype(BF16)


def pack_kernel(share, x_ref, cot_ref, out_ref, x_buf, cot_buf, rows_ref, sems):
    channels, cols, lat_rows = x_ref.shape
    devices, _, width = out_ref.shape
    groups = devices // cols
    halves = lat_rows // LANES
    copies = [
        pltpu.make_async_copy(ref, buf, sems.at[at])
        for at, (ref, buf) in enumerate(((x_ref, x_buf), (cot_ref, cot_buf)))
    ]
    for copy in copies:
        copy.start()
    order = lane_order(cols, lat_rows, share, False)
    for at, buf in enumerate((x_buf, cot_buf)):
        copies[at].wait()
        rows = buf[...].reshape(channels * cols, lat_rows)
        rows = jnp.dot(rows, order, preferred_element_type=F32)
        for half in range(halves):
            rows_ref[half] = rows[:, half * LANES : (half + 1) * LANES]
        for col in range(cols):
            column = jnp.concatenate(
                [rows_ref[half, pl.ds(col, channels, stride=cols), :] for half in range(halves)],
                axis=1,
            ).astype(BF16)
            for group in range(groups):
                out_ref[col * groups + group, at * channels : (at + 1) * channels, :] = column[
                    :, group * width : (group + 1) * width
                ]


def unpack_kernel(share, parts_ref, feat_ref, grad_ref, rows_ref):
    channels, cols, lat_rows = feat_ref.shape
    devices, _, width = parts_ref.shape
    groups = devices // cols
    halves = lat_rows // LANES
    order = lane_order(cols, lat_rows, share, True)
    for at, out_ref in enumerate((feat_ref, grad_ref)):
        for col in range(cols):
            column = jnp.concatenate(
                [
                    parts_ref[col * groups + g, at * channels : (at + 1) * channels, :]
                    for g in range(groups)
                ],
                axis=1,
            )
            column = jnp.dot(column, order, preferred_element_type=F32)
            for half in range(halves):
                rows_ref[half, pl.ds(col, channels, stride=cols), :] = column[
                    :, half * LANES : (half + 1) * LANES
                ]
        for half in range(halves):
            out_ref[:, :, half * LANES : (half + 1) * LANES] = (
                rows_ref[half].astype(BF16).reshape(channels, cols, LANES)
            )


def taps(row, shift):
    edge = jnp.zeros((row.shape[0], shift), row.dtype)
    before = jnp.concatenate([edge, row[:, :-shift]], axis=1)
    after = jnp.concatenate([row[:, shift:], edge], axis=1)
    return before, row, after


def stack_kernel(share, merged, parts_ref, w_ref, b_ref, *refs):
    if merged:
        out_ref, s0_ref, s1_ref, h_ref, y_ref, g_ref, sums_ref = refs
        first = 2 * w_ref.shape[-1]
        pieces_ref = out_ref
    else:
        out_ref, pieces_ref, s0_ref, s1_ref, h_ref, y_ref, g_ref, sums_ref = refs
        first = 0
    count = h_ref.shape[0]
    channels = w_ref.shape[-1]
    devices, _, width = parts_ref.shape
    blocks = devices // count

    def line_of(field, i):
        rows = slice(field * channels, (field + 1) * channels)
        return jnp.concatenate([parts_ref[i * blocks + k, rows, :] for k in range(blocks)], axis=1)

    def put(field, i, line):
        rows = slice(field * channels, (field + 1) * channels)
        for k in range(blocks):
            out_ref[i * blocks + k, rows, :] = line[:, k * width : (k + 1) * width]

    for layer in range(2):
        hops = 2**layer
        kernel = jnp.concatenate(
            [
                jnp.concatenate([w_ref[layer, a, b] for b in range(3)], axis=1)
                for a in range(3)
            ],
            axis=0,
        )
        for i in range(count):
            line = line_of(0, i) if layer == 0 else h_ref[i]
            stack = jnp.concatenate(taps(line, hops * share), axis=0)
            y_ref[i] = jnp.dot(kernel, stack, preferred_element_type=F32)
        bias = b_ref[layer]
        for i in range(count):
            pre = bias + y_ref[i, channels : 2 * channels]
            pre = pre + y_ref[(i - hops) % count, :channels]
            pre = pre + y_ref[(i + hops) % count, 2 * channels :]
            sigma = 1.0 / (1.0 + jnp.exp(-pre))
            state = (pre * sigma).astype(BF16)
            slope = sigma * (1.0 + pre * (1.0 - sigma))
            if layer == 0:
                h_ref[i] = state
                s0_ref[i] = slope
            else:
                s1_ref[i] = slope
                put(0, i, state)

    ones = jnp.ones((16, blocks * width), BF16)
    bias_rows = [None, None]
    for layer in (1, 0):
        hops = 2**layer
        kernel = jnp.concatenate(
            [
                jnp.concatenate([w_ref[layer, a, b].astype(F32).T for b in range(3)], axis=1)
                for a in range(3)
            ],
            axis=0,
        ).astype(BF16)
        total = jnp.zeros((3 * channels, 3 * channels), F32)
        bias = jnp.zeros((16, channels), F32)
        for i in range(count):
            if layer == 1:
                gated = (line_of(1, i).astype(F32) * s1_ref[i]).astype(BF16)
            else:
                gated = g_ref[i]
            bias = bias + lax.dot_general(
                ones, gated, (((1,), (1,)), ((), ())), preferred_element_type=F32
            )
            before, here, after = taps(gated, hops * share)
            stack = jnp.concatenate([after, here, before], axis=0)
            y_ref[i] = jnp.dot(kernel, stack, preferred_element_type=F32)
            around = [(i + (a - 1) * hops) % count for a in range(3)]
            lines = jnp.concatenate(
                [line_of(0, j) if layer == 0 else h_ref[j] for j in around], axis=0
            )
            total = total + lax.dot_general(
                stack, lines, (((1,), (1,)), ((), ())), preferred_element_type=F32
            )
        high = 3 * channels
        sums_ref[layer * high : (layer + 1) * high, :] = total[:, : 2 * channels]
        sums_ref[2 * high : 3 * high, layer * channels : (layer + 1) * channels] = total[
            :, 2 * channels :
        ]
        bias_rows[layer] = bias[:1]
        for i in range(count):
            g = y_ref[i, channels : 2 * channels]
            g = g + y_ref[(i + hops) % count, :channels]
            g = g + y_ref[(i - hops) % count, 2 * channels :]
            g = g.astype(BF16)
            if layer == 1:
                g_ref[i] = (g.astype(F32) * s0_ref[i]).astype(BF16)
            else:
                put(1, i, g)

    used = -(-9 * channels // devices)
    held = sums_ref.shape[0] - 9 * channels
    sums_ref[9 * channels :, :] = jnp.zeros((held, 2 * channels), F32)
    size = pieces_ref.shape[1] - first
    bias = jnp.concatenate(bias_rows, axis=1)
    high = bias.astype(BF16).astype(F32)
    low = bias - high
    row = lax.broadcasted_iota(jnp.int32, (size, 2 * channels), 0)
    for p in range(devices):
        piece = sums_ref[used * p : used * p + size, :]
        piece = jnp.where(row < used, piece, jnp.where(row == used, high, low))
        pieces_ref[p, first:, :] = piece.astype(BF16)


def reduce_kernel(scale, used, first, got_ref, mine_ref, bias_ref):
    devices, lanes = got_ref.shape[0], mine_ref.shape[1]
    total = got_ref[0, first:, :].astype(F32)
    for p in range(1, devices):
        total = total + got_ref[p, first:, :].astype(F32)
    total = total * scale
    bias = total[used : used + 1] + total[used + 1 : used + 2]
    bias_ref[0:1, :] = bias[:, : lanes // 2]
    bias_ref[1:2, :] = bias[:, lanes // 2 :]
    mine_ref[...] = total.astype(BF16)


def assemble_kernel(used, parts_ref, out_ref, rows_ref):
    devices = parts_ref.shape[0]
    channels = out_ref.shape[-1]
    for p in range(devices):
        rows_ref[used * p : used * (p + 1), :] = parts_ref[p].astype(F32)[:used]
    high = 3 * channels
    for layer in range(2):
        for b in range(3):
            pair = rows_ref[layer * high + b * channels : layer * high + (b + 1) * channels, :]
            out_ref[layer, 0, b] = pair[:, :channels]
            out_ref[layer, 1, b] = pair[:, channels:]
            third = rows_ref[2 * high + b * channels : 2 * high + (b + 1) * channels, :]
            out_ref[layer, 2, b] = third[:, layer * channels : (layer + 1) * channels]


def exchanged(parts):
    return lax.all_to_all(parts, AXES, 0, 0, tiled=True)


def local(inputs, weights, biases, cotangent):
    channels, cols, lat_rows = inputs.shape
    lons, lats = lax.axis_size("lon"), lax.axis_size("lat")
    devices = lons * lats
    share = cols * cols // devices
    width = lat_rows // cols * share
    span = lats * width
    scale = 1.0 / math.sqrt(cols * lons * lat_rows * lats)
    merged = width == LANES
    used = -(-9 * channels // devices)
    size = -(-(used + 2) // 8) * 8
    shape = jax.ShapeDtypeStruct
    rows = pltpu.VMEM((lat_rows // LANES, channels * cols, LANES), F32)

    packed = pl.pallas_call(
        functools.partial(pack_kernel, share),
        out_shape=shape((devices, 2 * channels, width), BF16),
        in_specs=[
            pl.BlockSpec(memory_space=pltpu.HBM),
            pl.BlockSpec(memory_space=pltpu.HBM),
        ],
        scratch_shapes=[
            pltpu.VMEM(inputs.shape, BF16),
            pltpu.VMEM(inputs.shape, BF16),
            rows,
            pltpu.SemaphoreType.DMA((2,)),
        ],
        compiler_params=pltpu.CompilerParams(vmem_limit_bytes=56 * 2**20),
    )(inputs, cotangent)
    parts = exchanged(packed)
    if not merged:
        parts = parts.reshape(lons, lats, 2 * channels, width).transpose(0, 2, 1, 3)
        parts = parts.reshape(lons, 2 * channels, span)

    cells = (lons, channels, span)
    pieces_shape = (devices, size, 2 * channels)
    if merged:
        out_shape = [shape((devices, 2 * channels + size, width), BF16)]
    else:
        out_shape = [shape(parts.shape, BF16), shape(pieces_shape, BF16)]
    results = pl.pallas_call(
        functools.partial(stack_kernel, share, merged),
        out_shape=out_shape,
        scratch_shapes=[
            pltpu.VMEM(cells, F32),
            pltpu.VMEM(cells, F32),
            pltpu.VMEM(cells, BF16),
            pltpu.VMEM((lons, 3 * channels, span), F32),
            pltpu.VMEM(cells, BF16),
            pltpu.VMEM((used * devices + size, 2 * channels), F32),
        ],
        compiler_params=PARAMS,
    )(parts, weights, biases[:, :, None])
    if merged:
        home = exchanged(results[0])
        got, first = home, 2 * channels
    else:
        home = results[0].reshape(lons, 2 * channels, lats, width).transpose(0, 2, 1, 3)
        home = exchanged(home.reshape(devices, 2 * channels, width))
        got, first = exchanged(results[1]), 0

    mine, bias_grads = pl.pallas_call(
        functools.partial(reduce_kernel, scale, used, first),
        out_shape=[shape(pieces_shape[1:], BF16), shape(biases.shape, F32)],
        compiler_params=PARAMS,
    )(got)
    home, mine = lax.optimization_barrier((home, mine))
    full = lax.all_gather(mine, AXES)
    features_out, grad_input = pl.pallas_call(
        functools.partial(unpack_kernel, share),
        out_shape=[shape(inputs.shape, BF16), shape(inputs.shape, BF16)],
        scratch_shapes=[rows],
        compiler_params=PARAMS,
        cost_estimate=pl.CostEstimate(
            flops=4 * inputs.size * lat_rows, bytes_accessed=8 * inputs.size, transcendentals=0
        ),
    )(home)
    weight_grads = pl.pallas_call(
        functools.partial(assemble_kernel, used),
        out_shape=shape(weights.shape, F32),
        scratch_shapes=[pltpu.VMEM((used * devices, 2 * channels), F32)],
        compiler_params=PARAMS,
    )(full)
    return features_out, grad_input, weight_grads, bias_grads


def solution(mesh):
    in_specs = (P(None, "lon", "lat"), P(), P(), P(None, "lon", "lat"))
    out_specs = (P(None, "lon", "lat"), P(None, "lon", "lat"), P(), P())
    return jax.shard_map(local, mesh=mesh, in_specs=in_specs, out_specs=out_specs, check_vma=False)
```

```python
import functools
import math

import jax
import jax.numpy as jnp
from jax import lax
from jax.experimental import pallas as pl
from jax.experimental.pallas import tpu as pltpu
from jax.sharding import PartitionSpec as P


AXES = ("lon", "lat")
LANES = 128
TAIL = 16
BF16, F32 = jnp.bfloat16, jnp.float32
PARAMS = pltpu.CompilerParams(vmem_limit_bytes=48 * 2**20)


def lane_order(cols, lat_rows, share, inverse):
    steps = lat_rows // cols
    place = lax.broadcasted_iota(jnp.int32, (lat_rows, lat_rows), 0 if inverse else 1)
    source = lax.broadcasted_iota(jnp.int32, (lat_rows, lat_rows), 1 if inverse else 0)
    group = lax.div(source & (cols - 1), share)
    wanted = (group * steps + lax.div(source, cols)) * share + (source & (share - 1))
    return (place == wanted).astype(F32).astype(BF16)


def row_order(outer, inner):
    rows = outer * inner
    place = lax.broadcasted_iota(jnp.int32, (rows, rows), 0)
    source = lax.broadcasted_iota(jnp.int32, (rows, rows), 1)
    wanted = (source & (inner - 1)) * outer + lax.div(source, inner)
    return (place == wanted).astype(F32).astype(BF16)


def product(left, right):
    return jnp.dot(left, right, preferred_element_type=F32)


def pack_kernel(share, x_ref, cot_ref, out_ref, x_buf, cot_buf, sems):
    channels, cols, lat_rows = x_ref.shape
    devices, _, width = out_ref.shape
    groups = devices // cols
    part = min(channels, 256 // cols)
    copies = [
        pltpu.make_async_copy(ref, buf, sems.at[at])
        for at, (ref, buf) in enumerate(((x_ref, x_buf), (cot_ref, cot_buf)))
    ]
    for copy in copies:
        copy.start()
    lanes = lane_order(cols, lat_rows, share, False)
    order = row_order(part, cols)
    for at, buf in enumerate((x_buf, cot_buf)):
        copies[at].wait()
        for first in range(0, channels, part):
            rows = buf[first : first + part].reshape(part * cols, lat_rows)
            rows = product(order, rows).astype(BF16)
            rows = product(rows, lanes).astype(BF16)
            start = at * channels + first
            for col in range(cols):
                for group in range(groups):
                    out_ref[col * groups + group, start : start + part, :] = rows[
                        col * part : (col + 1) * part, group * width : (group + 1) * width
                    ]


def unpack_kernel(share, parts_ref, feat_ref, grad_ref):
    channels, cols, lat_rows = feat_ref.shape
    devices, _, width = parts_ref.shape
    groups = devices // cols
    part = min(channels, 256 // cols)
    lanes = lane_order(cols, lat_rows, share, True)
    order = row_order(cols, part)
    for at, out_ref in enumerate((feat_ref, grad_ref)):
        for first in range(0, channels, part):
            start = at * channels + first
            rows = [
                jnp.concatenate(
                    [
                        parts_ref[col * groups + group, start : start + part, :]
                        for group in range(groups)
                    ],
                    axis=1,
                )
                for col in range(cols)
            ]
            rows = product(jnp.concatenate(rows, axis=0), lanes).astype(BF16)
            rows = product(order, rows).astype(BF16)
            out_ref[first : first + part] = rows.reshape(part, cols, lat_rows)


def taps(row, shift):
    edge = jnp.zeros((row.shape[0], shift), row.dtype)
    before = jnp.concatenate([edge, row[:, :-shift]], axis=1)
    after = jnp.concatenate([row[:, shift:], edge], axis=1)
    return before, row, after


def stack_kernel(
    share, parts_ref, w_ref, b_ref, out_ref, total_ref, s0_ref, s1_ref, h_ref, y_ref, g_ref
):
    count = h_ref.shape[0]
    channels = w_ref.shape[-1]
    devices, _, width = parts_ref.shape
    blocks = devices // count

    def line_of(field, i):
        rows = slice(field * channels, (field + 1) * channels)
        return jnp.concatenate([parts_ref[i * blocks + k, rows, :] for k in range(blocks)], axis=1)

    def put(field, i, line):
        rows = slice(field * channels, (field + 1) * channels)
        for k in range(blocks):
            out_ref[i * blocks + k, rows, :] = line[:, k * width : (k + 1) * width]

    for layer in range(2):
        hops = 2**layer
        kernel = jnp.concatenate(
            [
                jnp.concatenate([w_ref[layer, a, b] for b in range(3)], axis=1)
                for a in range(3)
            ],
            axis=0,
        )
        for i in range(count):
            line = line_of(0, i) if layer == 0 else h_ref[i]
            stack = jnp.concatenate(taps(line, hops * share), axis=0)
            y_ref[i] = jnp.dot(kernel, stack, preferred_element_type=F32)
        bias = b_ref[layer]
        for i in range(count):
            pre = bias + y_ref[i, channels : 2 * channels]
            pre = pre + y_ref[(i - hops) % count, :channels]
            pre = pre + y_ref[(i + hops) % count, 2 * channels :]
            sigma = 1.0 / (1.0 + jnp.exp(-pre))
            state = (pre * sigma).astype(BF16)
            slope = sigma * (1.0 + pre * (1.0 - sigma))
            if layer == 0:
                h_ref[i] = state
                s0_ref[i] = slope
            else:
                s1_ref[i] = slope
                put(0, i, state)

    ones = jnp.ones((16, blocks * width), BF16)
    bias_rows = [None, None]
    for layer in (1, 0):
        hops = 2**layer
        kernel = jnp.concatenate(
            [
                jnp.concatenate([w_ref[layer, a, b].astype(F32).T for b in range(3)], axis=1)
                for a in range(3)
            ],
            axis=0,
        ).astype(BF16)
        total = jnp.zeros((3 * channels, 3 * channels), F32)
        bias = jnp.zeros((16, channels), F32)
        for i in range(count):
            if layer == 1:
                gated = (line_of(1, i).astype(F32) * s1_ref[i]).astype(BF16)
            else:
                gated = g_ref[i]
            bias = bias + lax.dot_general(
                ones, gated, (((1,), (1,)), ((), ())), preferred_element_type=F32
            )
            before, here, after = taps(gated, hops * share)
            stack = jnp.concatenate([after, here, before], axis=0)
            y_ref[i] = jnp.dot(kernel, stack, preferred_element_type=F32)
            around = [(i + (a - 1) * hops) % count for a in range(3)]
            lines = jnp.concatenate(
                [line_of(0, j) if layer == 0 else h_ref[j] for j in around], axis=0
            )
            total = total + lax.dot_general(
                stack, lines, (((1,), (1,)), ((), ())), preferred_element_type=F32
            )
        high = 3 * channels
        total = total.astype(BF16)
        total_ref[layer * high : (layer + 1) * high, :] = total[:, : 2 * channels]
        total_ref[2 * high : 3 * high, layer * channels : (layer + 1) * channels] = total[
            :, 2 * channels :
        ]
        bias_rows[layer] = bias[:1]
        for i in range(count):
            g = y_ref[i, channels : 2 * channels]
            g = g + y_ref[(i + hops) % count, :channels]
            g = g + y_ref[(i - hops) % count, 2 * channels :]
            g = g.astype(BF16)
            if layer == 1:
                g_ref[i] = (g.astype(F32) * s0_ref[i]).astype(BF16)
            else:
                put(1, i, g)

    bias = jnp.concatenate(bias_rows, axis=1)
    high = bias.astype(BF16).astype(F32)
    low = bias - high
    row = lax.broadcasted_iota(jnp.int32, (TAIL, 2 * channels), 0)
    tail = jnp.where(row == 0, high, jnp.where(row == 1, low, 0.0))
    total_ref[9 * channels :, :] = tail.astype(BF16)


def assemble_kernel(scale, total_ref, out_ref, bias_ref):
    channels = out_ref.shape[-1]
    high = 3 * channels
    for layer in range(2):
        for b in range(3):
            first = layer * high + b * channels
            pair = total_ref[first : first + channels, :].astype(F32) * scale
            out_ref[layer, 0, b] = pair[:, :channels]
            out_ref[layer, 1, b] = pair[:, channels:]
            first = 2 * high + b * channels
            third = total_ref[first : first + channels, :].astype(F32) * scale
            out_ref[layer, 2, b] = third[:, layer * channels : (layer + 1) * channels]
    tail = total_ref[9 * channels :, :].astype(F32) * scale
    bias = tail[0:1] + tail[1:2]
    bias_ref[0:1, :] = bias[:, :channels]
    bias_ref[1:2, :] = bias[:, channels:]


def exchanged(parts):
    return lax.all_to_all(parts, AXES, 0, 0, tiled=True)


def local(inputs, weights, biases, cotangent):
    channels, cols, lat_rows = inputs.shape
    lons, lats = lax.axis_size("lon"), lax.axis_size("lat")
    devices = lons * lats
    share = cols * cols // devices
    width = lat_rows // cols * share
    span = lats * width
    scale = 1.0 / math.sqrt(cols * lons * lat_rows * lats)
    blocks = lats if width % LANES == 0 else 1
    shape = jax.ShapeDtypeStruct

    packed = pl.pallas_call(
        functools.partial(pack_kernel, share),
        out_shape=shape((devices, 2 * channels, width), BF16),
        in_specs=[pl.BlockSpec(memory_space=pltpu.HBM)] * 2,
        scratch_shapes=[
            pltpu.VMEM(inputs.shape, BF16),
            pltpu.VMEM(inputs.shape, BF16),
            pltpu.SemaphoreType.DMA((2,)),
        ],
        compiler_params=pltpu.CompilerParams(vmem_limit_bytes=56 * 2**20),
    )(inputs, cotangent)
    parts = exchanged(packed)
    if blocks == 1:
        parts = parts.reshape(lons, lats, 2 * channels, width).transpose(0, 2, 1, 3)
        parts = parts.reshape(lons, 2 * channels, span)

    cells = (lons, channels, span)
    fields, total = pl.pallas_call(
        functools.partial(stack_kernel, share),
        out_shape=[shape(parts.shape, BF16), shape((9 * channels + TAIL, 2 * channels), BF16)],
        scratch_shapes=[
            pltpu.VMEM(cells, F32),
            pltpu.VMEM(cells, F32),
            pltpu.VMEM(cells, BF16),
            pltpu.VMEM((lons, 3 * channels, span), F32),
            pltpu.VMEM(cells, BF16),
        ],
        compiler_params=PARAMS,
    )(parts, weights, biases[:, :, None])
    if blocks == 1:
        fields = fields.reshape(lons, 2 * channels, lats, width).transpose(0, 2, 1, 3)
        fields = fields.reshape(devices, 2 * channels, width)
    home = exchanged(fields)
    total = lax.optimization_barrier(lax.psum(total, "lat"))
    total = lax.psum(total, "lon")
    weight_grads, bias_grads = pl.pallas_call(
        functools.partial(assemble_kernel, scale),
        out_shape=[shape(weights.shape, F32), shape(biases.shape, F32)],
        compiler_params=PARAMS,
    )(total)
    features_out, grad_input = pl.pallas_call(
        functools.partial(unpack_kernel, share),
        out_shape=[shape(inputs.shape, BF16), shape(inputs.shape, BF16)],
        compiler_params=PARAMS,
    )(home)
    return features_out, grad_input, weight_grads, bias_grads


def solution(mesh):
    in_specs = (P(None, "lon", "lat"), P(), P(), P(None, "lon", "lat"))
    out_specs = (P(None, "lon", "lat"), P(None, "lon", "lat"), P(), P())
    return jax.shard_map(local, mesh=mesh, in_specs=in_specs, out_specs=out_specs, check_vma=False)
```

```python
import functools
import math

import jax
import jax.numpy as jnp
from jax import lax
from jax.experimental import pallas as pl
from jax.experimental.pallas import tpu as pltpu
from jax.sharding import PartitionSpec as P


AXES = ("lon", "lat")
LANES = 128
TAIL = 32
BF16, F32 = jnp.bfloat16, jnp.float32
PARAMS = pltpu.CompilerParams(vmem_limit_bytes=48 * 2**20)


def lane_order(cols, lat_rows, share, inverse):
    steps = lat_rows // cols
    place = lax.broadcasted_iota(jnp.int32, (lat_rows, lat_rows), 0 if inverse else 1)
    source = lax.broadcasted_iota(jnp.int32, (lat_rows, lat_rows), 1 if inverse else 0)
    group = lax.div(source & (cols - 1), share)
    wanted = (group * steps + lax.div(source, cols)) * share + (source & (share - 1))
    return (place == wanted).astype(F32).astype(BF16)


def row_order(outer, inner):
    rows = outer * inner
    place = lax.broadcasted_iota(jnp.int32, (rows, rows), 0)
    source = lax.broadcasted_iota(jnp.int32, (rows, rows), 1)
    wanted = (source & (inner - 1)) * outer + lax.div(source, inner)
    return (place == wanted).astype(F32).astype(BF16)


def product(left, right):
    return jnp.dot(left, right, preferred_element_type=F32)


def pack_kernel(share, x_ref, cot_ref, out_ref, x_buf, cot_buf, sems):
    channels, cols, lat_rows = x_ref.shape
    devices, _, width = out_ref.shape
    groups = devices // cols
    part = min(channels, 256 // cols)
    copies = [
        pltpu.make_async_copy(ref, buf, sems.at[at])
        for at, (ref, buf) in enumerate(((x_ref, x_buf), (cot_ref, cot_buf)))
    ]
    for copy in copies:
        copy.start()
    lanes = lane_order(cols, lat_rows, share, False)
    order = row_order(part, cols)
    for at, buf in enumerate((x_buf, cot_buf)):
        copies[at].wait()
        for first in range(0, channels, part):
            rows = buf[first : first + part].reshape(part * cols, lat_rows)
            rows = product(order, rows).astype(BF16)
            rows = product(rows, lanes).astype(BF16)
            start = at * channels + first
            for col in range(cols):
                for group in range(groups):
                    out_ref[col * groups + group, start : start + part, :] = rows[
                        col * part : (col + 1) * part, group * width : (group + 1) * width
                    ]


def unpack_kernel(share, parts_ref, feat_ref, grad_ref):
    channels, cols, lat_rows = feat_ref.shape
    devices, _, width = parts_ref.shape
    groups = devices // cols
    part = min(channels, 256 // cols)
    lanes = lane_order(cols, lat_rows, share, True)
    order = row_order(cols, part)
    for at, out_ref in enumerate((feat_ref, grad_ref)):
        for first in range(0, channels, part):
            start = at * channels + first
            rows = [
                jnp.concatenate(
                    [
                        parts_ref[col * groups + group, start : start + part, :]
                        for group in range(groups)
                    ],
                    axis=1,
                )
                for col in range(cols)
            ]
            rows = product(jnp.concatenate(rows, axis=0), lanes).astype(BF16)
            rows = product(order, rows).astype(BF16)
            out_ref[first : first + part] = rows.reshape(part, cols, lat_rows)


def taps(row, shift):
    edge = jnp.zeros((row.shape[0], shift), row.dtype)
    before = jnp.concatenate([edge, row[:, :-shift]], axis=1)
    after = jnp.concatenate([row[:, shift:], edge], axis=1)
    return before, row, after


def stack_kernel(
    share,
    parts_ref,
    w_ref,
    b_ref,
    out_ref,
    keep_ref,
    send_ref,
    s0_ref,
    s1_ref,
    h_ref,
    y_ref,
    g_ref,
    total_ref,
):
    count = h_ref.shape[0]
    channels = w_ref.shape[-1]
    devices, _, width = parts_ref.shape
    blocks = devices // count

    def line_of(field, i):
        rows = slice(field * channels, (field + 1) * channels)
        return jnp.concatenate([parts_ref[i * blocks + k, rows, :] for k in range(blocks)], axis=1)

    def put(field, i, line):
        rows = slice(field * channels, (field + 1) * channels)
        for k in range(blocks):
            out_ref[i * blocks + k, rows, :] = line[:, k * width : (k + 1) * width]

    for layer in range(2):
        hops = 2**layer
        kernel = jnp.concatenate(
            [
                jnp.concatenate([w_ref[layer, a, b] for b in range(3)], axis=1)
                for a in range(3)
            ],
            axis=0,
        )
        for i in range(count):
            line = line_of(0, i) if layer == 0 else h_ref[i]
            stack = jnp.concatenate(taps(line, hops * share), axis=0)
            y_ref[i] = jnp.dot(kernel, stack, preferred_element_type=F32)
        bias = b_ref[layer]
        for i in range(count):
            pre = bias + y_ref[i, channels : 2 * channels]
            pre = pre + y_ref[(i - hops) % count, :channels]
            pre = pre + y_ref[(i + hops) % count, 2 * channels :]
            sigma = 1.0 / (1.0 + jnp.exp(-pre))
            state = (pre * sigma).astype(BF16)
            slope = sigma * (1.0 + pre * (1.0 - sigma))
            if layer == 0:
                h_ref[i] = state
                s0_ref[i] = slope
            else:
                s1_ref[i] = slope
                put(0, i, state)

    ones = jnp.ones((16, blocks * width), BF16)
    bias_rows = [None, None]
    for layer in (1, 0):
        hops = 2**layer
        kernel = jnp.concatenate(
            [
                jnp.concatenate([w_ref[layer, a, b].astype(F32).T for b in range(3)], axis=1)
                for a in range(3)
            ],
            axis=0,
        ).astype(BF16)
        total = jnp.zeros((3 * channels, 3 * channels), F32)
        bias = jnp.zeros((16, channels), F32)
        for i in range(count):
            if layer == 1:
                gated = (line_of(1, i).astype(F32) * s1_ref[i]).astype(BF16)
            else:
                gated = g_ref[i]
            bias = bias + lax.dot_general(
                ones, gated, (((1,), (1,)), ((), ())), preferred_element_type=F32
            )
            before, here, after = taps(gated, hops * share)
            stack = jnp.concatenate([after, here, before], axis=0)
            y_ref[i] = jnp.dot(kernel, stack, preferred_element_type=F32)
            around = [(i + (a - 1) * hops) % count for a in range(3)]
            lines = jnp.concatenate(
                [line_of(0, j) if layer == 0 else h_ref[j] for j in around], axis=0
            )
            total = total + lax.dot_general(
                stack, lines, (((1,), (1,)), ((), ())), preferred_element_type=F32
            )
        high = 3 * channels
        total_ref[layer * high : (layer + 1) * high, :] = total[:, : 2 * channels]
        total_ref[2 * high : 3 * high, layer * channels : (layer + 1) * channels] = total[
            :, 2 * channels :
        ]
        bias_rows[layer] = bias[:1]
        for i in range(count):
            g = y_ref[i, channels : 2 * channels]
            g = g + y_ref[(i + hops) % count, :channels]
            g = g + y_ref[(i - hops) % count, 2 * channels :]
            g = g.astype(BF16)
            if layer == 1:
                g_ref[i] = (g.astype(F32) * s0_ref[i]).astype(BF16)
            else:
                put(1, i, g)

    bias = jnp.concatenate(bias_rows, axis=1)
    row = lax.broadcasted_iota(jnp.int32, (TAIL, 2 * channels), 0)
    total_ref[9 * channels :, :] = jnp.where(row == 0, bias, 0.0)
    half = keep_ref.shape[0]
    odd = lax.axis_index("lat") & 1
    keep_ref[...] = total_ref[pl.ds(pl.multiple_of(odd * half, 8), half), :].astype(BF16)
    send_ref[...] = total_ref[pl.ds(pl.multiple_of((1 - odd) * half, 8), half), :].astype(BF16)


def assemble_kernel(scale, mine_ref, other_ref, out_ref, bias_ref, total_ref):
    channels = out_ref.shape[-1]
    half = mine_ref.shape[0]
    odd = lax.axis_index("lat") & 1
    total_ref[pl.ds(pl.multiple_of(odd * half, 8), half), :] = mine_ref[...].astype(F32) * scale
    total_ref[pl.ds(pl.multiple_of((1 - odd) * half, 8), half), :] = (
        other_ref[...].astype(F32) * scale
    )
    high = 3 * channels
    for layer in range(2):
        for b in range(3):
            first = layer * high + b * channels
            pair = total_ref[first : first + channels, :]
            out_ref[layer, 0, b] = pair[:, :channels]
            out_ref[layer, 1, b] = pair[:, channels:]
            first = 2 * high + b * channels
            third = total_ref[first : first + channels, :]
            out_ref[layer, 2, b] = third[:, layer * channels : (layer + 1) * channels]
    bias = total_ref[9 * channels : 9 * channels + 1, :]
    bias_ref[0:1, :] = bias[:, :channels]
    bias_ref[1:2, :] = bias[:, channels:]


def partnered(block, devices, bit):
    return lax.ppermute(block, AXES, [(i, i ^ bit) for i in range(devices)])


def exchanged(parts):
    return lax.all_to_all(parts, AXES, 0, 0, tiled=True)


def local(inputs, weights, biases, cotangent):
    channels, cols, lat_rows = inputs.shape
    lons, lats = lax.axis_size("lon"), lax.axis_size("lat")
    devices = lons * lats
    share = cols * cols // devices
    width = lat_rows // cols * share
    span = lats * width
    scale = 1.0 / math.sqrt(cols * lons * lat_rows * lats)
    blocks = lats if width % LANES == 0 else 1
    shape = jax.ShapeDtypeStruct

    packed = pl.pallas_call(
        functools.partial(pack_kernel, share),
        out_shape=shape((devices, 2 * channels, width), BF16),
        in_specs=[pl.BlockSpec(memory_space=pltpu.HBM)] * 2,
        scratch_shapes=[
            pltpu.VMEM(inputs.shape, BF16),
            pltpu.VMEM(inputs.shape, BF16),
            pltpu.SemaphoreType.DMA((2,)),
        ],
        compiler_params=pltpu.CompilerParams(vmem_limit_bytes=56 * 2**20),
    )(inputs, cotangent)
    parts = exchanged(packed)
    if blocks == 1:
        parts = parts.reshape(lons, lats, 2 * channels, width).transpose(0, 2, 1, 3)
        parts = parts.reshape(lons, 2 * channels, span)

    cells = (lons, channels, span)
    half = (9 * channels + TAIL) // 2
    half_shape = shape((half, 2 * channels), BF16)
    fields, keep, send = pl.pallas_call(
        functools.partial(stack_kernel, share),
        out_shape=[shape(parts.shape, BF16), half_shape, half_shape],
        scratch_shapes=[
            pltpu.VMEM(cells, F32),
            pltpu.VMEM(cells, F32),
            pltpu.VMEM(cells, BF16),
            pltpu.VMEM((lons, 3 * channels, span), F32),
            pltpu.VMEM(cells, BF16),
            pltpu.VMEM((2 * half, 2 * channels), F32),
        ],
        compiler_params=PARAMS,
    )(parts, weights, biases[:, :, None])
    if blocks == 1:
        fields = fields.reshape(lons, 2 * channels, lats, width).transpose(0, 2, 1, 3)
        fields = fields.reshape(devices, 2 * channels, width)
    home = exchanged(fields)
    came = partnered(send, devices, 1)
    bit = 2
    while bit < devices:
        keep = (keep.astype(F32) + came.astype(F32)).astype(BF16)
        came = partnered(keep, devices, bit)
        bit *= 2
    keep = (keep.astype(F32) + came.astype(F32)).astype(BF16)
    came = partnered(keep, devices, 1)
    home, came = lax.optimization_barrier((home, came))
    weight_grads, bias_grads = pl.pallas_call(
        functools.partial(assemble_kernel, scale),
        out_shape=[shape(weights.shape, F32), shape(biases.shape, F32)],
        scratch_shapes=[pltpu.VMEM((2 * half, 2 * channels), F32)],
        compiler_params=PARAMS,
    )(keep, came)
    features_out, grad_input = pl.pallas_call(
        functools.partial(unpack_kernel, share),
        out_shape=[shape(inputs.shape, BF16), shape(inputs.shape, BF16)],
        compiler_params=PARAMS,
    )(home)
    return features_out, grad_input, weight_grads, bias_grads


def solution(mesh):
    in_specs = (P(None, "lon", "lat"), P(), P(), P(None, "lon", "lat"))
    out_specs = (P(None, "lon", "lat"), P(None, "lon", "lat"), P(), P())
    return jax.shard_map(local, mesh=mesh, in_specs=in_specs, out_specs=out_specs, check_vma=False)
```

```python
import functools
import math

import jax
import jax.numpy as jnp
from jax import lax
from jax.experimental import pallas as pl
from jax.experimental.pallas import tpu as pltpu
from jax.sharding import PartitionSpec as P


AXES = ("lon", "lat")
LANES = 128
TAIL = 64
BF16, F32 = jnp.bfloat16, jnp.float32
PARAMS = pltpu.CompilerParams(vmem_limit_bytes=24 * 2**20)


def lane_order(cols, lat_rows, share, inverse):
    steps = lat_rows // cols
    place = lax.broadcasted_iota(jnp.int32, (lat_rows, lat_rows), 0 if inverse else 1)
    source = lax.broadcasted_iota(jnp.int32, (lat_rows, lat_rows), 1 if inverse else 0)
    group = lax.div(source & (cols - 1), share)
    wanted = (group * steps + lax.div(source, cols)) * share + (source & (share - 1))
    return (place == wanted).astype(F32).astype(BF16)


def row_order(outer, inner):
    rows = outer * inner
    place = lax.broadcasted_iota(jnp.int32, (rows, rows), 0)
    source = lax.broadcasted_iota(jnp.int32, (rows, rows), 1)
    wanted = (source & (inner - 1)) * outer + lax.div(source, inner)
    return (place == wanted).astype(F32).astype(BF16)


def product(left, right):
    return jnp.dot(left, right, preferred_element_type=F32)


def pack_kernel(share, x_ref, cot_ref, out_ref, buf, packed, in_sems, out_sems):
    _, channels, cols, lat_rows = buf.shape
    devices, _, width = packed.shape
    groups = devices // cols
    part = min(channels, 256 // cols)
    parts = [(at, first) for at in range(2) for first in range(0, channels, part)]
    arrivals, departures = [], []
    for k, (at, first) in enumerate(parts):
        rows = pl.ds(first, part)
        source = (x_ref, cot_ref)[at].at[rows]
        arrivals.append(pltpu.make_async_copy(source, buf.at[at, rows], in_sems.at[k]))
        rows = (slice(None), pl.ds(at * channels + first, part), slice(None))
        departures.append(pltpu.make_async_copy(packed.at[rows], out_ref.at[rows], out_sems.at[k]))
        arrivals[k].start()
    lanes = lane_order(cols, lat_rows, share, False)
    order = row_order(part, cols)
    for k, (at, first) in enumerate(parts):
        arrivals[k].wait()
        rows = buf[at, first : first + part].reshape(part * cols, lat_rows)
        rows = product(order, rows).astype(BF16)
        rows = product(rows, lanes).astype(BF16)
        start = at * channels + first
        for col in range(cols):
            for group in range(groups):
                packed[col * groups + group, start : start + part, :] = rows[
                    col * part : (col + 1) * part, group * width : (group + 1) * width
                ]
        departures[k].start()
    for departure in departures:
        departure.wait()


def unpack_kernel(share, parts_ref, feat_ref, grad_ref, buf, sems):
    _, channels, cols, lat_rows = buf.shape
    devices, _, width = parts_ref.shape
    groups = devices // cols
    part = min(channels, 256 // cols)
    lanes = lane_order(cols, lat_rows, share, True)
    order = row_order(cols, part)
    departures = []
    for at, out_ref in enumerate((feat_ref, grad_ref)):
        for first in range(0, channels, part):
            start = at * channels + first
            rows = [
                jnp.concatenate(
                    [
                        parts_ref[col * groups + group, start : start + part, :]
                        for group in range(groups)
                    ],
                    axis=1,
                )
                for col in range(cols)
            ]
            rows = product(jnp.concatenate(rows, axis=0), lanes).astype(BF16)
            rows = product(order, rows).astype(BF16)
            buf[at, first : first + part] = rows.reshape(part, cols, lat_rows)
            rows = pl.ds(first, part)
            departures.append(
                pltpu.make_async_copy(buf.at[at, rows], out_ref.at[rows], sems.at[len(departures)])
            )
            departures[-1].start()
    for departure in departures:
        departure.wait()


def taps(row, shift):
    edge = jnp.zeros((row.shape[0], shift), row.dtype)
    before = jnp.concatenate([edge, row[:, :-shift]], axis=1)
    after = jnp.concatenate([row[:, shift:], edge], axis=1)
    return before, row, after


def line_of(parts_ref, count, channels, field, i):
    blocks = parts_ref.shape[0] // count
    rows = slice(field * channels, (field + 1) * channels)
    return jnp.concatenate([parts_ref[i * blocks + k, rows, :] for k in range(blocks)], axis=1)


def stack_kernel(
    share,
    parts_ref,
    w_ref,
    b_ref,
    out_ref,
    h_ref,
    gz0_ref,
    gz1_ref,
    s0_ref,
    s1_ref,
    y_ref,
    fields_ref,
    sems,
):
    count = h_ref.shape[0]
    channels = w_ref.shape[-1]
    devices, _, width = parts_ref.shape
    blocks = devices // count
    copies = []

    def put(field, i, line):
        rows = slice(field * channels, (field + 1) * channels)
        for k in range(blocks):
            fields_ref[i * blocks + k, rows, :] = line[:, k * width : (k + 1) * width]

    def send(field, i, lines):
        place = (pl.ds(i * blocks, lines * blocks), pl.ds(field * channels, channels))
        copies.append(
            pltpu.make_async_copy(fields_ref.at[place], out_ref.at[place], sems.at[len(copies)])
        )
        copies[-1].start()

    for layer in range(2):
        hops = 2**layer
        kernel = jnp.concatenate(
            [
                jnp.concatenate([w_ref[layer, a, b] for b in range(3)], axis=1)
                for a in range(3)
            ],
            axis=0,
        )
        for i in range(count):
            line = line_of(parts_ref, count, channels, 0, i) if layer == 0 else h_ref[i]
            stack = jnp.concatenate(taps(line, hops * share), axis=0)
            y_ref[i] = jnp.dot(kernel, stack, preferred_element_type=F32)
        bias = b_ref[layer]
        for i in range(count):
            pre = bias + y_ref[i, channels : 2 * channels]
            pre = pre + y_ref[(i - hops) % count, :channels]
            pre = pre + y_ref[(i + hops) % count, 2 * channels :]
            sigma = 1.0 / (1.0 + jnp.exp(-pre))
            state = (pre * sigma).astype(BF16)
            slope = sigma * (1.0 + pre * (1.0 - sigma))
            if layer == 0:
                h_ref[i] = state
                s0_ref[i] = slope
            else:
                s1_ref[i] = slope
                put(0, i, state)
    send(0, 0, count)

    for layer in (1, 0):
        hops = 2**layer
        kernel = jnp.concatenate(
            [
                jnp.concatenate([w_ref[layer, a, b].astype(F32).T for b in range(3)], axis=1)
                for a in range(3)
            ],
            axis=0,
        ).astype(BF16)
        for i in range(count):
            if layer == 1:
                gated = line_of(parts_ref, count, channels, 1, i).astype(F32) * s1_ref[i]
                gated = gated.astype(BF16)
                gz1_ref[i] = gated
            else:
                gated = gz0_ref[i]
            before, here, after = taps(gated, hops * share)
            stack = jnp.concatenate([after, here, before], axis=0)
            y_ref[i] = jnp.dot(kernel, stack, preferred_element_type=F32)
        for i in range(count):
            g = y_ref[i, channels : 2 * channels]
            g = g + y_ref[(i + hops) % count, :channels]
            g = g + y_ref[(i - hops) % count, 2 * channels :]
            g = g.astype(BF16)
            if layer == 1:
                gz0_ref[i] = (g.astype(F32) * s0_ref[i]).astype(BF16)
            else:
                put(1, i, g)
                send(1, i, 1)
    for copy in copies:
        copy.wait()


def quarters():
    lat = lax.axis_index("lat")
    odd, upper = lat & 1, lax.div(lat, 2) & 1
    mine = 2 * odd + upper
    other = 2 * (1 - odd) + upper
    return mine, 2 * odd + 1 - upper, other, 2 * (1 - odd) + 1 - upper


def sums_kernel(share, parts_ref, h_ref, gz0_ref, gz1_ref, keep_ref, send_ref, total_ref):
    count, channels, span = h_ref.shape
    ones = jnp.ones((16, span), BF16)
    high = 3 * channels
    bias_rows = [None, None]
    for layer, gz_ref in ((1, gz1_ref), (0, gz0_ref)):
        hops = 2**layer
        total = jnp.zeros((high, high), F32)
        bias = jnp.zeros((16, channels), F32)
        for i in range(count):
            gated = gz_ref[i]
            bias = bias + lax.dot_general(
                ones, gated, (((1,), (1,)), ((), ())), preferred_element_type=F32
            )
            before, here, after = taps(gated, hops * share)
            stack = jnp.concatenate([after, here, before], axis=0)
            around = [(i + (a - 1) * hops) % count for a in range(3)]
            lines = [
                line_of(parts_ref, count, channels, 0, j) if layer == 0 else h_ref[j]
                for j in around
            ]
            total = total + lax.dot_general(
                stack,
                jnp.concatenate(lines, axis=0),
                (((1,), (1,)), ((), ())),
                preferred_element_type=F32,
            )
        total_ref[layer * high : (layer + 1) * high, :] = total[:, : 2 * channels]
        total_ref[2 * high : 3 * high, layer * channels : (layer + 1) * channels] = total[
            :, 2 * channels :
        ]
        bias_rows[layer] = bias[:1]
    bias = jnp.concatenate(bias_rows, axis=1)
    row = lax.broadcasted_iota(jnp.int32, (TAIL, 2 * channels), 0)
    total_ref[3 * high :, :] = jnp.where(row == 0, bias, 0.0)
    size = keep_ref.shape[0] // 2
    for at, quarter in enumerate(quarters()):
        rows = total_ref[pl.ds(pl.multiple_of(quarter * size, 16), size), :]
        place = slice((at % 2) * size, (at % 2 + 1) * size)
        if at < 2:
            keep_ref[place, :] = rows
        else:
            send_ref[place, :] = rows.astype(BF16)


def assemble_kernel(scale, pair_ref, other_ref, out_ref, bias_ref, total_ref):
    channels = out_ref.shape[-1]
    size = pair_ref.shape[0] // 2
    for at, quarter in enumerate(quarters()):
        ref = pair_ref if at < 2 else other_ref
        rows = ref[(at % 2) * size : (at % 2 + 1) * size, :].astype(F32) * scale
        total_ref[pl.ds(pl.multiple_of(quarter * size, 16), size), :] = rows
    high = 3 * channels
    for layer in range(2):
        for b in range(3):
            first = layer * high + b * channels
            pair = total_ref[first : first + channels, :]
            out_ref[layer, 0, b] = pair[:, :channels]
            out_ref[layer, 1, b] = pair[:, channels:]
            first = 2 * high + b * channels
            third = total_ref[first : first + channels, :]
            out_ref[layer, 2, b] = third[:, layer * channels : (layer + 1) * channels]
    bias = total_ref[3 * high : 3 * high + 1, :]
    bias_ref[0:1, :] = bias[:, :channels]
    bias_ref[1:2, :] = bias[:, channels:]


def partnered(block, devices, bit):
    return lax.ppermute(block, AXES, [(i, i ^ bit) for i in range(devices)])


def added(keep, devices, send):
    size = keep.shape[0] // 2
    keep = keep + partnered(send, devices, 1).astype(F32)
    mine = keep[:size] + partnered(keep[size:].astype(BF16), devices, 2).astype(F32)
    bit = 4
    while bit < devices:
        rounded = mine.astype(BF16)
        mine = rounded.astype(F32) + partnered(rounded, devices, bit).astype(F32)
        bit *= 2
    mine = mine.astype(BF16)
    pair = jnp.concatenate([mine, partnered(mine, devices, 2)], axis=0)
    return pair, partnered(pair, devices, 1)


def exchanged(parts):
    return lax.all_to_all(parts, AXES, 0, 0, tiled=True)


def local(inputs, weights, biases, cotangent):
    channels, cols, lat_rows = inputs.shape
    lons, lats = lax.axis_size("lon"), lax.axis_size("lat")
    devices = lons * lats
    share = cols * cols // devices
    width = lat_rows // cols * share
    span = lats * width
    scale = 1.0 / math.sqrt(cols * lons * lat_rows * lats)
    blocks = lats if width % LANES == 0 else 1
    shape = jax.ShapeDtypeStruct

    chunks = 2 * channels // min(channels, 256 // cols)
    fields_shape = (devices, 2 * channels, width)
    hbm = pl.BlockSpec(memory_space=pltpu.HBM)
    vmem = pl.BlockSpec(memory_space=pltpu.VMEM)

    packed = pl.pallas_call(
        functools.partial(pack_kernel, share),
        out_shape=shape(fields_shape, BF16),
        in_specs=[hbm, hbm],
        out_specs=hbm,
        scratch_shapes=[
            pltpu.VMEM((2,) + inputs.shape, BF16),
            pltpu.VMEM(fields_shape, BF16),
            pltpu.SemaphoreType.DMA((chunks,)),
            pltpu.SemaphoreType.DMA((chunks,)),
        ],
        compiler_params=pltpu.CompilerParams(vmem_limit_bytes=56 * 2**20),
    )(inputs, cotangent)
    parts = exchanged(packed)
    if blocks == 1:
        parts = parts.reshape(lons, lats, 2 * channels, width).transpose(0, 2, 1, 3)
        parts = parts.reshape(lons, 2 * channels, span)

    cells = (lons, channels, span)
    fields, hidden, gated0, gated1 = pl.pallas_call(
        functools.partial(stack_kernel, share),
        out_shape=[shape(parts.shape, BF16)] + [shape(cells, BF16)] * 3,
        out_specs=[hbm, vmem, vmem, vmem],
        scratch_shapes=[
            pltpu.VMEM(cells, F32),
            pltpu.VMEM(cells, F32),
            pltpu.VMEM((lons, 3 * channels, span), F32),
            pltpu.VMEM(parts.shape, BF16),
            pltpu.SemaphoreType.DMA((lons + 1,)),
        ],
        compiler_params=PARAMS,
    )(parts, weights, biases[:, :, None])
    if blocks == 1:
        fields = fields.reshape(lons, 2 * channels, lats, width).transpose(0, 2, 1, 3)
        fields = fields.reshape(fields_shape)
    home = exchanged(fields)

    rows = 9 * channels + TAIL
    half_shape = (rows // 2, 2 * channels)
    flops = 2 * 2 * 9 * channels * parts.size // 2
    keep, send = pl.pallas_call(
        functools.partial(sums_kernel, share),
        out_shape=[shape(half_shape, F32), shape(half_shape, BF16)],
        scratch_shapes=[pltpu.VMEM((rows, 2 * channels), F32)],
        compiler_params=PARAMS,
        cost_estimate=pl.CostEstimate(flops=flops, bytes_accessed=5 * parts.size, transcendentals=0),
    )(parts, hidden, gated0, gated1)
    pair, other = added(keep, devices, send)
    weight_grads, bias_grads = pl.pallas_call(
        functools.partial(assemble_kernel, scale),
        out_shape=[shape(weights.shape, F32), shape(biases.shape, F32)],
        scratch_shapes=[pltpu.VMEM((rows, 2 * channels), F32)],
        compiler_params=PARAMS,
    )(pair, other)
    home, bias_grads = lax.optimization_barrier((home, bias_grads))
    features_out, grad_input = pl.pallas_call(
        functools.partial(unpack_kernel, share),
        out_shape=[shape(inputs.shape, BF16), shape(inputs.shape, BF16)],
        out_specs=[hbm, hbm],
        scratch_shapes=[
            pltpu.VMEM((2,) + inputs.shape, BF16),
            pltpu.SemaphoreType.DMA((chunks,)),
        ],
        compiler_params=PARAMS,
    )(home)
    return features_out, grad_input, weight_grads, bias_grads


def solution(mesh):
    in_specs = (P(None, "lon", "lat"), P(), P(), P(None, "lon", "lat"))
    out_specs = (P(None, "lon", "lat"), P(None, "lon", "lat"), P(), P())
    return jax.shard_map(local, mesh=mesh, in_specs=in_specs, out_specs=out_specs, check_vma=False)
```

```python
import functools
import math

import jax
import jax.numpy as jnp
from jax import lax
from jax.experimental import pallas as pl
from jax.experimental.pallas import tpu as pltpu
from jax.sharding import PartitionSpec as P


AXES = ("lon", "lat")
LANES = 128
TAIL = 64
BF16, F32 = jnp.bfloat16, jnp.float32
PARAMS = pltpu.CompilerParams(vmem_limit_bytes=24 * 2**20)
WIDE = pltpu.CompilerParams(vmem_limit_bytes=56 * 2**20)


def lane_order(cols, lat_rows, share, inverse):
    steps = lat_rows // cols
    place = lax.broadcasted_iota(jnp.int32, (lat_rows, lat_rows), 0 if inverse else 1)
    source = lax.broadcasted_iota(jnp.int32, (lat_rows, lat_rows), 1 if inverse else 0)
    group = lax.div(source & (cols - 1), share)
    wanted = (group * steps + lax.div(source, cols)) * share + (source & (share - 1))
    return (place == wanted).astype(F32).astype(BF16)


def row_order(outer, inner):
    rows = outer * inner
    place = lax.broadcasted_iota(jnp.int32, (rows, rows), 0)
    source = lax.broadcasted_iota(jnp.int32, (rows, rows), 1)
    wanted = (source & (inner - 1)) * outer + lax.div(source, inner)
    return (place == wanted).astype(F32).astype(BF16)


def product(left, right):
    return jnp.dot(left, right, preferred_element_type=F32)


def pack_kernel(share, x_ref, cot_ref, out_ref, buf, packed, in_sems, out_sems):
    _, channels, cols, lat_rows = buf.shape
    devices, _, width = packed.shape
    groups = devices // cols
    part = min(channels, 256 // cols)
    arrivals, departures = [], []
    for at, ref in enumerate((x_ref, cot_ref)):
        arrivals.append(pltpu.make_async_copy(ref, buf.at[at], in_sems.at[at]))
        rows = (slice(None), pl.ds(at * channels, channels), slice(None))
        departures.append(
            pltpu.make_async_copy(packed.at[rows], out_ref.at[rows], out_sems.at[at])
        )
        arrivals[at].start()
    lanes = lane_order(cols, lat_rows, share, False)
    order = row_order(part, cols)
    for at in range(2):
        arrivals[at].wait()
        for first in range(0, channels, part):
            rows = buf[at, first : first + part].reshape(part * cols, lat_rows)
            rows = product(order, rows).astype(BF16)
            rows = product(rows, lanes).astype(BF16)
            start = at * channels + first
            for col in range(cols):
                for group in range(groups):
                    packed[col * groups + group, start : start + part, :] = rows[
                        col * part : (col + 1) * part, group * width : (group + 1) * width
                    ]
        departures[at].start()
    for departure in departures:
        departure.wait()


def unpack_kernel(share, parts_ref, feat_ref, grad_ref, buf, sems):
    _, channels, cols, lat_rows = buf.shape
    devices, _, width = parts_ref.shape
    groups = devices // cols
    part = min(channels, 256 // cols)
    lanes = lane_order(cols, lat_rows, share, True)
    order = row_order(cols, part)
    departures = []
    for at, out_ref in enumerate((feat_ref, grad_ref)):
        for first in range(0, channels, part):
            start = at * channels + first
            rows = [
                jnp.concatenate(
                    [
                        parts_ref[col * groups + group, start : start + part, :]
                        for group in range(groups)
                    ],
                    axis=1,
                )
                for col in range(cols)
            ]
            rows = product(jnp.concatenate(rows, axis=0), lanes).astype(BF16)
            rows = product(order, rows).astype(BF16)
            buf[at, first : first + part] = rows.reshape(part, cols, lat_rows)
            rows = pl.ds(first, part)
            departures.append(
                pltpu.make_async_copy(buf.at[at, rows], out_ref.at[rows], sems.at[len(departures)])
            )
            departures[-1].start()
    for departure in departures:
        departure.wait()


def taps(row, shift):
    edge = jnp.zeros((row.shape[0], shift), row.dtype)
    before = jnp.concatenate([edge, row[:, :-shift]], axis=1)
    after = jnp.concatenate([row[:, shift:], edge], axis=1)
    return before, row, after


def line_of(parts_ref, count, channels, field, i):
    blocks = parts_ref.shape[0] // count
    rows = slice(field * channels, (field + 1) * channels)
    return jnp.concatenate([parts_ref[i * blocks + k, rows, :] for k in range(blocks)], axis=1)


def stack_kernel(
    share,
    parts_ref,
    w_ref,
    b_ref,
    out_ref,
    kept_ref,
    h_ref,
    gz0_ref,
    gz1_ref,
    s0_ref,
    s1_ref,
    y_ref,
    fields_ref,
    sems,
):
    count = h_ref.shape[0]
    channels = w_ref.shape[-1]
    devices, _, width = parts_ref.shape
    blocks = devices // count
    copies = []

    def put(field, i, line):
        rows = slice(field * channels, (field + 1) * channels)
        for k in range(blocks):
            fields_ref[i * blocks + k, rows, :] = line[:, k * width : (k + 1) * width]

    def copy(source, target):
        copies.append(pltpu.make_async_copy(source, target, sems.at[len(copies)]))
        copies[-1].start()

    def send(field, i, lines):
        place = (pl.ds(i * blocks, lines * blocks), pl.ds(field * channels, channels))
        copy(fields_ref.at[place], out_ref.at[place])

    for layer in range(2):
        hops = 2**layer
        kernel = jnp.concatenate(
            [
                jnp.concatenate([w_ref[layer, a, b] for b in range(3)], axis=1)
                for a in range(3)
            ],
            axis=0,
        )
        for i in range(count):
            line = line_of(parts_ref, count, channels, 0, i) if layer == 0 else h_ref[i]
            stack = jnp.concatenate(taps(line, hops * share), axis=0)
            y_ref[i] = jnp.dot(kernel, stack, preferred_element_type=F32)
        bias = b_ref[layer]
        for i in range(count):
            pre = bias + y_ref[i, channels : 2 * channels]
            pre = pre + y_ref[(i - hops) % count, :channels]
            pre = pre + y_ref[(i + hops) % count, 2 * channels :]
            sigma = 1.0 / (1.0 + jnp.exp(-pre))
            state = (pre * sigma).astype(BF16)
            slope = sigma * (1.0 + pre * (1.0 - sigma))
            if layer == 0:
                h_ref[i] = state
                s0_ref[i] = slope
            else:
                s1_ref[i] = slope
                put(0, i, state)
        if layer == 0:
            copy(h_ref, kept_ref.at[0])
    send(0, 0, count)

    for layer in (1, 0):
        hops = 2**layer
        kernel = jnp.concatenate(
            [
                jnp.concatenate([w_ref[layer, a, b].astype(F32).T for b in range(3)], axis=1)
                for a in range(3)
            ],
            axis=0,
        ).astype(BF16)
        for i in range(count):
            if layer == 1:
                gated = line_of(parts_ref, count, channels, 1, i).astype(F32) * s1_ref[i]
                gated = gated.astype(BF16)
                gz1_ref[i] = gated
            else:
                gated = gz0_ref[i]
            before, here, after = taps(gated, hops * share)
            stack = jnp.concatenate([after, here, before], axis=0)
            y_ref[i] = jnp.dot(kernel, stack, preferred_element_type=F32)
        for i in range(count):
            g = y_ref[i, channels : 2 * channels]
            g = g + y_ref[(i + hops) % count, :channels]
            g = g + y_ref[(i - hops) % count, 2 * channels :]
            g = g.astype(BF16)
            if layer == 1:
                gz0_ref[i] = (g.astype(F32) * s0_ref[i]).astype(BF16)
            else:
                put(1, i, g)
                send(1, i, 1)
        if layer == 1:
            copy(gz1_ref, kept_ref.at[1])
            copy(gz0_ref, kept_ref.at[2])
    for started in copies:
        started.wait()


def quarters():
    lat = lax.axis_index("lat")
    odd, upper = lat & 1, lax.div(lat, 2) & 1
    mine = 2 * odd + upper
    other = 2 * (1 - odd) + upper
    return mine, 2 * odd + 1 - upper, other, 2 * (1 - odd) + 1 - upper


def sums_kernel(share, parts_ref, kept_ref, keep_ref, *refs):
    send_refs, (buf, total_ref, sems) = refs[:3], refs[3:]
    _, count, channels, span = buf.shape
    h_ref, gz1_ref, gz0_ref = buf.at[0], buf.at[1], buf.at[2]
    copies = [pltpu.make_async_copy(kept_ref.at[k], buf.at[k], sems.at[k]) for k in range(3)]
    for copy in copies:
        copy.start()
    for copy in copies:
        copy.wait()
    ones = jnp.ones((16, span), BF16)
    high = 3 * channels
    bias_rows = [None, None]
    for layer, gz_ref in ((1, gz1_ref), (0, gz0_ref)):
        hops = 2**layer
        total = jnp.zeros((high, high), F32)
        bias = jnp.zeros((16, channels), F32)
        for i in range(count):
            gated = gz_ref[i]
            bias = bias + lax.dot_general(
                ones, gated, (((1,), (1,)), ((), ())), preferred_element_type=F32
            )
            before, here, after = taps(gated, hops * share)
            stack = jnp.concatenate([after, here, before], axis=0)
            around = [(i + (a - 1) * hops) % count for a in range(3)]
            lines = [
                line_of(parts_ref, count, channels, 0, j) if layer == 0 else h_ref[j]
                for j in around
            ]
            total = total + lax.dot_general(
                stack,
                jnp.concatenate(lines, axis=0),
                (((1,), (1,)), ((), ())),
                preferred_element_type=F32,
            )
        total_ref[layer * high : (layer + 1) * high, :] = total[:, : 2 * channels]
        total_ref[2 * high : 3 * high, layer * channels : (layer + 1) * channels] = total[
            :, 2 * channels :
        ]
        bias_rows[layer] = bias[:1]
    bias = jnp.concatenate(bias_rows, axis=1)
    row = lax.broadcasted_iota(jnp.int32, (TAIL, 2 * channels), 0)
    total_ref[3 * high :, :] = jnp.where(row == 0, bias, 0.0)
    size = keep_ref.shape[0]
    for at, quarter in enumerate(quarters()):
        rows = total_ref[pl.ds(pl.multiple_of(quarter * size, 16), size), :]
        if at == 0:
            keep_ref[...] = rows
        else:
            send_refs[at - 1][...] = rows.astype(BF16)


def assemble_kernel(scale, *refs):
    quarter_refs, (out_ref, bias_ref, total_ref) = refs[:4], refs[4:]
    channels = out_ref.shape[-1]
    size = quarter_refs[0].shape[0]
    for quarter, ref in zip(quarters(), quarter_refs):
        rows = ref[...].astype(F32) * scale
        total_ref[pl.ds(pl.multiple_of(quarter * size, 16), size), :] = rows
    high = 3 * channels
    for layer in range(2):
        for b in range(3):
            first = layer * high + b * channels
            pair = total_ref[first : first + channels, :]
            out_ref[layer, 0, b] = pair[:, :channels]
            out_ref[layer, 1, b] = pair[:, channels:]
            first = 2 * high + b * channels
            third = total_ref[first : first + channels, :]
            out_ref[layer, 2, b] = third[:, layer * channels : (layer + 1) * channels]
    bias = total_ref[3 * high : 3 * high + 1, :]
    bias_ref[0:1, :] = bias[:, :channels]
    bias_ref[1:2, :] = bias[:, channels:]


def partnered(block, devices, bit):
    return lax.ppermute(block, AXES, [(i, i ^ bit) for i in range(devices)])


def added(keep, sends, devices):
    bits = (2, 1, 3)
    came = [partnered(send, devices, bit).astype(F32) for send, bit in zip(sends, bits)]
    mine = (keep + came[0]) + (came[1] + came[2])
    low = 4
    while low < devices:
        high = 2 * low if 2 * low < devices else 0
        rounded = mine.astype(BF16)
        mine = rounded.astype(F32)
        if high:
            far = partnered(rounded, devices, high)
            across = partnered(rounded, devices, low + high)
            mine = mine + partnered(rounded, devices, low).astype(F32)
            mine = mine + (far.astype(F32) + across.astype(F32))
        else:
            mine = mine + partnered(rounded, devices, low).astype(F32)
        low *= 4
    mine = mine.astype(BF16)
    return [mine] + [partnered(mine, devices, bit) for bit in bits]


def exchanged(parts):
    return lax.all_to_all(parts, AXES, 0, 0, tiled=True)


def local(inputs, weights, biases, cotangent):
    channels, cols, lat_rows = inputs.shape
    lons, lats = lax.axis_size("lon"), lax.axis_size("lat")
    devices = lons * lats
    share = cols * cols // devices
    width = lat_rows // cols * share
    span = lats * width
    scale = 1.0 / math.sqrt(cols * lons * lat_rows * lats)
    blocks = lats if width % LANES == 0 else 1
    shape = jax.ShapeDtypeStruct

    chunks = 2 * channels // min(channels, 256 // cols)
    fields_shape = (devices, 2 * channels, width)
    hbm = pl.BlockSpec(memory_space=pltpu.HBM)
    vmem = pl.BlockSpec(memory_space=pltpu.VMEM)

    packed = pl.pallas_call(
        functools.partial(pack_kernel, share),
        out_shape=shape(fields_shape, BF16),
        in_specs=[hbm, hbm],
        out_specs=hbm,
        scratch_shapes=[
            pltpu.VMEM((2,) + inputs.shape, BF16),
            pltpu.VMEM(fields_shape, BF16),
            pltpu.SemaphoreType.DMA((2,)),
            pltpu.SemaphoreType.DMA((2,)),
        ],
        compiler_params=WIDE,
    )(inputs, cotangent)
    parts = exchanged(packed)
    if blocks == 1:
        parts = parts.reshape(lons, lats, 2 * channels, width).transpose(0, 2, 1, 3)
        parts = parts.reshape(lons, 2 * channels, span)

    cells = (lons, channels, span)
    fields, kept = pl.pallas_call(
        functools.partial(stack_kernel, share),
        out_shape=[shape(parts.shape, BF16), shape((3,) + cells, BF16)],
        out_specs=[hbm, hbm],
        scratch_shapes=[
            pltpu.VMEM(cells, BF16),
            pltpu.VMEM(cells, BF16),
            pltpu.VMEM(cells, BF16),
            pltpu.VMEM(cells, F32),
            pltpu.VMEM(cells, F32),
            pltpu.VMEM((lons, 3 * channels, span), F32),
            pltpu.VMEM(parts.shape, BF16),
            pltpu.SemaphoreType.DMA((lons + 4,)),
        ],
        compiler_params=PARAMS,
    )(parts, weights, biases[:, :, None])
    if blocks == 1:
        fields = fields.reshape(lons, 2 * channels, lats, width).transpose(0, 2, 1, 3)
        fields = fields.reshape(fields_shape)
    home = exchanged(fields)

    rows = 9 * channels + TAIL
    quarter_shape = (rows // 4, 2 * channels)
    flops = 2 * 2 * 9 * channels * parts.size // 2
    keep, *sends = pl.pallas_call(
        functools.partial(sums_kernel, share),
        out_shape=[shape(quarter_shape, F32)] + [shape(quarter_shape, BF16)] * 3,
        in_specs=[vmem, hbm],
        scratch_shapes=[
            pltpu.VMEM((3,) + cells, BF16),
            pltpu.VMEM((rows, 2 * channels), F32),
            pltpu.SemaphoreType.DMA((3,)),
        ],
        compiler_params=PARAMS,
        cost_estimate=pl.CostEstimate(flops=flops, bytes_accessed=5 * parts.size, transcendentals=0),
    )(parts, kept)
    weight_grads, bias_grads = pl.pallas_call(
        functools.partial(assemble_kernel, scale),
        out_shape=[shape(weights.shape, F32), shape(biases.shape, F32)],
        scratch_shapes=[pltpu.VMEM((rows, 2 * channels), F32)],
        compiler_params=PARAMS,
    )(*added(keep, sends, devices))
    home, bias_grads = lax.optimization_barrier((home, bias_grads))
    features_out, grad_input = pl.pallas_call(
        functools.partial(unpack_kernel, share),
        out_shape=[shape(inputs.shape, BF16), shape(inputs.shape, BF16)],
        out_specs=[hbm, hbm],
        scratch_shapes=[
            pltpu.VMEM((2,) + inputs.shape, BF16),
            pltpu.SemaphoreType.DMA((chunks,)),
        ],
        compiler_params=PARAMS,
    )(home)
    return features_out, grad_input, weight_grads, bias_grads


def solution(mesh):
    in_specs = (P(None, "lon", "lat"), P(), P(), P(None, "lon", "lat"))
    out_specs = (P(None, "lon", "lat"), P(None, "lon", "lat"), P(), P())
    return jax.shard_map(local, mesh=mesh, in_specs=in_specs, out_specs=out_specs, check_vma=False)
```

```python
import functools
import math

import jax
import jax.numpy as jnp
from jax import lax
from jax.experimental import pallas as pl
from jax.experimental.pallas import tpu as pltpu
from jax.sharding import PartitionSpec as P


AXES = ("lon", "lat")
LANES = 128
TAIL = 64
QUARTERS = (2, 1, 3)
BF16, F32 = jnp.bfloat16, jnp.float32
PARAMS = pltpu.CompilerParams(vmem_limit_bytes=24 * 2**20)
MIDDLE = pltpu.CompilerParams(vmem_limit_bytes=207 * 2**18)
WIDE = pltpu.CompilerParams(vmem_limit_bytes=56 * 2**20)


def lane_order(cols, lat_rows, share, inverse):
    steps = lat_rows // cols
    place = lax.broadcasted_iota(jnp.int32, (lat_rows, lat_rows), 0 if inverse else 1)
    source = lax.broadcasted_iota(jnp.int32, (lat_rows, lat_rows), 1 if inverse else 0)
    group = lax.div(source & (cols - 1), share)
    wanted = (group * steps + lax.div(source, cols)) * share + (source & (share - 1))
    return (place == wanted).astype(F32).astype(BF16)


def row_order(outer, inner):
    rows = outer * inner
    place = lax.broadcasted_iota(jnp.int32, (rows, rows), 0)
    source = lax.broadcasted_iota(jnp.int32, (rows, rows), 1)
    wanted = (source & (inner - 1)) * outer + lax.div(source, inner)
    return (place == wanted).astype(F32).astype(BF16)


def product(left, right):
    return jnp.dot(left, right, preferred_element_type=F32)


def pack_kernel(share, x_ref, cot_ref, out_ref, buf, packed, in_sems, out_sems):
    _, channels, cols, lat_rows = buf.shape
    devices, _, width = packed.shape
    groups = devices // cols
    part = min(channels, 256 // cols)
    arrivals, departures = [], []
    for at, ref in enumerate((x_ref, cot_ref)):
        arrivals.append(pltpu.make_async_copy(ref, buf.at[at], in_sems.at[at]))
        rows = (slice(None), pl.ds(at * channels, channels), slice(None))
        departures.append(
            pltpu.make_async_copy(packed.at[rows], out_ref.at[rows], out_sems.at[at])
        )
        arrivals[at].start()
    lanes = lane_order(cols, lat_rows, share, False)
    order = row_order(part, cols)
    for at in range(2):
        arrivals[at].wait()
        for first in range(0, channels, part):
            rows = buf[at, first : first + part].reshape(part * cols, lat_rows)
            rows = product(order, rows).astype(BF16)
            rows = product(rows, lanes).astype(BF16)
            start = at * channels + first
            for col in range(cols):
                for group in range(groups):
                    packed[col * groups + group, start : start + part, :] = rows[
                        col * part : (col + 1) * part, group * width : (group + 1) * width
                    ]
        departures[at].start()
    for departure in departures:
        departure.wait()


def unpack_kernel(share, parts_ref, feat_ref, grad_ref, buf, sems):
    _, channels, cols, lat_rows = buf.shape
    devices, _, width = parts_ref.shape
    groups = devices // cols
    part = min(channels, 256 // cols)
    lanes = lane_order(cols, lat_rows, share, True)
    order = row_order(cols, part)
    departures = []
    for at, out_ref in enumerate((feat_ref, grad_ref)):
        for first in range(0, channels, part):
            start = at * channels + first
            rows = [
                jnp.concatenate(
                    [
                        parts_ref[col * groups + group, start : start + part, :]
                        for group in range(groups)
                    ],
                    axis=1,
                )
                for col in range(cols)
            ]
            rows = product(jnp.concatenate(rows, axis=0), lanes).astype(BF16)
            rows = product(order, rows).astype(BF16)
            buf[at, first : first + part] = rows.reshape(part, cols, lat_rows)
            rows = pl.ds(first, part)
            departures.append(
                pltpu.make_async_copy(buf.at[at, rows], out_ref.at[rows], sems.at[len(departures)])
            )
            departures[-1].start()
    for departure in departures:
        departure.wait()


def taps(row, shift):
    edge = jnp.zeros((row.shape[0], shift), row.dtype)
    before = jnp.concatenate([edge, row[:, :-shift]], axis=1)
    after = jnp.concatenate([row[:, shift:], edge], axis=1)
    return before, row, after


def line_of(parts_ref, count, channels, field, i):
    blocks = parts_ref.shape[0] // count
    rows = slice(field * channels, (field + 1) * channels)
    return jnp.concatenate([parts_ref[i * blocks + k, rows, :] for k in range(blocks)], axis=1)


def stack_kernel(
    share,
    parts_ref,
    w_ref,
    b_ref,
    out_ref,
    kept_ref,
    h_ref,
    gz0_ref,
    gz1_ref,
    s0_ref,
    s1_ref,
    y_ref,
    fields_ref,
    sems,
):
    count = h_ref.shape[0]
    channels = w_ref.shape[-1]
    devices, _, width = parts_ref.shape
    blocks = devices // count
    copies = []

    def put(field, i, line):
        rows = slice(field * channels, (field + 1) * channels)
        for k in range(blocks):
            fields_ref[i * blocks + k, rows, :] = line[:, k * width : (k + 1) * width]

    def copy(source, target):
        copies.append(pltpu.make_async_copy(source, target, sems.at[len(copies)]))
        copies[-1].start()

    def send(field, i, lines):
        place = (pl.ds(i * blocks, lines * blocks), pl.ds(field * channels, channels))
        copy(fields_ref.at[place], out_ref.at[place])

    for layer in range(2):
        hops = 2**layer
        kernel = jnp.concatenate(
            [
                jnp.concatenate([w_ref[layer, a, b] for b in range(3)], axis=1)
                for a in range(3)
            ],
            axis=0,
        )
        for i in range(count):
            line = line_of(parts_ref, count, channels, 0, i) if layer == 0 else h_ref[i]
            stack = jnp.concatenate(taps(line, hops * share), axis=0)
            y_ref[i] = jnp.dot(kernel, stack, preferred_element_type=F32)
        bias = b_ref[layer]
        for i in range(count):
            pre = bias + y_ref[i, channels : 2 * channels]
            pre = pre + y_ref[(i - hops) % count, :channels]
            pre = pre + y_ref[(i + hops) % count, 2 * channels :]
            sigma = 1.0 / (1.0 + jnp.exp(-pre))
            state = (pre * sigma).astype(BF16)
            slope = sigma * (1.0 + pre * (1.0 - sigma))
            if layer == 0:
                h_ref[i] = state
                s0_ref[i] = slope
            else:
                s1_ref[i] = slope
                put(0, i, state)
        if layer == 0:
            copy(h_ref, kept_ref.at[0])
    send(0, 0, count)

    for layer in (1, 0):
        hops = 2**layer
        kernel = jnp.concatenate(
            [
                jnp.concatenate([w_ref[layer, a, b].astype(F32).T for b in range(3)], axis=1)
                for a in range(3)
            ],
            axis=0,
        ).astype(BF16)
        for i in range(count):
            if layer == 1:
                gated = line_of(parts_ref, count, channels, 1, i).astype(F32) * s1_ref[i]
                gated = gated.astype(BF16)
                gz1_ref[i] = gated
            else:
                gated = gz0_ref[i]
            before, here, after = taps(gated, hops * share)
            stack = jnp.concatenate([after, here, before], axis=0)
            y_ref[i] = jnp.dot(kernel, stack, preferred_element_type=F32)
        for i in range(count):
            g = y_ref[i, channels : 2 * channels]
            g = g + y_ref[(i + hops) % count, :channels]
            g = g + y_ref[(i - hops) % count, 2 * channels :]
            g = g.astype(BF16)
            if layer == 1:
                gz0_ref[i] = (g.astype(F32) * s0_ref[i]).astype(BF16)
            else:
                put(1, i, g)
                send(1, i, 1)
        if layer == 1:
            copy(gz1_ref, kept_ref.at[1])
            copy(gz0_ref, kept_ref.at[2])
    for started in copies:
        started.wait()


def quarters():
    lat = lax.axis_index("lat")
    odd, upper = lat & 1, lax.div(lat, 2) & 1
    mine = 2 * odd + upper
    other = 2 * (1 - odd) + upper
    return mine, 2 * odd + 1 - upper, other, 2 * (1 - odd) + 1 - upper


def sums_kernel(share, parts_ref, kept_ref, keep_ref, *refs):
    send_refs, (buf, total_ref, sems) = refs[:3], refs[3:]
    _, count, channels, span = buf.shape
    h_ref, gz1_ref, gz0_ref = buf.at[0], buf.at[1], buf.at[2]
    copies = [pltpu.make_async_copy(kept_ref.at[k], buf.at[k], sems.at[k]) for k in range(3)]
    for copy in copies:
        copy.start()
    copies[0].wait()
    copies[1].wait()
    ones = jnp.ones((16, span), BF16)
    high = 3 * channels
    bias_rows = [None, None]
    for layer, gz_ref in ((1, gz1_ref), (0, gz0_ref)):
        hops = 2**layer
        if layer == 0:
            copies[2].wait()
        total = jnp.zeros((high, high), F32)
        bias = jnp.zeros((16, channels), F32)
        for i in range(count):
            gated = gz_ref[i]
            bias = bias + lax.dot_general(
                ones, gated, (((1,), (1,)), ((), ())), preferred_element_type=F32
            )
            before, here, after = taps(gated, hops * share)
            stack = jnp.concatenate([after, here, before], axis=0)
            around = [(i + (a - 1) * hops) % count for a in range(3)]
            lines = [
                line_of(parts_ref, count, channels, 0, j) if layer == 0 else h_ref[j]
                for j in around
            ]
            total = total + lax.dot_general(
                stack,
                jnp.concatenate(lines, axis=0),
                (((1,), (1,)), ((), ())),
                preferred_element_type=F32,
            )
        total_ref[layer * high : (layer + 1) * high, :] = total[:, : 2 * channels]
        total_ref[2 * high : 3 * high, layer * channels : (layer + 1) * channels] = total[
            :, 2 * channels :
        ]
        bias_rows[layer] = bias[:1]
    bias = jnp.concatenate(bias_rows, axis=1)
    row = lax.broadcasted_iota(jnp.int32, (TAIL, 2 * channels), 0)
    total_ref[3 * high :, :] = jnp.where(row == 0, bias, 0.0)
    size = keep_ref.shape[0]
    for at, quarter in enumerate(quarters()):
        rows = total_ref[pl.ds(pl.multiple_of(quarter * size, 16), size), :]
        if at == 0:
            keep_ref[...] = rows
        else:
            send_refs[at - 1][...] = rows.astype(BF16)


def assemble_kernel(scale, *refs):
    quarter_refs, (out_ref, bias_ref, total_ref) = refs[:4], refs[4:]
    channels = out_ref.shape[-1]
    size = quarter_refs[0].shape[0]
    for quarter, ref in zip(quarters(), quarter_refs):
        rows = ref[...].astype(F32) * scale
        total_ref[pl.ds(pl.multiple_of(quarter * size, 16), size), :] = rows
    high = 3 * channels
    for layer in range(2):
        for b in range(3):
            first = layer * high + b * channels
            pair = total_ref[first : first + channels, :]
            out_ref[layer, 0, b] = pair[:, :channels]
            out_ref[layer, 1, b] = pair[:, channels:]
            first = 2 * high + b * channels
            third = total_ref[first : first + channels, :]
            out_ref[layer, 2, b] = third[:, layer * channels : (layer + 1) * channels]
    bias = total_ref[3 * high : 3 * high + 1, :]
    bias_ref[0:1, :] = bias[:, :channels]
    bias_ref[1:2, :] = bias[:, channels:]


def partnered(block, devices, bit):
    return lax.ppermute(block, AXES, [(i, i ^ bit) for i in range(devices)])


def added(keep, sends, devices):
    came = [partnered(send, devices, bit).astype(F32) for send, bit in zip(sends, QUARTERS)]
    mine = (keep + came[0]) + (came[1] + came[2])
    low = 4
    while low < devices:
        high = 2 * low if 2 * low < devices else 0
        rounded = mine.astype(BF16)
        mine = rounded.astype(F32)
        if high:
            far = partnered(rounded, devices, high)
            across = partnered(rounded, devices, low + high)
            mine = mine + partnered(rounded, devices, low).astype(F32)
            mine = mine + (far.astype(F32) + across.astype(F32))
        else:
            mine = mine + partnered(rounded, devices, low).astype(F32)
        low *= 4
    return mine.astype(BF16)


def exchanged(parts):
    return lax.all_to_all(parts, AXES, 0, 0, tiled=True)


def local(inputs, weights, biases, cotangent):
    channels, cols, lat_rows = inputs.shape
    lons, lats = lax.axis_size("lon"), lax.axis_size("lat")
    devices = lons * lats
    share = cols * cols // devices
    width = lat_rows // cols * share
    span = lats * width
    scale = 1.0 / math.sqrt(cols * lons * lat_rows * lats)
    blocks = lats if width % LANES == 0 else 1
    shape = jax.ShapeDtypeStruct

    chunks = 2 * channels // min(channels, 256 // cols)
    fields_shape = (devices, 2 * channels, width)
    hbm = pl.BlockSpec(memory_space=pltpu.HBM)
    vmem = pl.BlockSpec(memory_space=pltpu.VMEM)

    packed = pl.pallas_call(
        functools.partial(pack_kernel, share),
        out_shape=shape(fields_shape, BF16),
        in_specs=[hbm, hbm],
        out_specs=hbm,
        scratch_shapes=[
            pltpu.VMEM((2,) + inputs.shape, BF16),
            pltpu.VMEM(fields_shape, BF16),
            pltpu.SemaphoreType.DMA((2,)),
            pltpu.SemaphoreType.DMA((2,)),
        ],
        compiler_params=WIDE,
    )(inputs, cotangent)
    parts = exchanged(packed)
    if blocks == 1:
        parts = parts.reshape(lons, lats, 2 * channels, width).transpose(0, 2, 1, 3)
        parts = parts.reshape(lons, 2 * channels, span)

    cells = (lons, channels, span)
    fields, kept = pl.pallas_call(
        functools.partial(stack_kernel, share),
        out_shape=[shape(parts.shape, BF16), shape((3,) + cells, BF16)],
        out_specs=[hbm, hbm],
        scratch_shapes=[
            pltpu.VMEM(cells, BF16),
            pltpu.VMEM(cells, BF16),
            pltpu.VMEM(cells, BF16),
            pltpu.VMEM(cells, F32),
            pltpu.VMEM(cells, F32),
            pltpu.VMEM((lons, 3 * channels, span), F32),
            pltpu.VMEM(parts.shape, BF16),
            pltpu.SemaphoreType.DMA((lons + 4,)),
        ],
        compiler_params=MIDDLE,
    )(parts, weights, biases[:, :, None])
    if blocks == 1:
        fields = fields.reshape(lons, 2 * channels, lats, width).transpose(0, 2, 1, 3)
        fields = fields.reshape(fields_shape)
    home = exchanged(fields)

    rows = 9 * channels + TAIL
    quarter_shape = (rows // 4, 2 * channels)
    flops = 2 * 2 * 9 * channels * parts.size // 2
    keep, *sends = pl.pallas_call(
        functools.partial(sums_kernel, share),
        out_shape=[shape(quarter_shape, F32)] + [shape(quarter_shape, BF16)] * 3,
        in_specs=[vmem, hbm],
        scratch_shapes=[
            pltpu.VMEM((3,) + cells, BF16),
            pltpu.VMEM((rows, 2 * channels), F32),
            pltpu.SemaphoreType.DMA((3,)),
        ],
        compiler_params=PARAMS,
        cost_estimate=pl.CostEstimate(flops=flops, bytes_accessed=5 * parts.size, transcendentals=0),
    )(parts, kept)
    mine = added(keep, sends, devices)
    home, mine = lax.optimization_barrier((home, mine))
    others = [partnered(mine, devices, bit) for bit in QUARTERS]
    features_out, grad_input = pl.pallas_call(
        functools.partial(unpack_kernel, share),
        out_shape=[shape(inputs.shape, BF16), shape(inputs.shape, BF16)],
        out_specs=[hbm, hbm],
        scratch_shapes=[
            pltpu.VMEM((2,) + inputs.shape, BF16),
            pltpu.SemaphoreType.DMA((chunks,)),
        ],
        compiler_params=PARAMS,
        cost_estimate=pl.CostEstimate(
            flops=4 * inputs.size * lat_rows, bytes_accessed=8 * inputs.size, transcendentals=0
        ),
    )(home)
    weight_grads, bias_grads = pl.pallas_call(
        functools.partial(assemble_kernel, scale),
        out_shape=[shape(weights.shape, F32), shape(biases.shape, F32)],
        scratch_shapes=[pltpu.VMEM((rows, 2 * channels), F32)],
        compiler_params=PARAMS,
    )(mine, *others)
    return features_out, grad_input, weight_grads, bias_grads


def solution(mesh):
    in_specs = (P(None, "lon", "lat"), P(), P(), P(None, "lon", "lat"))
    out_specs = (P(None, "lon", "lat"), P(None, "lon", "lat"), P(), P())
    return jax.shard_map(local, mesh=mesh, in_specs=in_specs, out_specs=out_specs, check_vma=False)
```

```python
import functools
import math

import jax
import jax.numpy as jnp
from jax import lax
from jax.experimental import pallas as pl
from jax.experimental.pallas import tpu as pltpu
from jax.sharding import PartitionSpec as P


AXES = ("lon", "lat")
LANES = 128
TAIL = 64
QUARTERS = (2, 1, 3)
BF16, F32 = jnp.bfloat16, jnp.float32
PARAMS = pltpu.CompilerParams(vmem_limit_bytes=24 * 2**20)
WIDE = pltpu.CompilerParams(vmem_limit_bytes=56 * 2**20)


def lane_order(cols, lat_rows, share, inverse):
    steps = lat_rows // cols
    place = lax.broadcasted_iota(jnp.int32, (lat_rows, lat_rows), 0 if inverse else 1)
    source = lax.broadcasted_iota(jnp.int32, (lat_rows, lat_rows), 1 if inverse else 0)
    group = lax.div(source & (cols - 1), share)
    wanted = (group * steps + lax.div(source, cols)) * share + (source & (share - 1))
    return (place == wanted).astype(F32).astype(BF16)


def row_order(outer, inner):
    rows = outer * inner
    place = lax.broadcasted_iota(jnp.int32, (rows, rows), 0)
    source = lax.broadcasted_iota(jnp.int32, (rows, rows), 1)
    wanted = (source & (inner - 1)) * outer + lax.div(source, inner)
    return (place == wanted).astype(F32).astype(BF16)


def product(left, right):
    return jnp.dot(left, right, preferred_element_type=F32)


def pack_kernel(share, x_ref, cot_ref, out_ref, buf, packed, in_sems, out_sems):
    _, channels, cols, lat_rows = buf.shape
    devices, _, width = packed.shape
    groups = devices // cols
    part = min(channels, 256 // cols)
    arrivals, departures = [], []
    for at, ref in enumerate((x_ref, cot_ref)):
        arrivals.append(pltpu.make_async_copy(ref, buf.at[at], in_sems.at[at]))
        rows = (slice(None), pl.ds(at * channels, channels), slice(None))
        departures.append(
            pltpu.make_async_copy(packed.at[rows], out_ref.at[rows], out_sems.at[at])
        )
        arrivals[at].start()
    lanes = lane_order(cols, lat_rows, share, False)
    order = row_order(part, cols)
    for at in range(2):
        arrivals[at].wait()
        for first in range(0, channels, part):
            rows = buf[at, first : first + part].reshape(part * cols, lat_rows)
            rows = product(order, rows).astype(BF16)
            rows = product(rows, lanes).astype(BF16)
            start = at * channels + first
            for col in range(cols):
                for group in range(groups):
                    packed[col * groups + group, start : start + part, :] = rows[
                        col * part : (col + 1) * part, group * width : (group + 1) * width
                    ]
        departures[at].start()
    for departure in departures:
        departure.wait()


def unpack_kernel(share, parts_ref, feat_ref, grad_ref, buf, sems):
    _, channels, cols, lat_rows = buf.shape
    devices, _, width = parts_ref.shape
    groups = devices // cols
    part = min(channels, 256 // cols)
    lanes = lane_order(cols, lat_rows, share, True)
    order = row_order(cols, part)
    departures = []
    for at, out_ref in enumerate((feat_ref, grad_ref)):
        for first in range(0, channels, part):
            start = at * channels + first
            rows = [
                jnp.concatenate(
                    [
                        parts_ref[col * groups + group, start : start + part, :]
                        for group in range(groups)
                    ],
                    axis=1,
                )
                for col in range(cols)
            ]
            rows = product(jnp.concatenate(rows, axis=0), lanes).astype(BF16)
            rows = product(order, rows).astype(BF16)
            buf[at, first : first + part] = rows.reshape(part, cols, lat_rows)
            rows = pl.ds(first, part)
            departures.append(
                pltpu.make_async_copy(buf.at[at, rows], out_ref.at[rows], sems.at[len(departures)])
            )
            departures[-1].start()
    for departure in departures:
        departure.wait()


def taps(row, shift):
    edge = jnp.zeros((row.shape[0], shift), row.dtype)
    before = jnp.concatenate([edge, row[:, :-shift]], axis=1)
    after = jnp.concatenate([row[:, shift:], edge], axis=1)
    return before, row, after


def kernels_kernel(w_ref, out_ref):
    for layer in range(2):
        for back in range(2):
            rows = []
            for a in range(3):
                row = [w_ref[layer, a, b] for b in range(3)]
                if back:
                    row = [tap.astype(F32).T.astype(BF16) for tap in row]
                rows.append(jnp.concatenate(row, axis=1))
            out_ref[2 * layer + back] = jnp.concatenate(rows, axis=0)


def line_of(parts_ref, count, channels, field, i):
    blocks = parts_ref.shape[0] // count
    rows = slice(field * channels, (field + 1) * channels)
    return jnp.concatenate([parts_ref[i * blocks + k, rows, :] for k in range(blocks)], axis=1)


def weight_product(gated, stack, lines):
    ones = jnp.ones((16, gated.shape[1]), BF16)
    across = (((1,), (1,)), ((), ()))
    bias = lax.dot_general(ones, gated, across, preferred_element_type=F32)
    lines = jnp.concatenate(lines, axis=0)
    return lax.dot_general(stack, lines, across, preferred_element_type=F32), bias


def back_taps(gated, shift):
    before, here, after = taps(gated, shift)
    return jnp.concatenate([after, here, before], axis=0)


def stack_kernel(
    share,
    parts_ref,
    w_ref,
    b_ref,
    out_ref,
    gz_ref,
    total_ref,
    bias_ref,
    h_ref,
    s0_ref,
    s1_ref,
    y_ref,
    fields_ref,
    sems,
):
    count, channels, _ = h_ref.shape
    devices, _, width = parts_ref.shape
    blocks = devices // count
    copies = []

    def put(field, i, line):
        rows = slice(field * channels, (field + 1) * channels)
        for k in range(blocks):
            fields_ref[i * blocks + k, rows, :] = line[:, k * width : (k + 1) * width]

    def send(field, i, lines):
        place = (pl.ds(i * blocks, lines * blocks), pl.ds(field * channels, channels))
        copies.append(
            pltpu.make_async_copy(fields_ref.at[place], out_ref.at[place], sems.at[len(copies)])
        )
        copies[-1].start()

    for layer in range(2):
        hops = 2**layer
        kernel = w_ref[2 * layer]
        for i in range(count):
            line = line_of(parts_ref, count, channels, 0, i) if layer == 0 else h_ref[i]
            stack = jnp.concatenate(taps(line, hops * share), axis=0)
            y_ref[i] = product(kernel, stack)
        bias = b_ref[layer]
        for i in range(count):
            pre = bias + y_ref[i, channels : 2 * channels]
            pre = pre + y_ref[(i - hops) % count, :channels]
            pre = pre + y_ref[(i + hops) % count, 2 * channels :]
            sigma = 0.5 * jnp.tanh(0.5 * pre) + 0.5
            state = pre * sigma
            slope = sigma + state * (1.0 - sigma)
            if layer == 0:
                h_ref[i] = state.astype(BF16)
                s0_ref[i] = slope
            else:
                s1_ref[i] = slope
                put(0, i, state.astype(BF16))
    send(0, 0, count)

    total, bias = 0.0, 0.0
    for layer in (1, 0):
        hops = 2**layer
        kernel = w_ref[2 * layer + 1]
        for i in range(count):
            if layer == 1:
                gated = line_of(parts_ref, count, channels, 1, i).astype(F32) * s1_ref[i]
                gated = gated.astype(BF16)
            else:
                gated = gz_ref[i]
            stack = back_taps(gated, hops * share)
            y_ref[i] = product(kernel, stack)
            if layer == 1:
                around = [h_ref[(i + (a - 1) * hops) % count] for a in range(3)]
                term, bias_term = weight_product(gated, stack, around)
                total, bias = total + term, bias + bias_term
        for i in range(count):
            g = y_ref[i, channels : 2 * channels]
            g = g + y_ref[(i + hops) % count, :channels]
            g = g + y_ref[(i - hops) % count, 2 * channels :]
            g = g.astype(BF16)
            if layer == 1:
                gz_ref[i] = (g.astype(F32) * s0_ref[i]).astype(BF16)
            else:
                put(1, i, g)
                send(1, i, 1)
        if layer == 1:
            total_ref[...] = total
            bias_ref[...] = bias
    for started in copies:
        started.wait()


def quarters():
    lat = lax.axis_index("lat")
    odd, upper = lat & 1, lax.div(lat, 2) & 1
    mine = 2 * odd + upper
    other = 2 * (1 - odd) + upper
    return mine, 2 * odd + 1 - upper, other, 2 * (1 - odd) + 1 - upper


def sums_kernel(share, parts_ref, gz_ref, total_ref, bias_ref, keep_ref, *refs):
    send_refs, (rows_ref,) = refs[:3], refs[3:]
    count, channels, _ = gz_ref.shape
    high = 3 * channels
    total, bias = 0.0, 0.0
    for i in range(count):
        gated = gz_ref[i]
        around = [
            line_of(parts_ref, count, channels, 0, (i + a - 1) % count) for a in range(3)
        ]
        term, bias_term = weight_product(gated, back_taps(gated, share), around)
        total, bias = total + term, bias + bias_term
    for layer, sums in enumerate((total, total_ref[...])):
        rows_ref[layer * high : (layer + 1) * high, :] = sums[:, : 2 * channels]
        rows_ref[2 * high : 3 * high, layer * channels : (layer + 1) * channels] = sums[
            :, 2 * channels :
        ]
    bias = jnp.concatenate([bias[:1], bias_ref[:1]], axis=1)
    row = lax.broadcasted_iota(jnp.int32, (TAIL, 2 * channels), 0)
    rows_ref[3 * high :, :] = jnp.where(row == 0, bias, 0.0)
    size = keep_ref.shape[0]
    for at, quarter in enumerate(quarters()):
        rows = rows_ref[pl.ds(pl.multiple_of(quarter * size, 16), size), :]
        if at == 0:
            keep_ref[...] = rows
        else:
            send_refs[at - 1][...] = rows.astype(BF16)


def assemble_kernel(scale, *refs):
    quarter_refs, (out_ref, bias_ref, total_ref) = refs[:4], refs[4:]
    channels = out_ref.shape[-1]
    size = quarter_refs[0].shape[0]
    for quarter, ref in zip(quarters(), quarter_refs):
        rows = ref[...].astype(F32) * scale
        total_ref[pl.ds(pl.multiple_of(quarter * size, 16), size), :] = rows
    high = 3 * channels
    for layer in range(2):
        for b in range(3):
            first = layer * high + b * channels
            pair = total_ref[first : first + channels, :]
            out_ref[layer, 0, b] = pair[:, :channels]
            out_ref[layer, 1, b] = pair[:, channels:]
            first = 2 * high + b * channels
            third = total_ref[first : first + channels, :]
            out_ref[layer, 2, b] = third[:, layer * channels : (layer + 1) * channels]
    bias = total_ref[3 * high : 3 * high + 1, :]
    bias_ref[0:1, :] = bias[:, :channels]
    bias_ref[1:2, :] = bias[:, channels:]


def partnered(block, devices, bit):
    return lax.ppermute(block, AXES, [(i, i ^ bit) for i in range(devices)])


def added(keep, sends, devices):
    came = [partnered(send, devices, bit).astype(F32) for send, bit in zip(sends, QUARTERS)]
    mine = (keep + came[0]) + (came[1] + came[2])
    low = 4
    while low < devices:
        high = 2 * low if 2 * low < devices else 0
        rounded = mine.astype(BF16)
        mine = rounded.astype(F32)
        if high:
            far = partnered(rounded, devices, high)
            across = partnered(rounded, devices, low + high)
            mine = mine + partnered(rounded, devices, low).astype(F32)
            mine = mine + (far.astype(F32) + across.astype(F32))
        else:
            mine = mine + partnered(rounded, devices, low).astype(F32)
        low *= 4
    return mine.astype(BF16)


def exchanged(parts):
    return lax.all_to_all(parts, AXES, 0, 0, tiled=True)


def local(inputs, weights, biases, cotangent):
    channels, cols, lat_rows = inputs.shape
    lons, lats = lax.axis_size("lon"), lax.axis_size("lat")
    devices = lons * lats
    share = cols * cols // devices
    width = lat_rows // cols * share
    span = lats * width
    scale = 1.0 / math.sqrt(cols * lons * lat_rows * lats)
    blocks = lats if width % LANES == 0 else 1
    shape = jax.ShapeDtypeStruct

    chunks = 2 * channels // min(channels, 256 // cols)
    fields_shape = (devices, 2 * channels, width)
    hbm = pl.BlockSpec(memory_space=pltpu.HBM)
    vmem = pl.BlockSpec(memory_space=pltpu.VMEM)

    packed = pl.pallas_call(
        functools.partial(pack_kernel, share),
        out_shape=shape(fields_shape, BF16),
        in_specs=[hbm, hbm],
        out_specs=hbm,
        scratch_shapes=[
            pltpu.VMEM((2,) + inputs.shape, BF16),
            pltpu.VMEM(fields_shape, BF16),
            pltpu.SemaphoreType.DMA((2,)),
            pltpu.SemaphoreType.DMA((2,)),
        ],
        compiler_params=WIDE,
    )(inputs, cotangent)
    packed, weights = lax.optimization_barrier((packed, weights))
    kernels = pl.pallas_call(
        kernels_kernel,
        out_shape=shape((4, 3 * channels, 3 * channels), BF16),
        compiler_params=PARAMS,
    )(weights)
    parts = exchanged(packed)
    if blocks == 1:
        parts = parts.reshape(lons, lats, 2 * channels, width).transpose(0, 2, 1, 3)
        parts = parts.reshape(lons, 2 * channels, span)

    cells = (lons, channels, span)
    high = 3 * channels
    fields, gated, total, bias_sums = pl.pallas_call(
        functools.partial(stack_kernel, share),
        out_shape=[
            shape(parts.shape, BF16),
            shape(cells, BF16),
            shape((high, high), F32),
            shape((16, channels), F32),
        ],
        out_specs=[hbm, vmem, vmem, vmem],
        scratch_shapes=[
            pltpu.VMEM(cells, BF16),
            pltpu.VMEM(cells, F32),
            pltpu.VMEM(cells, F32),
            pltpu.VMEM((lons, 3 * channels, span), F32),
            pltpu.VMEM(parts.shape, BF16),
            pltpu.SemaphoreType.DMA((lons + 1,)),
        ],
        compiler_params=PARAMS,
    )(parts, kernels, biases[:, :, None])
    if blocks == 1:
        fields = fields.reshape(lons, 2 * channels, lats, width).transpose(0, 2, 1, 3)
        fields = fields.reshape(fields_shape)
    home = exchanged(fields)

    rows = 9 * channels + TAIL
    quarter_shape = (rows // 4, 2 * channels)
    flops = 9 * channels * parts.size
    keep, *sends = pl.pallas_call(
        functools.partial(sums_kernel, share),
        out_shape=[shape(quarter_shape, F32)] + [shape(quarter_shape, BF16)] * 3,
        scratch_shapes=[pltpu.VMEM((rows, 2 * channels), F32)],
        compiler_params=PARAMS,
        cost_estimate=pl.CostEstimate(flops=flops, bytes_accessed=3 * parts.size, transcendentals=0),
    )(parts, gated, total, bias_sums)
    mine = added(keep, sends, devices)
    home, mine = lax.optimization_barrier((home, mine))
    others = [partnered(mine, devices, bit) for bit in QUARTERS]
    features_out, grad_input = pl.pallas_call(
        functools.partial(unpack_kernel, share),
        out_shape=[shape(inputs.shape, BF16), shape(inputs.shape, BF16)],
        out_specs=[hbm, hbm],
        scratch_shapes=[
            pltpu.VMEM((2,) + inputs.shape, BF16),
            pltpu.SemaphoreType.DMA((chunks,)),
        ],
        compiler_params=PARAMS,
        cost_estimate=pl.CostEstimate(
            flops=4 * inputs.size * lat_rows, bytes_accessed=8 * inputs.size, transcendentals=0
        ),
    )(home)
    weight_grads, bias_grads = pl.pallas_call(
        functools.partial(assemble_kernel, scale),
        out_shape=[shape(weights.shape, F32), shape(biases.shape, F32)],
        scratch_shapes=[pltpu.VMEM((rows, 2 * channels), F32)],
        compiler_params=PARAMS,
    )(mine, *others)
    return features_out, grad_input, weight_grads, bias_grads


def solution(mesh):
    in_specs = (P(None, "lon", "lat"), P(), P(), P(None, "lon", "lat"))
    out_specs = (P(None, "lon", "lat"), P(None, "lon", "lat"), P(), P())
    return jax.shard_map(local, mesh=mesh, in_specs=in_specs, out_specs=out_specs, check_vma=False)
```

```python
import functools
import math

import jax
import jax.numpy as jnp
from jax import lax
from jax.experimental import pallas as pl
from jax.experimental.pallas import tpu as pltpu
from jax.sharding import PartitionSpec as P


AXES = ("lon", "lat")
LANES = 128
TAIL = 32
BF16, F32 = jnp.bfloat16, jnp.float32
PARAMS = pltpu.CompilerParams(vmem_limit_bytes=24 * 2**20)
WIDE = pltpu.CompilerParams(vmem_limit_bytes=56 * 2**20)


def lane_order(cols, lat_rows, share, inverse):
    steps = lat_rows // cols
    place = lax.broadcasted_iota(jnp.int32, (lat_rows, lat_rows), 0 if inverse else 1)
    source = lax.broadcasted_iota(jnp.int32, (lat_rows, lat_rows), 1 if inverse else 0)
    group = lax.div(source & (cols - 1), share)
    wanted = (group * steps + lax.div(source, cols)) * share + (source & (share - 1))
    return (place == wanted).astype(F32).astype(BF16)


def row_order(outer, inner):
    rows = outer * inner
    place = lax.broadcasted_iota(jnp.int32, (rows, rows), 0)
    source = lax.broadcasted_iota(jnp.int32, (rows, rows), 1)
    wanted = (source & (inner - 1)) * outer + lax.div(source, inner)
    return (place == wanted).astype(F32).astype(BF16)


def product(left, right):
    return jnp.dot(left, right, preferred_element_type=F32)


def pack_kernel(share, x_ref, cot_ref, out_ref, buf, packed, in_sems, out_sems):
    _, channels, cols, lat_rows = buf.shape
    devices, _, width = packed.shape
    groups = devices // cols
    part = min(channels, 256 // cols)
    arrivals, departures = [], []
    for at, ref in enumerate((x_ref, cot_ref)):
        arrivals.append(pltpu.make_async_copy(ref, buf.at[at], in_sems.at[at]))
        rows = (slice(None), pl.ds(at * channels, channels), slice(None))
        departures.append(
            pltpu.make_async_copy(packed.at[rows], out_ref.at[rows], out_sems.at[at])
        )
        arrivals[at].start()
    lanes = lane_order(cols, lat_rows, share, False)
    order = row_order(part, cols)
    for at in range(2):
        arrivals[at].wait()
        for first in range(0, channels, part):
            rows = buf[at, first : first + part].reshape(part * cols, lat_rows)
            rows = product(order, rows).astype(BF16)
            rows = product(rows, lanes).astype(BF16)
            start = at * channels + first
            for col in range(cols):
                for group in range(groups):
                    packed[col * groups + group, start : start + part, :] = rows[
                        col * part : (col + 1) * part, group * width : (group + 1) * width
                    ]
        departures[at].start()
    for departure in departures:
        departure.wait()


def unpack_kernel(share, parts_ref, feat_ref, grad_ref, buf, sems):
    _, channels, cols, lat_rows = buf.shape
    devices, _, width = parts_ref.shape
    groups = devices // cols
    part = min(channels, 256 // cols)
    lanes = lane_order(cols, lat_rows, share, True)
    order = row_order(cols, part)
    departures = []
    for at, out_ref in enumerate((feat_ref, grad_ref)):
        for first in range(0, channels, part):
            start = at * channels + first
            rows = [
                jnp.concatenate(
                    [
                        parts_ref[col * groups + group, start : start + part, :]
                        for group in range(groups)
                    ],
                    axis=1,
                )
                for col in range(cols)
            ]
            rows = product(jnp.concatenate(rows, axis=0), lanes).astype(BF16)
            rows = product(order, rows).astype(BF16)
            buf[at, first : first + part] = rows.reshape(part, cols, lat_rows)
            rows = pl.ds(first, part)
            departures.append(
                pltpu.make_async_copy(buf.at[at, rows], out_ref.at[rows], sems.at[len(departures)])
            )
            departures[-1].start()
    for departure in departures:
        departure.wait()


def taps(row, shift):
    edge = jnp.zeros((row.shape[0], shift), row.dtype)
    before = jnp.concatenate([edge, row[:, :-shift]], axis=1)
    after = jnp.concatenate([row[:, shift:], edge], axis=1)
    return before, row, after


def kernels_kernel(w_ref, out_ref):
    for layer in range(2):
        for back in range(2):
            rows = []
            for a in range(3):
                row = [w_ref[layer, a, b] for b in range(3)]
                if back:
                    row = [tap.astype(F32).T.astype(BF16) for tap in row]
                rows.append(jnp.concatenate(row, axis=1))
            out_ref[2 * layer + back] = jnp.concatenate(rows, axis=0)


def line_of(parts_ref, count, channels, field, i):
    blocks = parts_ref.shape[0] // count
    rows = slice(field * channels, (field + 1) * channels)
    return jnp.concatenate([parts_ref[i * blocks + k, rows, :] for k in range(blocks)], axis=1)


def weight_product(gated, stack, lines):
    ones = jnp.ones((16, gated.shape[1]), BF16)
    across = (((1,), (1,)), ((), ()))
    bias = lax.dot_general(ones, gated, across, preferred_element_type=F32)
    lines = jnp.concatenate(lines, axis=0)
    return lax.dot_general(stack, lines, across, preferred_element_type=F32), bias


def back_taps(gated, shift):
    before, here, after = taps(gated, shift)
    return jnp.concatenate([after, here, before], axis=0)


def stack_kernel(
    share,
    parts_ref,
    w_ref,
    b_ref,
    out_ref,
    gz_ref,
    total_ref,
    bias_ref,
    h_ref,
    s0_ref,
    s1_ref,
    y_ref,
    fields_ref,
    sems,
):
    count, channels, _ = h_ref.shape
    devices, _, width = parts_ref.shape
    blocks = devices // count
    copies = []

    def put(field, i, line):
        rows = slice(field * channels, (field + 1) * channels)
        for k in range(blocks):
            fields_ref[i * blocks + k, rows, :] = line[:, k * width : (k + 1) * width]

    def send(field, i, lines):
        place = (pl.ds(i * blocks, lines * blocks), pl.ds(field * channels, channels))
        copies.append(
            pltpu.make_async_copy(fields_ref.at[place], out_ref.at[place], sems.at[len(copies)])
        )
        copies[-1].start()

    for layer in range(2):
        hops = 2**layer
        kernel = w_ref[2 * layer]
        for i in range(count):
            line = line_of(parts_ref, count, channels, 0, i) if layer == 0 else h_ref[i]
            stack = jnp.concatenate(taps(line, hops * share), axis=0)
            y_ref[i] = product(kernel, stack)
        bias = b_ref[layer]
        for i in range(count):
            pre = bias + y_ref[i, channels : 2 * channels]
            pre = pre + y_ref[(i - hops) % count, :channels]
            pre = pre + y_ref[(i + hops) % count, 2 * channels :]
            sigma = 0.5 * jnp.tanh(0.5 * pre) + 0.5
            state = pre * sigma
            slope = sigma + state * (1.0 - sigma)
            if layer == 0:
                h_ref[i] = state.astype(BF16)
                s0_ref[i] = slope
            else:
                s1_ref[i] = slope
                put(0, i, state.astype(BF16))
    send(0, 0, count)

    total, bias = 0.0, 0.0
    for layer in (1, 0):
        hops = 2**layer
        kernel = w_ref[2 * layer + 1]
        for i in range(count):
            if layer == 1:
                gated = line_of(parts_ref, count, channels, 1, i).astype(F32) * s1_ref[i]
                gated = gated.astype(BF16)
            else:
                gated = gz_ref[i]
            stack = back_taps(gated, hops * share)
            y_ref[i] = product(kernel, stack)
            if layer == 1:
                around = [h_ref[(i + (a - 1) * hops) % count] for a in range(3)]
                term, bias_term = weight_product(gated, stack, around)
                total, bias = total + term, bias + bias_term
        for i in range(count):
            g = y_ref[i, channels : 2 * channels]
            g = g + y_ref[(i + hops) % count, :channels]
            g = g + y_ref[(i - hops) % count, 2 * channels :]
            g = g.astype(BF16)
            if layer == 1:
                gz_ref[i] = (g.astype(F32) * s0_ref[i]).astype(BF16)
            else:
                put(1, i, g)
                send(1, i, 1)
        if layer == 1:
            total_ref[...] = total
            bias_ref[...] = bias
    for started in copies:
        started.wait()


def sums_kernel(share, parts_ref, gz_ref, total_ref, bias_ref, keep_ref, send_ref, rows_ref):
    count, channels, _ = gz_ref.shape
    high = 3 * channels
    total, bias = 0.0, 0.0
    for i in range(count):
        gated = gz_ref[i]
        around = [
            line_of(parts_ref, count, channels, 0, (i + a - 1) % count) for a in range(3)
        ]
        term, bias_term = weight_product(gated, back_taps(gated, share), around)
        total, bias = total + term, bias + bias_term
    for layer, sums in enumerate((total, total_ref[...])):
        rows_ref[layer * high : (layer + 1) * high, :] = sums[:, : 2 * channels]
        rows_ref[2 * high : 3 * high, layer * channels : (layer + 1) * channels] = sums[
            :, 2 * channels :
        ]
    bias = jnp.concatenate([bias[:1], bias_ref[:1]], axis=1)
    row = lax.broadcasted_iota(jnp.int32, (TAIL, 2 * channels), 0)
    rows_ref[3 * high :, :] = jnp.where(row == 0, bias, 0.0)
    half = keep_ref.shape[0]
    odd = lax.axis_index("lat") & 1
    keep_ref[...] = rows_ref[pl.ds(pl.multiple_of(odd * half, 16), half), :]
    send_ref[...] = rows_ref[pl.ds(pl.multiple_of((1 - odd) * half, 16), half), :].astype(BF16)


def assemble_kernel(scale, mine_ref, other_ref, out_ref, bias_ref, total_ref):
    channels = out_ref.shape[-1]
    half = mine_ref.shape[0]
    odd = lax.axis_index("lat") & 1
    for side, ref in ((odd, mine_ref), (1 - odd, other_ref)):
        total_ref[pl.ds(pl.multiple_of(side * half, 16), half), :] = ref[...].astype(F32) * scale
    high = 3 * channels
    for layer in range(2):
        for b in range(3):
            first = layer * high + b * channels
            pair = total_ref[first : first + channels, :]
            out_ref[layer, 0, b] = pair[:, :channels]
            out_ref[layer, 1, b] = pair[:, channels:]
            first = 2 * high + b * channels
            third = total_ref[first : first + channels, :]
            out_ref[layer, 2, b] = third[:, layer * channels : (layer + 1) * channels]
    bias = total_ref[3 * high : 3 * high + 1, :]
    bias_ref[0:1, :] = bias[:, :channels]
    bias_ref[1:2, :] = bias[:, channels:]


def partnered(block, devices, bit):
    return lax.ppermute(block, AXES, [(i, i ^ bit) for i in range(devices)])


def added(keep, send, devices):
    total = keep + partnered(send, devices, 1).astype(F32)
    bits = [4 << k for k in range((devices // 4).bit_length() - 1)] + [2]
    for bit in bits:
        rounded = total.astype(BF16)
        total = rounded.astype(F32) + partnered(rounded, devices, bit).astype(F32)
    return total.astype(BF16)


def exchanged(parts):
    return lax.all_to_all(parts, AXES, 0, 0, tiled=True)


def local(inputs, weights, biases, cotangent):
    channels, cols, lat_rows = inputs.shape
    lons, lats = lax.axis_size("lon"), lax.axis_size("lat")
    devices = lons * lats
    share = cols * cols // devices
    width = lat_rows // cols * share
    span = lats * width
    scale = 1.0 / math.sqrt(cols * lons * lat_rows * lats)
    blocks = lats if width % LANES == 0 else 1
    shape = jax.ShapeDtypeStruct

    chunks = 2 * channels // min(channels, 256 // cols)
    fields_shape = (devices, 2 * channels, width)
    hbm = pl.BlockSpec(memory_space=pltpu.HBM)
    vmem = pl.BlockSpec(memory_space=pltpu.VMEM)

    packed = pl.pallas_call(
        functools.partial(pack_kernel, share),
        out_shape=shape(fields_shape, BF16),
        in_specs=[hbm, hbm],
        out_specs=hbm,
        scratch_shapes=[
            pltpu.VMEM((2,) + inputs.shape, BF16),
            pltpu.VMEM(fields_shape, BF16),
            pltpu.SemaphoreType.DMA((2,)),
            pltpu.SemaphoreType.DMA((2,)),
        ],
        compiler_params=WIDE,
    )(inputs, cotangent)
    packed, weights = lax.optimization_barrier((packed, weights))
    kernels = pl.pallas_call(
        kernels_kernel,
        out_shape=shape((4, 3 * channels, 3 * channels), BF16),
        compiler_params=PARAMS,
    )(weights)
    parts = exchanged(packed)
    if blocks == 1:
        parts = parts.reshape(lons, lats, 2 * channels, width).transpose(0, 2, 1, 3)
        parts = parts.reshape(lons, 2 * channels, span)

    cells = (lons, channels, span)
    high = 3 * channels
    fields, gated, total, bias_sums = pl.pallas_call(
        functools.partial(stack_kernel, share),
        out_shape=[
            shape(parts.shape, BF16),
            shape(cells, BF16),
            shape((high, high), F32),
            shape((16, channels), F32),
        ],
        out_specs=[hbm, vmem, vmem, vmem],
        scratch_shapes=[
            pltpu.VMEM(cells, BF16),
            pltpu.VMEM(cells, F32),
            pltpu.VMEM(cells, F32),
            pltpu.VMEM((lons, 3 * channels, span), F32),
            pltpu.VMEM(parts.shape, BF16),
            pltpu.SemaphoreType.DMA((lons + 1,)),
        ],
        compiler_params=PARAMS,
    )(parts, kernels, biases[:, :, None])
    if blocks == 1:
        fields = fields.reshape(lons, 2 * channels, lats, width).transpose(0, 2, 1, 3)
        fields = fields.reshape(fields_shape)
    home = exchanged(fields)

    rows = 9 * channels + TAIL
    half_shape = (rows // 2, 2 * channels)
    flops = 9 * channels * parts.size
    keep, send = pl.pallas_call(
        functools.partial(sums_kernel, share),
        out_shape=[shape(half_shape, F32), shape(half_shape, BF16)],
        scratch_shapes=[pltpu.VMEM((rows, 2 * channels), F32)],
        compiler_params=PARAMS,
        cost_estimate=pl.CostEstimate(flops=flops, bytes_accessed=3 * parts.size, transcendentals=0),
    )(parts, gated, total, bias_sums)
    mine = added(keep, send, devices)
    home, mine = lax.optimization_barrier((home, mine))
    other = partnered(mine, devices, 1)
    features_out, grad_input = pl.pallas_call(
        functools.partial(unpack_kernel, share),
        out_shape=[shape(inputs.shape, BF16), shape(inputs.shape, BF16)],
        out_specs=[hbm, hbm],
        scratch_shapes=[
            pltpu.VMEM((2,) + inputs.shape, BF16),
            pltpu.SemaphoreType.DMA((chunks,)),
        ],
        compiler_params=PARAMS,
        cost_estimate=pl.CostEstimate(
            flops=4 * inputs.size * lat_rows, bytes_accessed=8 * inputs.size, transcendentals=0
        ),
    )(home)
    weight_grads, bias_grads = pl.pallas_call(
        functools.partial(assemble_kernel, scale),
        out_shape=[shape(weights.shape, F32), shape(biases.shape, F32)],
        scratch_shapes=[pltpu.VMEM((rows, 2 * channels), F32)],
        compiler_params=PARAMS,
    )(mine, other)
    return features_out, grad_input, weight_grads, bias_grads


def solution(mesh):
    in_specs = (P(None, "lon", "lat"), P(), P(), P(None, "lon", "lat"))
    out_specs = (P(None, "lon", "lat"), P(None, "lon", "lat"), P(), P())
    return jax.shard_map(local, mesh=mesh, in_specs=in_specs, out_specs=out_specs, check_vma=False)
```

```python
import functools
import math

import jax
import jax.numpy as jnp
from jax import lax
from jax.experimental import pallas as pl
from jax.experimental.pallas import tpu as pltpu
from jax.sharding import PartitionSpec as P


AXES = ("lon", "lat")
LANES = 128
TAIL = 64
BF16, F32 = jnp.bfloat16, jnp.float32
PARAMS = pltpu.CompilerParams(vmem_limit_bytes=24 * 2**20)
WIDE = pltpu.CompilerParams(vmem_limit_bytes=56 * 2**20)


def lane_order(cols, lat_rows, share, inverse):
    steps = lat_rows // cols
    place = lax.broadcasted_iota(jnp.int32, (lat_rows, lat_rows), 0 if inverse else 1)
    source = lax.broadcasted_iota(jnp.int32, (lat_rows, lat_rows), 1 if inverse else 0)
    group = lax.div(source & (cols - 1), share)
    wanted = (group * steps + lax.div(source, cols)) * share + (source & (share - 1))
    return (place == wanted).astype(F32).astype(BF16)


def row_order(outer, inner):
    rows = outer * inner
    place = lax.broadcasted_iota(jnp.int32, (rows, rows), 0)
    source = lax.broadcasted_iota(jnp.int32, (rows, rows), 1)
    wanted = (source & (inner - 1)) * outer + lax.div(source, inner)
    return (place == wanted).astype(F32).astype(BF16)


def product(left, right):
    return jnp.dot(left, right, preferred_element_type=F32)


def pack_kernel(share, x_ref, cot_ref, out_ref, buf, packed, in_sems, out_sems):
    _, channels, cols, lat_rows = buf.shape
    devices, _, width = packed.shape
    groups = devices // cols
    part = min(channels, 256 // cols)
    arrivals, departures = [], []
    for at, ref in enumerate((x_ref, cot_ref)):
        arrivals.append(pltpu.make_async_copy(ref, buf.at[at], in_sems.at[at]))
        rows = (slice(None), pl.ds(at * channels, channels), slice(None))
        departures.append(
            pltpu.make_async_copy(packed.at[rows], out_ref.at[rows], out_sems.at[at])
        )
        arrivals[at].start()
    lanes = lane_order(cols, lat_rows, share, False)
    order = row_order(part, cols)
    for at in range(2):
        arrivals[at].wait()
        for first in range(0, channels, part):
            rows = buf[at, first : first + part].reshape(part * cols, lat_rows)
            rows = product(order, rows).astype(BF16)
            rows = product(rows, lanes).astype(BF16)
            start = at * channels + first
            for col in range(cols):
                for group in range(groups):
                    packed[col * groups + group, start : start + part, :] = rows[
                        col * part : (col + 1) * part, group * width : (group + 1) * width
                    ]
        departures[at].start()
    for departure in departures:
        departure.wait()


def unpack_kernel(share, parts_ref, feat_ref, grad_ref, buf, sems):
    _, channels, cols, lat_rows = buf.shape
    devices, _, width = parts_ref.shape
    groups = devices // cols
    part = min(channels, 256 // cols)
    lanes = lane_order(cols, lat_rows, share, True)
    order = row_order(cols, part)
    departures = []
    for at, out_ref in enumerate((feat_ref, grad_ref)):
        for first in range(0, channels, part):
            start = at * channels + first
            rows = [
                jnp.concatenate(
                    [
                        parts_ref[col * groups + group, start : start + part, :]
                        for group in range(groups)
                    ],
                    axis=1,
                )
                for col in range(cols)
            ]
            rows = product(jnp.concatenate(rows, axis=0), lanes).astype(BF16)
            rows = product(order, rows).astype(BF16)
            buf[at, first : first + part] = rows.reshape(part, cols, lat_rows)
            rows = pl.ds(first, part)
            departures.append(
                pltpu.make_async_copy(buf.at[at, rows], out_ref.at[rows], sems.at[len(departures)])
            )
            departures[-1].start()
    for departure in departures:
        departure.wait()


def taps(row, shift):
    edge = jnp.zeros((row.shape[0], shift), row.dtype)
    before = jnp.concatenate([edge, row[:, :-shift]], axis=1)
    after = jnp.concatenate([row[:, shift:], edge], axis=1)
    return before, row, after


def kernels_kernel(w_ref, out_ref):
    for layer in range(2):
        for back in range(2):
            rows = []
            for a in range(3):
                row = [w_ref[layer, a, b] for b in range(3)]
                if back:
                    row = [tap.astype(F32).T.astype(BF16) for tap in row]
                rows.append(jnp.concatenate(row, axis=1))
            out_ref[2 * layer + back] = jnp.concatenate(rows, axis=0)


def line_of(parts_ref, count, channels, field, i):
    blocks = parts_ref.shape[0] // count
    rows = slice(field * channels, (field + 1) * channels)
    return jnp.concatenate([parts_ref[i * blocks + k, rows, :] for k in range(blocks)], axis=1)


def weight_product(gated, stack, lines):
    ones = jnp.ones((16, gated.shape[1]), BF16)
    across = (((1,), (1,)), ((), ()))
    bias = lax.dot_general(ones, gated, across, preferred_element_type=F32)
    lines = jnp.concatenate(lines, axis=0)
    return lax.dot_general(stack, lines, across, preferred_element_type=F32), bias


def back_taps(gated, shift):
    before, here, after = taps(gated, shift)
    return jnp.concatenate([after, here, before], axis=0)


def stack_kernel(
    share,
    parts_ref,
    w_ref,
    b_ref,
    out_ref,
    gz_ref,
    total_ref,
    bias_ref,
    h_ref,
    s0_ref,
    s1_ref,
    y_ref,
    fields_ref,
    sems,
):
    count, channels, _ = h_ref.shape
    devices, _, width = parts_ref.shape
    blocks = devices // count
    copies = []

    def put(field, i, line):
        rows = slice(field * channels, (field + 1) * channels)
        for k in range(blocks):
            fields_ref[i * blocks + k, rows, :] = line[:, k * width : (k + 1) * width]

    def send(field, i, lines):
        place = (pl.ds(i * blocks, lines * blocks), pl.ds(field * channels, channels))
        copies.append(
            pltpu.make_async_copy(fields_ref.at[place], out_ref.at[place], sems.at[len(copies)])
        )
        copies[-1].start()

    for layer in range(2):
        hops = 2**layer
        kernel = w_ref[2 * layer]
        for i in range(count):
            line = line_of(parts_ref, count, channels, 0, i) if layer == 0 else h_ref[i]
            stack = jnp.concatenate(taps(line, hops * share), axis=0)
            y_ref[i] = product(kernel, stack)
        bias = b_ref[layer]
        for i in range(count):
            pre = bias + y_ref[i, channels : 2 * channels]
            pre = pre + y_ref[(i - hops) % count, :channels]
            pre = pre + y_ref[(i + hops) % count, 2 * channels :]
            sigma = 0.5 * jnp.tanh(0.5 * pre) + 0.5
            state = pre * sigma
            slope = sigma + state * (1.0 - sigma)
            if layer == 0:
                h_ref[i] = state.astype(BF16)
                s0_ref[i] = slope
            else:
                s1_ref[i] = slope
                put(0, i, state.astype(BF16))
    send(0, 0, count)

    total, bias = 0.0, 0.0
    for layer in (1, 0):
        hops = 2**layer
        kernel = w_ref[2 * layer + 1]
        for i in range(count):
            if layer == 1:
                gated = line_of(parts_ref, count, channels, 1, i).astype(F32) * s1_ref[i]
                gated = gated.astype(BF16)
            else:
                gated = gz_ref[i]
            stack = back_taps(gated, hops * share)
            y_ref[i] = product(kernel, stack)
            if layer == 1:
                around = [h_ref[(i + (a - 1) * hops) % count] for a in range(3)]
                term, bias_term = weight_product(gated, stack, around)
                total, bias = total + term, bias + bias_term
        for i in range(count):
            g = y_ref[i, channels : 2 * channels]
            g = g + y_ref[(i + hops) % count, :channels]
            g = g + y_ref[(i - hops) % count, 2 * channels :]
            g = g.astype(BF16)
            if layer == 1:
                gz_ref[i] = (g.astype(F32) * s0_ref[i]).astype(BF16)
            else:
                put(1, i, g)
                send(1, i, 1)
        if layer == 1:
            total_ref[...] = total
            bias_ref[...] = bias
    for started in copies:
        started.wait()


def quarters():
    lat = lax.axis_index("lat")
    odd, upper = lat & 1, lax.div(lat, 2) & 1
    return 2 * odd + upper, 2 * odd + 1 - upper, 2 * (1 - odd) + upper, 3 - 2 * odd - upper


def sums_kernel(share, parts_ref, gz_ref, total_ref, bias_ref, keep_ref, send_ref, rows_ref):
    count, channels, _ = gz_ref.shape
    high = 3 * channels
    total, bias = 0.0, 0.0
    for i in range(count):
        gated = gz_ref[i]
        around = [
            line_of(parts_ref, count, channels, 0, (i + a - 1) % count) for a in range(3)
        ]
        term, bias_term = weight_product(gated, back_taps(gated, share), around)
        total, bias = total + term, bias + bias_term
    for layer, sums in enumerate((total, total_ref[...])):
        rows_ref[layer * high : (layer + 1) * high, :] = sums[:, : 2 * channels]
        rows_ref[2 * high : 3 * high, layer * channels : (layer + 1) * channels] = sums[
            :, 2 * channels :
        ]
    bias = jnp.concatenate([bias[:1], bias_ref[:1]], axis=1)
    row = lax.broadcasted_iota(jnp.int32, (TAIL, 2 * channels), 0)
    rows_ref[3 * high :, :] = jnp.where(row == 0, bias, 0.0)
    size = keep_ref.shape[0] // 2
    for at, quarter in enumerate(quarters()):
        rows = rows_ref[pl.ds(pl.multiple_of(quarter * size, 16), size), :]
        place = slice((at % 2) * size, (at % 2 + 1) * size)
        if at < 2:
            keep_ref[place, :] = rows
        else:
            send_ref[place, :] = rows.astype(BF16)


def assemble_kernel(scale, pair_ref, other_ref, out_ref, bias_ref, total_ref):
    channels = out_ref.shape[-1]
    size = pair_ref.shape[0] // 2
    for at, quarter in enumerate(quarters()):
        ref = pair_ref if at < 2 else other_ref
        rows = ref[(at % 2) * size : (at % 2 + 1) * size, :].astype(F32) * scale
        total_ref[pl.ds(pl.multiple_of(quarter * size, 16), size), :] = rows
    high = 3 * channels
    for layer in range(2):
        for b in range(3):
            first = layer * high + b * channels
            pair = total_ref[first : first + channels, :]
            out_ref[layer, 0, b] = pair[:, :channels]
            out_ref[layer, 1, b] = pair[:, channels:]
            first = 2 * high + b * channels
            third = total_ref[first : first + channels, :]
            out_ref[layer, 2, b] = third[:, layer * channels : (layer + 1) * channels]
    bias = total_ref[3 * high : 3 * high + 1, :]
    bias_ref[0:1, :] = bias[:, :channels]
    bias_ref[1:2, :] = bias[:, channels:]


def partnered(block, devices, bit):
    return lax.ppermute(block, AXES, [(i, i ^ bit) for i in range(devices)])


def added(keep, send, devices):
    size = keep.shape[0] // 2
    keep = keep + partnered(send, devices, 1).astype(F32)
    total = keep[:size] + partnered(keep[size:].astype(BF16), devices, 2).astype(F32)
    bit = 4
    while bit < devices:
        rounded = total.astype(BF16)
        total = rounded.astype(F32) + partnered(rounded, devices, bit).astype(F32)
        bit *= 2
    return total.astype(BF16)


def exchanged(parts):
    return lax.all_to_all(parts, AXES, 0, 0, tiled=True)


def local(inputs, weights, biases, cotangent):
    channels, cols, lat_rows = inputs.shape
    lons, lats = lax.axis_size("lon"), lax.axis_size("lat")
    devices = lons * lats
    share = cols * cols // devices
    width = lat_rows // cols * share
    span = lats * width
    scale = 1.0 / math.sqrt(cols * lons * lat_rows * lats)
    blocks = lats if width % LANES == 0 else 1
    shape = jax.ShapeDtypeStruct

    chunks = 2 * channels // min(channels, 256 // cols)
    fields_shape = (devices, 2 * channels, width)
    hbm = pl.BlockSpec(memory_space=pltpu.HBM)
    vmem = pl.BlockSpec(memory_space=pltpu.VMEM)

    packed = pl.pallas_call(
        functools.partial(pack_kernel, share),
        out_shape=shape(fields_shape, BF16),
        in_specs=[hbm, hbm],
        out_specs=hbm,
        scratch_shapes=[
            pltpu.VMEM((2,) + inputs.shape, BF16),
            pltpu.VMEM(fields_shape, BF16),
            pltpu.SemaphoreType.DMA((2,)),
            pltpu.SemaphoreType.DMA((2,)),
        ],
        compiler_params=WIDE,
    )(inputs, cotangent)
    packed, weights = lax.optimization_barrier((packed, weights))
    kernels = pl.pallas_call(
        kernels_kernel,
        out_shape=shape((4, 3 * channels, 3 * channels), BF16),
        compiler_params=PARAMS,
    )(weights)
    parts = exchanged(packed)
    if blocks == 1:
        parts = parts.reshape(lons, lats, 2 * channels, width).transpose(0, 2, 1, 3)
        parts = parts.reshape(lons, 2 * channels, span)

    cells = (lons, channels, span)
    high = 3 * channels
    fields, gated, total, bias_sums = pl.pallas_call(
        functools.partial(stack_kernel, share),
        out_shape=[
            shape(parts.shape, BF16),
            shape(cells, BF16),
            shape((high, high), F32),
            shape((16, channels), F32),
        ],
        out_specs=[hbm, vmem, vmem, vmem],
        scratch_shapes=[
            pltpu.VMEM(cells, BF16),
            pltpu.VMEM(cells, F32),
            pltpu.VMEM(cells, F32),
            pltpu.VMEM((lons, 3 * channels, span), F32),
            pltpu.VMEM(parts.shape, BF16),
            pltpu.SemaphoreType.DMA((lons + 1,)),
        ],
        compiler_params=PARAMS,
    )(parts, kernels, biases[:, :, None])
    if blocks == 1:
        fields = fields.reshape(lons, 2 * channels, lats, width).transpose(0, 2, 1, 3)
        fields = fields.reshape(fields_shape)
    home = exchanged(fields)

    rows = 9 * channels + TAIL
    half_shape = (rows // 2, 2 * channels)
    flops = 9 * channels * parts.size
    keep, send = pl.pallas_call(
        functools.partial(sums_kernel, share),
        out_shape=[shape(half_shape, F32), shape(half_shape, BF16)],
        scratch_shapes=[pltpu.VMEM((rows, 2 * channels), F32)],
        compiler_params=PARAMS,
        cost_estimate=pl.CostEstimate(flops=flops, bytes_accessed=3 * parts.size, transcendentals=0),
    )(parts, gated, total, bias_sums)
    mine = added(keep, send, devices)
    home, mine = lax.optimization_barrier((home, mine))
    pair = jnp.concatenate([mine, partnered(mine, devices, 2)], axis=0)
    other = partnered(pair, devices, 1)
    features_out, grad_input = pl.pallas_call(
        functools.partial(unpack_kernel, share),
        out_shape=[shape(inputs.shape, BF16), shape(inputs.shape, BF16)],
        out_specs=[hbm, hbm],
        scratch_shapes=[
            pltpu.VMEM((2,) + inputs.shape, BF16),
            pltpu.SemaphoreType.DMA((chunks,)),
        ],
        compiler_params=PARAMS,
        cost_estimate=pl.CostEstimate(
            flops=4 * inputs.size * lat_rows, bytes_accessed=8 * inputs.size, transcendentals=0
        ),
    )(home)
    weight_grads, bias_grads = pl.pallas_call(
        functools.partial(assemble_kernel, scale),
        out_shape=[shape(weights.shape, F32), shape(biases.shape, F32)],
        scratch_shapes=[pltpu.VMEM((rows, 2 * channels), F32)],
        compiler_params=PARAMS,
    )(pair, other)
    return features_out, grad_input, weight_grads, bias_grads


def solution(mesh):
    in_specs = (P(None, "lon", "lat"), P(), P(), P(None, "lon", "lat"))
    out_specs = (P(None, "lon", "lat"), P(None, "lon", "lat"), P(), P())
    return jax.shard_map(local, mesh=mesh, in_specs=in_specs, out_specs=out_specs, check_vma=False)
```

```python
import functools
import math

import jax
import jax.numpy as jnp
from jax import lax
from jax.experimental import pallas as pl
from jax.experimental.pallas import tpu as pltpu
from jax.sharding import PartitionSpec as P


AXES = ("lon", "lat")
LANES = 128
TAIL = 32
BF16, F32 = jnp.bfloat16, jnp.float32
PARAMS = pltpu.CompilerParams(vmem_limit_bytes=24 * 2**20)
WIDE = pltpu.CompilerParams(vmem_limit_bytes=56 * 2**20)


def lane_order(cols, lat_rows, share, inverse):
    steps = lat_rows // cols
    place = lax.broadcasted_iota(jnp.int32, (lat_rows, lat_rows), 0 if inverse else 1)
    source = lax.broadcasted_iota(jnp.int32, (lat_rows, lat_rows), 1 if inverse else 0)
    group = lax.div(source & (cols - 1), share)
    wanted = (group * steps + lax.div(source, cols)) * share + (source & (share - 1))
    return (place == wanted).astype(F32).astype(BF16)


def row_order(outer, inner):
    rows = outer * inner
    place = lax.broadcasted_iota(jnp.int32, (rows, rows), 0)
    source = lax.broadcasted_iota(jnp.int32, (rows, rows), 1)
    wanted = (source & (inner - 1)) * outer + lax.div(source, inner)
    return (place == wanted).astype(F32).astype(BF16)


def product(left, right):
    return jnp.dot(left, right, preferred_element_type=F32)


def pack_kernel(share, x_ref, cot_ref, out_ref, buf, packed, in_sems, out_sems):
    _, channels, cols, lat_rows = buf.shape
    devices, _, width = packed.shape
    groups = devices // cols
    part = min(channels, 256 // cols)
    arrivals, departures = [], []
    for at, ref in enumerate((x_ref, cot_ref)):
        arrivals.append(pltpu.make_async_copy(ref, buf.at[at], in_sems.at[at]))
        rows = (slice(None), pl.ds(at * channels, channels), slice(None))
        departures.append(
            pltpu.make_async_copy(packed.at[rows], out_ref.at[rows], out_sems.at[at])
        )
        arrivals[at].start()
    lanes = lane_order(cols, lat_rows, share, False)
    order = row_order(part, cols)
    for at in range(2):
        arrivals[at].wait()
        for first in range(0, channels, part):
            rows = buf[at, first : first + part].reshape(part * cols, lat_rows)
            rows = product(order, rows).astype(BF16)
            rows = product(rows, lanes).astype(BF16)
            start = at * channels + first
            for col in range(cols):
                for group in range(groups):
                    packed[col * groups + group, start : start + part, :] = rows[
                        col * part : (col + 1) * part, group * width : (group + 1) * width
                    ]
        departures[at].start()
    for departure in departures:
        departure.wait()


def unpack_kernel(share, parts_ref, feat_ref, grad_ref, buf, sems):
    _, channels, cols, lat_rows = buf.shape
    devices, _, width = parts_ref.shape
    groups = devices // cols
    part = min(channels, 256 // cols)
    lanes = lane_order(cols, lat_rows, share, True)
    order = row_order(cols, part)
    departures = []
    for at, out_ref in enumerate((feat_ref, grad_ref)):
        for first in range(0, channels, part):
            start = at * channels + first
            rows = [
                jnp.concatenate(
                    [
                        parts_ref[col * groups + group, start : start + part, :]
                        for group in range(groups)
                    ],
                    axis=1,
                )
                for col in range(cols)
            ]
            rows = product(jnp.concatenate(rows, axis=0), lanes).astype(BF16)
            rows = product(order, rows).astype(BF16)
            buf[at, first : first + part] = rows.reshape(part, cols, lat_rows)
            rows = pl.ds(first, part)
            departures.append(
                pltpu.make_async_copy(buf.at[at, rows], out_ref.at[rows], sems.at[len(departures)])
            )
            departures[-1].start()
    for departure in departures:
        departure.wait()


def taps(row, shift):
    edge = jnp.zeros((row.shape[0], shift), row.dtype)
    before = jnp.concatenate([edge, row[:, :-shift]], axis=1)
    after = jnp.concatenate([row[:, shift:], edge], axis=1)
    return before, row, after


def kernels_kernel(w_ref, out_ref):
    for layer in range(2):
        for back in range(2):
            rows = []
            for a in range(3):
                row = [w_ref[layer, a, b] for b in range(3)]
                if back:
                    row = [tap.astype(F32).T.astype(BF16) for tap in row]
                rows.append(jnp.concatenate(row, axis=1))
            out_ref[2 * layer + back] = jnp.concatenate(rows, axis=0)


def line_of(parts_ref, count, channels, field, i):
    blocks = parts_ref.shape[0] // count
    rows = slice(field * channels, (field + 1) * channels)
    return jnp.concatenate([parts_ref[i * blocks + k, rows, :] for k in range(blocks)], axis=1)


def weight_product(gated, stack, lines):
    ones = jnp.ones((16, gated.shape[1]), BF16)
    across = (((1,), (1,)), ((), ()))
    bias = lax.dot_general(ones, gated, across, preferred_element_type=F32)
    lines = jnp.concatenate(lines, axis=0)
    return lax.dot_general(stack, lines, across, preferred_element_type=F32), bias


def back_taps(gated, shift):
    before, here, after = taps(gated, shift)
    return jnp.concatenate([after, here, before], axis=0)


def stack_kernel(
    share,
    parts_ref,
    w_ref,
    b_ref,
    out_ref,
    gz_ref,
    total_ref,
    bias_ref,
    h_ref,
    s0_ref,
    s1_ref,
    y_ref,
    fields_ref,
    sems,
):
    count, channels, _ = h_ref.shape
    devices, _, width = parts_ref.shape
    blocks = devices // count
    copies = []

    def put(field, i, line):
        rows = slice(field * channels, (field + 1) * channels)
        for k in range(blocks):
            fields_ref[i * blocks + k, rows, :] = line[:, k * width : (k + 1) * width]

    def send(field, i, lines):
        place = (pl.ds(i * blocks, lines * blocks), pl.ds(field * channels, channels))
        copies.append(
            pltpu.make_async_copy(fields_ref.at[place], out_ref.at[place], sems.at[len(copies)])
        )
        copies[-1].start()

    for layer in range(2):
        hops = 2**layer
        kernel = w_ref[2 * layer]
        for i in range(count):
            line = line_of(parts_ref, count, channels, 0, i) if layer == 0 else h_ref[i]
            stack = jnp.concatenate(taps(line, hops * share), axis=0)
            y_ref[i] = product(kernel, stack).astype(BF16)
        bias = b_ref[layer]
        for i in range(count):
            pre = bias + y_ref[i, channels : 2 * channels].astype(F32)
            pre = pre + y_ref[(i - hops) % count, :channels].astype(F32)
            pre = pre + y_ref[(i + hops) % count, 2 * channels :].astype(F32)
            sigma = 0.5 * jnp.tanh(0.5 * pre) + 0.5
            state = pre * sigma
            slope = sigma + state * (1.0 - sigma)
            if layer == 0:
                h_ref[i] = state.astype(BF16)
                s0_ref[i] = slope
            else:
                s1_ref[i] = slope
                put(0, i, state.astype(BF16))
    send(0, 0, count)

    total, bias = 0.0, 0.0
    for layer in (1, 0):
        hops = 2**layer
        kernel = w_ref[2 * layer + 1]
        for i in range(count):
            if layer == 1:
                gated = line_of(parts_ref, count, channels, 1, i).astype(F32) * s1_ref[i]
                gated = gated.astype(BF16)
            else:
                gated = gz_ref[i]
            stack = back_taps(gated, hops * share)
            y_ref[i] = product(kernel, stack).astype(BF16)
            if layer == 1:
                around = [h_ref[(i + (a - 1) * hops) % count] for a in range(3)]
                term, bias_term = weight_product(gated, stack, around)
                total, bias = total + term, bias + bias_term
        for i in range(count):
            g = y_ref[i, channels : 2 * channels].astype(F32)
            g = g + y_ref[(i + hops) % count, :channels].astype(F32)
            g = g + y_ref[(i - hops) % count, 2 * channels :].astype(F32)
            g = g.astype(BF16)
            if layer == 1:
                gz_ref[i] = (g.astype(F32) * s0_ref[i]).astype(BF16)
            else:
                put(1, i, g)
                send(1, i, 1)
        if layer == 1:
            total_ref[...] = total
            bias_ref[...] = bias
    for started in copies:
        started.wait()


def sums_kernel(share, parts_ref, gz_ref, total_ref, bias_ref, keep_ref, send_ref, rows_ref):
    count, channels, _ = gz_ref.shape
    high = 3 * channels
    total, bias = 0.0, 0.0
    for i in range(count):
        gated = gz_ref[i]
        around = [
            line_of(parts_ref, count, channels, 0, (i + a - 1) % count) for a in range(3)
        ]
        term, bias_term = weight_product(gated, back_taps(gated, share), around)
        total, bias = total + term, bias + bias_term
    for layer, sums in enumerate((total, total_ref[...])):
        rows_ref[layer * high : (layer + 1) * high, :] = sums[:, : 2 * channels]
        rows_ref[2 * high : 3 * high, layer * channels : (layer + 1) * channels] = sums[
            :, 2 * channels :
        ]
    bias = jnp.concatenate([bias[:1], bias_ref[:1]], axis=1)
    row = lax.broadcasted_iota(jnp.int32, (TAIL, 2 * channels), 0)
    rows_ref[3 * high :, :] = jnp.where(row == 0, bias, 0.0)
    half = keep_ref.shape[0]
    odd = lax.axis_index("lat") & 1
    keep_ref[...] = rows_ref[pl.ds(pl.multiple_of(odd * half, 16), half), :]
    send_ref[...] = rows_ref[pl.ds(pl.multiple_of((1 - odd) * half, 16), half), :].astype(BF16)


def assemble_kernel(scale, mine_ref, other_ref, out_ref, bias_ref, total_ref):
    channels = out_ref.shape[-1]
    half = mine_ref.shape[0]
    odd = lax.axis_index("lat") & 1
    for side, ref in ((odd, mine_ref), (1 - odd, other_ref)):
        total_ref[pl.ds(pl.multiple_of(side * half, 16), half), :] = ref[...].astype(F32) * scale
    high = 3 * channels
    for layer in range(2):
        for b in range(3):
            first = layer * high + b * channels
            pair = total_ref[first : first + channels, :]
            out_ref[layer, 0, b] = pair[:, :channels]
            out_ref[layer, 1, b] = pair[:, channels:]
            first = 2 * high + b * channels
            third = total_ref[first : first + channels, :]
            out_ref[layer, 2, b] = third[:, layer * channels : (layer + 1) * channels]
    bias = total_ref[3 * high : 3 * high + 1, :]
    bias_ref[0:1, :] = bias[:, :channels]
    bias_ref[1:2, :] = bias[:, channels:]


def partnered(block, devices, bit):
    return lax.ppermute(block, AXES, [(i, i ^ bit) for i in range(devices)])


def added(keep, send, devices):
    total = keep + partnered(send, devices, 1).astype(F32)
    for bit in [2 << k for k in range((devices // 2).bit_length() - 1)]:
        rounded = total.astype(BF16)
        total = rounded.astype(F32) + partnered(rounded, devices, bit).astype(F32)
    return total.astype(BF16)


def exchanged(parts):
    return lax.all_to_all(parts, AXES, 0, 0, tiled=True)


def local(inputs, weights, biases, cotangent):
    channels, cols, lat_rows = inputs.shape
    lons, lats = lax.axis_size("lon"), lax.axis_size("lat")
    devices = lons * lats
    share = cols * cols // devices
    width = lat_rows // cols * share
    span = lats * width
    scale = 1.0 / math.sqrt(cols * lons * lat_rows * lats)
    blocks = lats if width % LANES == 0 else 1
    shape = jax.ShapeDtypeStruct

    chunks = 2 * channels // min(channels, 256 // cols)
    fields_shape = (devices, 2 * channels, width)
    hbm = pl.BlockSpec(memory_space=pltpu.HBM)
    vmem = pl.BlockSpec(memory_space=pltpu.VMEM)

    packed = pl.pallas_call(
        functools.partial(pack_kernel, share),
        out_shape=shape(fields_shape, BF16),
        in_specs=[hbm, hbm],
        out_specs=hbm,
        scratch_shapes=[
            pltpu.VMEM((2,) + inputs.shape, BF16),
            pltpu.VMEM(fields_shape, BF16),
            pltpu.SemaphoreType.DMA((2,)),
            pltpu.SemaphoreType.DMA((2,)),
        ],
        compiler_params=WIDE,
    )(inputs, cotangent)
    packed, weights = lax.optimization_barrier((packed, weights))
    kernels = pl.pallas_call(
        kernels_kernel,
        out_shape=shape((4, 3 * channels, 3 * channels), BF16),
        compiler_params=PARAMS,
    )(weights)
    parts = exchanged(packed)
    if blocks == 1:
        parts = parts.reshape(lons, lats, 2 * channels, width).transpose(0, 2, 1, 3)
        parts = parts.reshape(lons, 2 * channels, span)

    cells = (lons, channels, span)
    high = 3 * channels
    fields, gated, total, bias_sums = pl.pallas_call(
        functools.partial(stack_kernel, share),
        out_shape=[
            shape(parts.shape, BF16),
            shape(cells, BF16),
            shape((high, high), F32),
            shape((16, channels), F32),
        ],
        out_specs=[hbm, vmem, vmem, vmem],
        scratch_shapes=[
            pltpu.VMEM(cells, BF16),
            pltpu.VMEM(cells, F32),
            pltpu.VMEM(cells, F32),
            pltpu.VMEM((lons, 3 * channels, span), BF16),
            pltpu.VMEM(parts.shape, BF16),
            pltpu.SemaphoreType.DMA((lons + 1,)),
        ],
        compiler_params=PARAMS,
    )(parts, kernels, biases[:, :, None])
    if blocks == 1:
        fields = fields.reshape(lons, 2 * channels, lats, width).transpose(0, 2, 1, 3)
        fields = fields.reshape(fields_shape)
    home = exchanged(fields)

    rows = 9 * channels + TAIL
    half_shape = (rows // 2, 2 * channels)
    flops = 9 * channels * parts.size
    keep, send = pl.pallas_call(
        functools.partial(sums_kernel, share),
        out_shape=[shape(half_shape, F32), shape(half_shape, BF16)],
        scratch_shapes=[pltpu.VMEM((rows, 2 * channels), F32)],
        compiler_params=PARAMS,
        cost_estimate=pl.CostEstimate(flops=flops, bytes_accessed=3 * parts.size, transcendentals=0),
    )(parts, gated, total, bias_sums)
    mine = added(keep, send, devices)
    home, mine = lax.optimization_barrier((home, mine))
    other = partnered(mine, devices, 1)
    features_out, grad_input = pl.pallas_call(
        functools.partial(unpack_kernel, share),
        out_shape=[shape(inputs.shape, BF16), shape(inputs.shape, BF16)],
        out_specs=[hbm, hbm],
        scratch_shapes=[
            pltpu.VMEM((2,) + inputs.shape, BF16),
            pltpu.SemaphoreType.DMA((chunks,)),
        ],
        compiler_params=PARAMS,
        cost_estimate=pl.CostEstimate(
            flops=4 * inputs.size * lat_rows, bytes_accessed=8 * inputs.size, transcendentals=0
        ),
    )(home)
    weight_grads, bias_grads = pl.pallas_call(
        functools.partial(assemble_kernel, scale),
        out_shape=[shape(weights.shape, F32), shape(biases.shape, F32)],
        scratch_shapes=[pltpu.VMEM((rows, 2 * channels), F32)],
        compiler_params=PARAMS,
    )(mine, other)
    return features_out, grad_input, weight_grads, bias_grads


def solution(mesh):
    in_specs = (P(None, "lon", "lat"), P(), P(), P(None, "lon", "lat"))
    out_specs = (P(None, "lon", "lat"), P(None, "lon", "lat"), P(), P())
    return jax.shard_map(local, mesh=mesh, in_specs=in_specs, out_specs=out_specs, check_vma=False)
```

```python
import functools
import math

import jax
import jax.numpy as jnp
from jax import lax
from jax.experimental import pallas as pl
from jax.experimental.pallas import tpu as pltpu
from jax.sharding import PartitionSpec as P


AXES = ("lon", "lat")
LANES = 128
TAIL = 32
BF16, F32 = jnp.bfloat16, jnp.float32
PARAMS = pltpu.CompilerParams(vmem_limit_bytes=24 * 2**20)
WIDE = pltpu.CompilerParams(vmem_limit_bytes=56 * 2**20)


def lane_order(cols, lat_rows, share, inverse):
    steps = lat_rows // cols
    place = lax.broadcasted_iota(jnp.int32, (lat_rows, lat_rows), 0 if inverse else 1)
    source = lax.broadcasted_iota(jnp.int32, (lat_rows, lat_rows), 1 if inverse else 0)
    group = lax.div(source & (cols - 1), share)
    wanted = (group * steps + lax.div(source, cols)) * share + (source & (share - 1))
    return (place == wanted).astype(F32).astype(BF16)


def row_order(outer, inner):
    rows = outer * inner
    place = lax.broadcasted_iota(jnp.int32, (rows, rows), 0)
    source = lax.broadcasted_iota(jnp.int32, (rows, rows), 1)
    wanted = (source & (inner - 1)) * outer + lax.div(source, inner)
    return (place == wanted).astype(F32).astype(BF16)


def product(left, right):
    return jnp.dot(left, right, preferred_element_type=F32)


def pack_kernel(share, x_ref, cot_ref, out_ref, buf, packed, in_sems, out_sems):
    _, channels, cols, lat_rows = buf.shape
    devices, _, width = packed.shape
    groups = devices // cols
    part = min(channels, 256 // cols)
    arrivals, departures = [], []
    for at, ref in enumerate((x_ref, cot_ref)):
        arrivals.append(pltpu.make_async_copy(ref, buf.at[at], in_sems.at[at]))
        rows = (slice(None), pl.ds(at * channels, channels), slice(None))
        departures.append(
            pltpu.make_async_copy(packed.at[rows], out_ref.at[rows], out_sems.at[at])
        )
        arrivals[at].start()
    lanes = lane_order(cols, lat_rows, share, False)
    order = row_order(part, cols)
    for at in range(2):
        arrivals[at].wait()
        for first in range(0, channels, part):
            rows = buf[at, first : first + part].reshape(part * cols, lat_rows)
            rows = product(order, rows).astype(BF16)
            rows = product(rows, lanes).astype(BF16)
            start = at * channels + first
            for col in range(cols):
                for group in range(groups):
                    packed[col * groups + group, start : start + part, :] = rows[
                        col * part : (col + 1) * part, group * width : (group + 1) * width
                    ]
        departures[at].start()
    for departure in departures:
        departure.wait()


def unpack_kernel(share, parts_ref, feat_ref, grad_ref, buf, sems):
    _, channels, cols, lat_rows = buf.shape
    devices, _, width = parts_ref.shape
    groups = devices // cols
    part = min(channels, 256 // cols)
    lanes = lane_order(cols, lat_rows, share, True)
    order = row_order(cols, part)
    departures = []
    for at, out_ref in enumerate((feat_ref, grad_ref)):
        for first in range(0, channels, part):
            start = at * channels + first
            rows = [
                jnp.concatenate(
                    [
                        parts_ref[col * groups + group, start : start + part, :]
                        for group in range(groups)
                    ],
                    axis=1,
                )
                for col in range(cols)
            ]
            rows = product(jnp.concatenate(rows, axis=0), lanes).astype(BF16)
            rows = product(order, rows).astype(BF16)
            buf[at, first : first + part] = rows.reshape(part, cols, lat_rows)
            rows = pl.ds(first, part)
            departures.append(
                pltpu.make_async_copy(buf.at[at, rows], out_ref.at[rows], sems.at[len(departures)])
            )
            departures[-1].start()
    for departure in departures:
        departure.wait()


def taps(row, shift):
    edge = jnp.zeros((row.shape[0], shift), row.dtype)
    before = jnp.concatenate([edge, row[:, :-shift]], axis=1)
    after = jnp.concatenate([row[:, shift:], edge], axis=1)
    return before, row, after


def kernels_kernel(w_ref, out_ref):
    for layer in range(2):
        for back in range(2):
            rows = []
            for a in range(3):
                row = [w_ref[layer, a, b] for b in range(3)]
                if back:
                    row = [tap.astype(F32).T.astype(BF16) for tap in row]
                rows.append(jnp.concatenate(row, axis=1))
            out_ref[2 * layer + back] = jnp.concatenate(rows, axis=0)


def line_of(parts_ref, count, channels, field, i):
    blocks = parts_ref.shape[0] // count
    rows = slice(field * channels, (field + 1) * channels)
    return jnp.concatenate([parts_ref[i * blocks + k, rows, :] for k in range(blocks)], axis=1)


def weight_product(gated, stack, lines):
    ones = jnp.ones((16, gated.shape[1]), BF16)
    across = (((1,), (1,)), ((), ()))
    bias = lax.dot_general(ones, gated, across, preferred_element_type=F32)
    lines = jnp.concatenate(lines, axis=0)
    return lax.dot_general(stack, lines, across, preferred_element_type=F32), bias


def back_taps(gated, shift):
    before, here, after = taps(gated, shift)
    return jnp.concatenate([after, here, before], axis=0)


def interleaved(count, hops, produce, consume):
    waiting = list(range(count))
    for i in range(count):
        produce(i)
        for j in list(waiting):
            if max((j - hops) % count, j, (j + hops) % count) <= i:
                waiting.remove(j)
                consume(j)


def stack_kernel(
    share,
    parts_ref,
    w_ref,
    b_ref,
    out_ref,
    gz_ref,
    total_ref,
    bias_ref,
    h_ref,
    s0_ref,
    s1_ref,
    y_ref,
    fields_ref,
    sems,
):
    count, channels, _ = h_ref.shape
    devices, _, width = parts_ref.shape
    blocks = devices // count
    copies = []

    def put(field, i, line):
        rows = slice(field * channels, (field + 1) * channels)
        for k in range(blocks):
            fields_ref[i * blocks + k, rows, :] = line[:, k * width : (k + 1) * width]

    def send(field, i, lines):
        place = (pl.ds(i * blocks, lines * blocks), pl.ds(field * channels, channels))
        copies.append(
            pltpu.make_async_copy(fields_ref.at[place], out_ref.at[place], sems.at[len(copies)])
        )
        copies[-1].start()

    def multiply(layer, i):
        line = line_of(parts_ref, count, channels, 0, i) if layer == 0 else h_ref[i]
        stack = jnp.concatenate(taps(line, 2**layer * share), axis=0)
        y_ref[i] = product(w_ref[2 * layer], stack)

    def activate(layer, i):
        hops = 2**layer
        pre = b_ref[layer] + y_ref[i, channels : 2 * channels]
        pre = pre + y_ref[(i - hops) % count, :channels]
        pre = pre + y_ref[(i + hops) % count, 2 * channels :]
        sigma = 0.5 * jnp.tanh(0.5 * pre) + 0.5
        state = pre * sigma
        slope = sigma + state * (1.0 - sigma)
        if layer == 0:
            h_ref[i] = state.astype(BF16)
            s0_ref[i] = slope
        else:
            s1_ref[i] = slope
            put(0, i, state.astype(BF16))

    def multiply_back(layer, i):
        hops = 2**layer
        if layer == 1:
            gated = line_of(parts_ref, count, channels, 1, i).astype(F32) * s1_ref[i]
            gated = gated.astype(BF16)
        else:
            gated = gz_ref[i]
        stack = back_taps(gated, hops * share)
        y_ref[i] = product(w_ref[2 * layer + 1], stack)
        if layer == 1:
            around = [h_ref[(i + (a - 1) * hops) % count] for a in range(3)]
            term, bias_term = weight_product(gated, stack, around)
            sums[0], sums[1] = sums[0] + term, sums[1] + bias_term

    def pass_back(layer, i):
        hops = 2**layer
        g = y_ref[i, channels : 2 * channels]
        g = g + y_ref[(i + hops) % count, :channels]
        g = g + y_ref[(i - hops) % count, 2 * channels :]
        g = g.astype(BF16)
        if layer == 1:
            gz_ref[i] = (g.astype(F32) * s0_ref[i]).astype(BF16)
        else:
            put(1, i, g)
            send(1, i, 1)

    sums = [0.0, 0.0]
    for layer in range(2):
        interleaved(count, 2**layer, functools.partial(multiply, layer), functools.partial(activate, layer))
    send(0, 0, count)
    for layer in (1, 0):
        interleaved(
            count,
            2**layer,
            functools.partial(multiply_back, layer),
            functools.partial(pass_back, layer),
        )
    total_ref[...], bias_ref[...] = sums
    for started in copies:
        started.wait()


def sums_kernel(share, parts_ref, gz_ref, total_ref, bias_ref, keep_ref, send_ref, rows_ref):
    count, channels, _ = gz_ref.shape
    high = 3 * channels
    total, bias = 0.0, 0.0
    for i in range(count):
        gated = gz_ref[i]
        around = [
            line_of(parts_ref, count, channels, 0, (i + a - 1) % count) for a in range(3)
        ]
        term, bias_term = weight_product(gated, back_taps(gated, share), around)
        total, bias = total + term, bias + bias_term
    for layer, sums in enumerate((total, total_ref[...])):
        rows_ref[layer * high : (layer + 1) * high, :] = sums[:, : 2 * channels]
        rows_ref[2 * high : 3 * high, layer * channels : (layer + 1) * channels] = sums[
            :, 2 * channels :
        ]
    bias = jnp.concatenate([bias[:1], bias_ref[:1]], axis=1)
    row = lax.broadcasted_iota(jnp.int32, (TAIL, 2 * channels), 0)
    rows_ref[3 * high :, :] = jnp.where(row == 0, bias, 0.0)
    half = keep_ref.shape[0]
    odd = lax.axis_index("lat") & 1
    keep_ref[...] = rows_ref[pl.ds(pl.multiple_of(odd * half, 16), half), :]
    send_ref[...] = rows_ref[pl.ds(pl.multiple_of((1 - odd) * half, 16), half), :].astype(BF16)


def assemble_kernel(scale, mine_ref, other_ref, out_ref, bias_ref, total_ref):
    channels = out_ref.shape[-1]
    half = mine_ref.shape[0]
    odd = lax.axis_index("lat") & 1
    for side, ref in ((odd, mine_ref), (1 - odd, other_ref)):
        total_ref[pl.ds(pl.multiple_of(side * half, 16), half), :] = ref[...].astype(F32) * scale
    high = 3 * channels
    for layer in range(2):
        for b in range(3):
            first = layer * high + b * channels
            pair = total_ref[first : first + channels, :]
            out_ref[layer, 0, b] = pair[:, :channels]
            out_ref[layer, 1, b] = pair[:, channels:]
            first = 2 * high + b * channels
            third = total_ref[first : first + channels, :]
            out_ref[layer, 2, b] = third[:, layer * channels : (layer + 1) * channels]
    bias = total_ref[3 * high : 3 * high + 1, :]
    bias_ref[0:1, :] = bias[:, :channels]
    bias_ref[1:2, :] = bias[:, channels:]


def partnered(block, devices, bit):
    return lax.ppermute(block, AXES, [(i, i ^ bit) for i in range(devices)])


def added(keep, send, devices):
    total = keep + partnered(send, devices, 1).astype(F32)
    for bit in [2 << k for k in range((devices // 2).bit_length() - 1)]:
        rounded = total.astype(BF16)
        total = rounded.astype(F32) + partnered(rounded, devices, bit).astype(F32)
    return total.astype(BF16)


def exchanged(parts):
    return lax.all_to_all(parts, AXES, 0, 0, tiled=True)


def local(inputs, weights, biases, cotangent):
    channels, cols, lat_rows = inputs.shape
    lons, lats = lax.axis_size("lon"), lax.axis_size("lat")
    devices = lons * lats
    share = cols * cols // devices
    width = lat_rows // cols * share
    span = lats * width
    scale = 1.0 / math.sqrt(cols * lons * lat_rows * lats)
    blocks = lats if width % LANES == 0 else 1
    shape = jax.ShapeDtypeStruct

    chunks = 2 * channels // min(channels, 256 // cols)
    fields_shape = (devices, 2 * channels, width)
    hbm = pl.BlockSpec(memory_space=pltpu.HBM)
    vmem = pl.BlockSpec(memory_space=pltpu.VMEM)

    packed = pl.pallas_call(
        functools.partial(pack_kernel, share),
        out_shape=shape(fields_shape, BF16),
        in_specs=[hbm, hbm],
        out_specs=hbm,
        scratch_shapes=[
            pltpu.VMEM((2,) + inputs.shape, BF16),
            pltpu.VMEM(fields_shape, BF16),
            pltpu.SemaphoreType.DMA((2,)),
            pltpu.SemaphoreType.DMA((2,)),
        ],
        compiler_params=WIDE,
    )(inputs, cotangent)
    packed, weights = lax.optimization_barrier((packed, weights))
    kernels = pl.pallas_call(
        kernels_kernel,
        out_shape=shape((4, 3 * channels, 3 * channels), BF16),
        compiler_params=PARAMS,
    )(weights)
    parts = exchanged(packed)
    if blocks == 1:
        parts = parts.reshape(lons, lats, 2 * channels, width).transpose(0, 2, 1, 3)
        parts = parts.reshape(lons, 2 * channels, span)

    cells = (lons, channels, span)
    high = 3 * channels
    fields, gated, total, bias_sums = pl.pallas_call(
        functools.partial(stack_kernel, share),
        out_shape=[
            shape(parts.shape, BF16),
            shape(cells, BF16),
            shape((high, high), F32),
            shape((16, channels), F32),
        ],
        out_specs=[hbm, vmem, vmem, vmem],
        scratch_shapes=[
            pltpu.VMEM(cells, BF16),
            pltpu.VMEM(cells, F32),
            pltpu.VMEM(cells, F32),
            pltpu.VMEM((lons, 3 * channels, span), F32),
            pltpu.VMEM(parts.shape, BF16),
            pltpu.SemaphoreType.DMA((lons + 1,)),
        ],
        compiler_params=PARAMS,
    )(parts, kernels, biases[:, :, None])
    if blocks == 1:
        fields = fields.reshape(lons, 2 * channels, lats, width).transpose(0, 2, 1, 3)
        fields = fields.reshape(fields_shape)
    home = exchanged(fields)

    rows = 9 * channels + TAIL
    half_shape = (rows // 2, 2 * channels)
    flops = 9 * channels * parts.size
    keep, send = pl.pallas_call(
        functools.partial(sums_kernel, share),
        out_shape=[shape(half_shape, F32), shape(half_shape, BF16)],
        scratch_shapes=[pltpu.VMEM((rows, 2 * channels), F32)],
        compiler_params=PARAMS,
        cost_estimate=pl.CostEstimate(flops=flops, bytes_accessed=3 * parts.size, transcendentals=0),
    )(parts, gated, total, bias_sums)
    mine = added(keep, send, devices)
    home, mine = lax.optimization_barrier((home, mine))
    other = partnered(mine, devices, 1)
    features_out, grad_input = pl.pallas_call(
        functools.partial(unpack_kernel, share),
        out_shape=[shape(inputs.shape, BF16), shape(inputs.shape, BF16)],
        out_specs=[hbm, hbm],
        scratch_shapes=[
            pltpu.VMEM((2,) + inputs.shape, BF16),
            pltpu.SemaphoreType.DMA((chunks,)),
        ],
        compiler_params=PARAMS,
        cost_estimate=pl.CostEstimate(
            flops=4 * inputs.size * lat_rows, bytes_accessed=8 * inputs.size, transcendentals=0
        ),
    )(home)
    weight_grads, bias_grads = pl.pallas_call(
        functools.partial(assemble_kernel, scale),
        out_shape=[shape(weights.shape, F32), shape(biases.shape, F32)],
        scratch_shapes=[pltpu.VMEM((rows, 2 * channels), F32)],
        compiler_params=PARAMS,
    )(mine, other)
    return features_out, grad_input, weight_grads, bias_grads


def solution(mesh):
    in_specs = (P(None, "lon", "lat"), P(), P(), P(None, "lon", "lat"))
    out_specs = (P(None, "lon", "lat"), P(None, "lon", "lat"), P(), P())
    return jax.shard_map(local, mesh=mesh, in_specs=in_specs, out_specs=out_specs, check_vma=False)
```

```python
import functools
import math

import jax
import jax.numpy as jnp
from jax import lax
from jax.experimental import pallas as pl
from jax.experimental.pallas import tpu as pltpu
from jax.sharding import PartitionSpec as P


AXES = ("lon", "lat")
LANES = 128
TAIL = 32
BF16, F32 = jnp.bfloat16, jnp.float32
PARAMS = pltpu.CompilerParams(vmem_limit_bytes=24 * 2**20)
WIDE = pltpu.CompilerParams(vmem_limit_bytes=56 * 2**20)


def lane_order(cols, lat_rows, share, inverse):
    steps = lat_rows // cols
    place = lax.broadcasted_iota(jnp.int32, (lat_rows, lat_rows), 0 if inverse else 1)
    source = lax.broadcasted_iota(jnp.int32, (lat_rows, lat_rows), 1 if inverse else 0)
    group = lax.div(source & (cols - 1), share)
    wanted = (group * steps + lax.div(source, cols)) * share + (source & (share - 1))
    return (place == wanted).astype(F32).astype(BF16)


def row_order(outer, inner):
    rows = outer * inner
    place = lax.broadcasted_iota(jnp.int32, (rows, rows), 0)
    source = lax.broadcasted_iota(jnp.int32, (rows, rows), 1)
    wanted = (source & (inner - 1)) * outer + lax.div(source, inner)
    return (place == wanted).astype(F32).astype(BF16)


def product(left, right):
    return jnp.dot(left, right, preferred_element_type=F32)


def pack_kernel(share, x_ref, cot_ref, out_ref, buf, packed, in_sems, out_sems):
    _, channels, cols, lat_rows = buf.shape
    devices, _, width = packed.shape
    groups = devices // cols
    part = min(channels, 256 // cols)
    arrivals, departures = [], []
    for at, ref in enumerate((x_ref, cot_ref)):
        arrivals.append(pltpu.make_async_copy(ref, buf.at[at], in_sems.at[at]))
        rows = (slice(None), pl.ds(at * channels, channels), slice(None))
        departures.append(
            pltpu.make_async_copy(packed.at[rows], out_ref.at[rows], out_sems.at[at])
        )
        arrivals[at].start()
    lanes = lane_order(cols, lat_rows, share, False)
    order = row_order(part, cols)
    for at in range(2):
        arrivals[at].wait()
        for first in range(0, channels, part):
            rows = buf[at, first : first + part].reshape(part * cols, lat_rows)
            rows = product(order, rows).astype(BF16)
            rows = product(rows, lanes).astype(BF16)
            start = at * channels + first
            for col in range(cols):
                for group in range(groups):
                    packed[col * groups + group, start : start + part, :] = rows[
                        col * part : (col + 1) * part, group * width : (group + 1) * width
                    ]
        departures[at].start()
    for departure in departures:
        departure.wait()


def unpack_kernel(share, parts_ref, feat_ref, grad_ref, buf, sems):
    _, channels, cols, lat_rows = buf.shape
    devices, _, width = parts_ref.shape
    groups = devices // cols
    part = min(channels, 256 // cols)
    lanes = lane_order(cols, lat_rows, share, True)
    order = row_order(cols, part)
    departures = []
    for at, out_ref in enumerate((feat_ref, grad_ref)):
        for first in range(0, channels, part):
            start = at * channels + first
            rows = [
                jnp.concatenate(
                    [
                        parts_ref[col * groups + group, start : start + part, :]
                        for group in range(groups)
                    ],
                    axis=1,
                )
                for col in range(cols)
            ]
            rows = product(jnp.concatenate(rows, axis=0), lanes).astype(BF16)
            rows = product(order, rows).astype(BF16)
            buf[at, first : first + part] = rows.reshape(part, cols, lat_rows)
            rows = pl.ds(first, part)
            departures.append(
                pltpu.make_async_copy(buf.at[at, rows], out_ref.at[rows], sems.at[len(departures)])
            )
            departures[-1].start()
    for departure in departures:
        departure.wait()


def taps(row, shift):
    edge = jnp.zeros((row.shape[0], shift), row.dtype)
    before = jnp.concatenate([edge, row[:, :-shift]], axis=1)
    after = jnp.concatenate([row[:, shift:], edge], axis=1)
    return before, row, after


def kernels_kernel(w_ref, out_ref):
    for layer in range(2):
        for back in range(2):
            rows = []
            for a in range(3):
                row = [w_ref[layer, a, b] for b in range(3)]
                if back:
                    row = [tap.astype(F32).T.astype(BF16) for tap in row]
                rows.append(jnp.concatenate(row, axis=1))
            out_ref[2 * layer + back] = jnp.concatenate(rows, axis=0)


def line_of(parts_ref, count, channels, field, i):
    blocks = parts_ref.shape[0] // count
    rows = slice(field * channels, (field + 1) * channels)
    return jnp.concatenate([parts_ref[i * blocks + k, rows, :] for k in range(blocks)], axis=1)


def weight_product(gated, stack, lines):
    ones = jnp.ones((16, gated.shape[1]), BF16)
    across = (((1,), (1,)), ((), ()))
    bias = lax.dot_general(ones, gated, across, preferred_element_type=F32)
    lines = jnp.concatenate(lines, axis=0)
    return lax.dot_general(stack, lines, across, preferred_element_type=F32), bias


def back_taps(gated, shift):
    before, here, after = taps(gated, shift)
    return jnp.concatenate([after, here, before], axis=0)


def forward_layer(layer, share, lines, w_ref, b_ref, y_ref, give):
    count, channels = y_ref.shape[0], y_ref.shape[1] // 3
    hops = 2**layer
    kernel = w_ref[2 * layer]
    for i in range(count):
        stack = jnp.concatenate(taps(lines(i), hops * share), axis=0)
        y_ref[i] = product(kernel, stack)
    bias = b_ref[layer]
    for i in range(count):
        pre = bias + y_ref[i, channels : 2 * channels]
        pre = pre + y_ref[(i - hops) % count, :channels]
        pre = pre + y_ref[(i + hops) % count, 2 * channels :]
        give(i, pre, 0.5 * jnp.tanh(0.5 * pre) + 0.5)


def stack_kernel(
    share,
    parts_ref,
    w_ref,
    b_ref,
    out_ref,
    gz0_ref,
    gz1_ref,
    h_ref,
    s0_ref,
    s1_ref,
    y_ref,
    fields_ref,
    sems,
):
    count, channels, _ = h_ref.shape
    devices, _, width = parts_ref.shape
    blocks = devices // count
    copies = []

    def put(field, i, line):
        rows = slice(field * channels, (field + 1) * channels)
        for k in range(blocks):
            fields_ref[i * blocks + k, rows, :] = line[:, k * width : (k + 1) * width]

    def send(field, i, lines):
        place = (pl.ds(i * blocks, lines * blocks), pl.ds(field * channels, channels))
        copies.append(
            pltpu.make_async_copy(fields_ref.at[place], out_ref.at[place], sems.at[len(copies)])
        )
        copies[-1].start()

    def give_hidden(i, pre, sigma):
        state = pre * sigma
        h_ref[i] = state.astype(BF16)
        s0_ref[i] = sigma + state * (1.0 - sigma)

    def give_features(i, pre, sigma):
        state = pre * sigma
        s1_ref[i] = sigma + state * (1.0 - sigma)
        put(0, i, state.astype(BF16))

    def line(i):
        return line_of(parts_ref, count, channels, 0, i)

    forward_layer(0, share, line, w_ref, b_ref, y_ref, give_hidden)
    forward_layer(1, share, lambda i: h_ref[i], w_ref, b_ref, y_ref, give_features)
    send(0, 0, count)

    for layer in (1, 0):
        hops = 2**layer
        kernel = w_ref[2 * layer + 1]
        for i in range(count):
            if layer == 1:
                gated = line_of(parts_ref, count, channels, 1, i).astype(F32) * s1_ref[i]
                gated = gated.astype(BF16)
                gz1_ref[i] = gated
            else:
                gated = gz0_ref[i]
            y_ref[i] = product(kernel, back_taps(gated, hops * share))
        for i in range(count):
            g = y_ref[i, channels : 2 * channels]
            g = g + y_ref[(i + hops) % count, :channels]
            g = g + y_ref[(i - hops) % count, 2 * channels :]
            g = g.astype(BF16)
            if layer == 1:
                gz0_ref[i] = (g.astype(F32) * s0_ref[i]).astype(BF16)
            else:
                put(1, i, g)
                send(1, i, 1)
    for started in copies:
        started.wait()


def sums_kernel(
    share, parts_ref, w_ref, b_ref, gz0_ref, gz1_ref, keep_ref, send_ref, rows_ref, h_ref, y_ref
):
    count, channels, _ = gz0_ref.shape
    high = 3 * channels

    def line(i):
        return line_of(parts_ref, count, channels, 0, i)

    def give_hidden(i, pre, sigma):
        h_ref[i] = (pre * sigma).astype(BF16)

    forward_layer(0, share, line, w_ref, b_ref, y_ref, give_hidden)
    biases = []
    for layer, gz_ref, lines in ((0, gz0_ref, line), (1, gz1_ref, lambda i: h_ref[i])):
        hops = 2**layer
        total, bias = 0.0, 0.0
        for i in range(count):
            gated = gz_ref[i]
            around = [lines((i + (a - 1) * hops) % count) for a in range(3)]
            term, bias_term = weight_product(gated, back_taps(gated, hops * share), around)
            total, bias = total + term, bias + bias_term
        rows_ref[layer * high : (layer + 1) * high, :] = total[:, : 2 * channels]
        rows_ref[2 * high : 3 * high, layer * channels : (layer + 1) * channels] = total[
            :, 2 * channels :
        ]
        biases.append(bias[:1])
    bias = jnp.concatenate(biases, axis=1)
    row = lax.broadcasted_iota(jnp.int32, (TAIL, 2 * channels), 0)
    rows_ref[3 * high :, :] = jnp.where(row == 0, bias, 0.0)
    half = keep_ref.shape[0]
    odd = lax.axis_index("lat") & 1
    keep_ref[...] = rows_ref[pl.ds(pl.multiple_of(odd * half, 16), half), :]
    send_ref[...] = rows_ref[pl.ds(pl.multiple_of((1 - odd) * half, 16), half), :].astype(BF16)


def assemble_kernel(scale, mine_ref, other_ref, out_ref, bias_ref, total_ref):
    channels = out_ref.shape[-1]
    half = mine_ref.shape[0]
    odd = lax.axis_index("lat") & 1
    for side, ref in ((odd, mine_ref), (1 - odd, other_ref)):
        total_ref[pl.ds(pl.multiple_of(side * half, 16), half), :] = ref[...].astype(F32) * scale
    high = 3 * channels
    for layer in range(2):
        for b in range(3):
            first = layer * high + b * channels
            pair = total_ref[first : first + channels, :]
            out_ref[layer, 0, b] = pair[:, :channels]
            out_ref[layer, 1, b] = pair[:, channels:]
            first = 2 * high + b * channels
            third = total_ref[first : first + channels, :]
            out_ref[layer, 2, b] = third[:, layer * channels : (layer + 1) * channels]
    bias = total_ref[3 * high : 3 * high + 1, :]
    bias_ref[0:1, :] = bias[:, :channels]
    bias_ref[1:2, :] = bias[:, channels:]


def partnered(block, devices, bit):
    return lax.ppermute(block, AXES, [(i, i ^ bit) for i in range(devices)])


def added(keep, send, devices):
    total = keep + partnered(send, devices, 1).astype(F32)
    for bit in [2 << k for k in range((devices // 2).bit_length() - 1)]:
        rounded = total.astype(BF16)
        total = rounded.astype(F32) + partnered(rounded, devices, bit).astype(F32)
    return total.astype(BF16)


def exchanged(parts):
    return lax.all_to_all(parts, AXES, 0, 0, tiled=True)


def local(inputs, weights, biases, cotangent):
    channels, cols, lat_rows = inputs.shape
    lons, lats = lax.axis_size("lon"), lax.axis_size("lat")
    devices = lons * lats
    share = cols * cols // devices
    width = lat_rows // cols * share
    span = lats * width
    scale = 1.0 / math.sqrt(cols * lons * lat_rows * lats)
    blocks = lats if width % LANES == 0 else 1
    shape = jax.ShapeDtypeStruct

    chunks = 2 * channels // min(channels, 256 // cols)
    fields_shape = (devices, 2 * channels, width)
    hbm = pl.BlockSpec(memory_space=pltpu.HBM)
    vmem = pl.BlockSpec(memory_space=pltpu.VMEM)

    packed = pl.pallas_call(
        functools.partial(pack_kernel, share),
        out_shape=shape(fields_shape, BF16),
        in_specs=[hbm, hbm],
        out_specs=hbm,
        scratch_shapes=[
            pltpu.VMEM((2,) + inputs.shape, BF16),
            pltpu.VMEM(fields_shape, BF16),
            pltpu.SemaphoreType.DMA((2,)),
            pltpu.SemaphoreType.DMA((2,)),
        ],
        compiler_params=WIDE,
    )(inputs, cotangent)
    packed, weights = lax.optimization_barrier((packed, weights))
    kernels = pl.pallas_call(
        kernels_kernel,
        out_shape=shape((4, 3 * channels, 3 * channels), BF16),
        compiler_params=PARAMS,
    )(weights)
    parts = exchanged(packed)
    if blocks == 1:
        parts = parts.reshape(lons, lats, 2 * channels, width).transpose(0, 2, 1, 3)
        parts = parts.reshape(lons, 2 * channels, span)

    cells = (lons, channels, span)
    column = biases[:, :, None]
    fields, gated0, gated1 = pl.pallas_call(
        functools.partial(stack_kernel, share),
        out_shape=[shape(parts.shape, BF16), shape(cells, BF16), shape(cells, BF16)],
        out_specs=[hbm, vmem, vmem],
        scratch_shapes=[
            pltpu.VMEM(cells, BF16),
            pltpu.VMEM(cells, F32),
            pltpu.VMEM(cells, F32),
            pltpu.VMEM((lons, 3 * channels, span), F32),
            pltpu.VMEM(parts.shape, BF16),
            pltpu.SemaphoreType.DMA((lons + 1,)),
        ],
        compiler_params=PARAMS,
    )(parts, kernels, column)
    if blocks == 1:
        fields = fields.reshape(lons, 2 * channels, lats, width).transpose(0, 2, 1, 3)
        fields = fields.reshape(fields_shape)
    home = exchanged(fields)

    rows = 9 * channels + TAIL
    half_shape = (rows // 2, 2 * channels)
    flops = 9 * channels * parts.size
    keep, send = pl.pallas_call(
        functools.partial(sums_kernel, share),
        out_shape=[shape(half_shape, F32), shape(half_shape, BF16)],
        scratch_shapes=[
            pltpu.VMEM((rows, 2 * channels), F32),
            pltpu.VMEM(cells, BF16),
            pltpu.VMEM((lons, 3 * channels, span), F32),
        ],
        compiler_params=PARAMS,
        cost_estimate=pl.CostEstimate(flops=flops, bytes_accessed=3 * parts.size, transcendentals=0),
    )(parts, kernels, column, gated0, gated1)
    mine = added(keep, send, devices)
    home, mine = lax.optimization_barrier((home, mine))
    other = partnered(mine, devices, 1)
    features_out, grad_input = pl.pallas_call(
        functools.partial(unpack_kernel, share),
        out_shape=[shape(inputs.shape, BF16), shape(inputs.shape, BF16)],
        out_specs=[hbm, hbm],
        scratch_shapes=[
            pltpu.VMEM((2,) + inputs.shape, BF16),
            pltpu.SemaphoreType.DMA((chunks,)),
        ],
        compiler_params=PARAMS,
        cost_estimate=pl.CostEstimate(
            flops=4 * inputs.size * lat_rows, bytes_accessed=8 * inputs.size, transcendentals=0
        ),
    )(home)
    weight_grads, bias_grads = pl.pallas_call(
        functools.partial(assemble_kernel, scale),
        out_shape=[shape(weights.shape, F32), shape(biases.shape, F32)],
        scratch_shapes=[pltpu.VMEM((rows, 2 * channels), F32)],
        compiler_params=PARAMS,
    )(mine, other)
    return features_out, grad_input, weight_grads, bias_grads


def solution(mesh):
    in_specs = (P(None, "lon", "lat"), P(), P(), P(None, "lon", "lat"))
    out_specs = (P(None, "lon", "lat"), P(None, "lon", "lat"), P(), P())
    return jax.shard_map(local, mesh=mesh, in_specs=in_specs, out_specs=out_specs, check_vma=False)
```

```python
import functools
import math

import jax
import jax.numpy as jnp
from jax import lax
from jax.experimental import pallas as pl
from jax.experimental.pallas import tpu as pltpu
from jax.sharding import PartitionSpec as P


AXES = ("lon", "lat")
LANES = 128
TAIL = 32
BF16, F32 = jnp.bfloat16, jnp.float32
PARAMS = pltpu.CompilerParams(vmem_limit_bytes=24 * 2**20)
WIDE = pltpu.CompilerParams(vmem_limit_bytes=56 * 2**20)


def lane_order(cols, lat_rows, share, inverse):
    steps = lat_rows // cols
    place = lax.broadcasted_iota(jnp.int32, (lat_rows, lat_rows), 0 if inverse else 1)
    source = lax.broadcasted_iota(jnp.int32, (lat_rows, lat_rows), 1 if inverse else 0)
    group = lax.div(source & (cols - 1), share)
    wanted = (group * steps + lax.div(source, cols)) * share + (source & (share - 1))
    return (place == wanted).astype(F32).astype(BF16)


def row_order(outer, inner):
    rows = outer * inner
    place = lax.broadcasted_iota(jnp.int32, (rows, rows), 0)
    source = lax.broadcasted_iota(jnp.int32, (rows, rows), 1)
    wanted = (source & (inner - 1)) * outer + lax.div(source, inner)
    return (place == wanted).astype(F32).astype(BF16)


def product(left, right):
    return jnp.dot(left, right, preferred_element_type=F32)


def pack_kernel(share, x_ref, cot_ref, out_ref, buf, packed, in_sems, out_sems):
    _, channels, cols, lat_rows = buf.shape
    devices, _, width = packed.shape
    groups = devices // cols
    part = min(channels, 256 // cols)
    arrivals, departures = [], []
    for at, ref in enumerate((x_ref, cot_ref)):
        arrivals.append(pltpu.make_async_copy(ref, buf.at[at], in_sems.at[at]))
        rows = (slice(None), pl.ds(at * channels, channels), slice(None))
        departures.append(
            pltpu.make_async_copy(packed.at[rows], out_ref.at[rows], out_sems.at[at])
        )
        arrivals[at].start()
    lanes = lane_order(cols, lat_rows, share, False)
    order = row_order(part, cols)
    for at in range(2):
        arrivals[at].wait()
        for first in range(0, channels, part):
            rows = buf[at, first : first + part].reshape(part * cols, lat_rows)
            rows = product(order, rows).astype(BF16)
            rows = product(rows, lanes).astype(BF16)
            start = at * channels + first
            for col in range(cols):
                for group in range(groups):
                    packed[col * groups + group, start : start + part, :] = rows[
                        col * part : (col + 1) * part, group * width : (group + 1) * width
                    ]
        departures[at].start()
    for departure in departures:
        departure.wait()


def unpack_kernel(share, parts_ref, feat_ref, grad_ref, buf, sems):
    _, channels, cols, lat_rows = buf.shape
    devices, _, width = parts_ref.shape
    groups = devices // cols
    part = min(channels, 256 // cols)
    lanes = lane_order(cols, lat_rows, share, True)
    order = row_order(cols, part)
    departures = []
    for at, out_ref in enumerate((feat_ref, grad_ref)):
        for first in range(0, channels, part):
            start = at * channels + first
            rows = [
                jnp.concatenate(
                    [
                        parts_ref[col * groups + group, start : start + part, :]
                        for group in range(groups)
                    ],
                    axis=1,
                )
                for col in range(cols)
            ]
            rows = product(jnp.concatenate(rows, axis=0), lanes).astype(BF16)
            rows = product(order, rows).astype(BF16)
            buf[at, first : first + part] = rows.reshape(part, cols, lat_rows)
            rows = pl.ds(first, part)
            departures.append(
                pltpu.make_async_copy(buf.at[at, rows], out_ref.at[rows], sems.at[len(departures)])
            )
            departures[-1].start()
    for departure in departures:
        departure.wait()


def taps(row, shift):
    edge = jnp.zeros((row.shape[0], shift), row.dtype)
    before = jnp.concatenate([edge, row[:, :-shift]], axis=1)
    after = jnp.concatenate([row[:, shift:], edge], axis=1)
    return before, row, after


def kernels_kernel(w_ref, first_ref, rest_ref):
    for layer in range(2):
        for back in range(2):
            rows = []
            for a in range(3):
                row = [w_ref[layer, a, b] for b in range(3)]
                if back:
                    row = [tap.astype(F32).T.astype(BF16) for tap in row]
                rows.append(jnp.concatenate(row, axis=1))
            rows = jnp.concatenate(rows, axis=0)
            if layer or back:
                rest_ref[2 * layer + back - 1] = rows
            else:
                first_ref[...] = rows


def line_of(parts_ref, count, channels, field, i):
    blocks = parts_ref.shape[0] // count
    rows = slice(field * channels, (field + 1) * channels)
    return jnp.concatenate([parts_ref[i * blocks + k, rows, :] for k in range(blocks)], axis=1)


def weight_product(gated, stack, lines):
    ones = jnp.ones((16, gated.shape[1]), BF16)
    across = (((1,), (1,)), ((), ()))
    bias = lax.dot_general(ones, gated, across, preferred_element_type=F32)
    lines = jnp.concatenate(lines, axis=0)
    return lax.dot_general(stack, lines, across, preferred_element_type=F32), bias


def back_taps(gated, shift):
    before, here, after = taps(gated, shift)
    return jnp.concatenate([after, here, before], axis=0)


def forward_layer(layer, share, lines, kernel, b_ref, y_ref, give):
    count, channels = y_ref.shape[0], y_ref.shape[1] // 3
    hops = 2**layer
    for i in range(count):
        stack = jnp.concatenate(taps(lines(i), hops * share), axis=0)
        y_ref[i] = product(kernel, stack)
    bias = b_ref[layer]
    for i in range(count):
        pre = bias + y_ref[i, channels : 2 * channels]
        pre = pre + y_ref[(i - hops) % count, :channels]
        pre = pre + y_ref[(i + hops) % count, 2 * channels :]
        give(i, pre, 0.5 * jnp.tanh(0.5 * pre) + 0.5)


def stack_kernel(
    share,
    parts_ref,
    first_ref,
    rest_ref,
    b_ref,
    out_ref,
    gz0_ref,
    gz1_ref,
    h_ref,
    s0_ref,
    s1_ref,
    y_ref,
    fields_ref,
    sems,
):
    count, channels, _ = h_ref.shape
    devices, _, width = parts_ref.shape
    blocks = devices // count
    copies = []

    def put(field, i, line):
        rows = slice(field * channels, (field + 1) * channels)
        for k in range(blocks):
            fields_ref[i * blocks + k, rows, :] = line[:, k * width : (k + 1) * width]

    def send(field, i, lines):
        place = (pl.ds(i * blocks, lines * blocks), pl.ds(field * channels, channels))
        copies.append(
            pltpu.make_async_copy(fields_ref.at[place], out_ref.at[place], sems.at[len(copies)])
        )
        copies[-1].start()

    def give_hidden(i, pre, sigma):
        state = pre * sigma
        h_ref[i] = state.astype(BF16)
        s0_ref[i] = sigma + state * (1.0 - sigma)

    def give_features(i, pre, sigma):
        state = pre * sigma
        s1_ref[i] = sigma + state * (1.0 - sigma)
        put(0, i, state.astype(BF16))

    def line(i):
        return line_of(parts_ref, count, channels, 0, i)

    forward_layer(0, share, line, first_ref[...], b_ref, y_ref, give_hidden)
    forward_layer(1, share, lambda i: h_ref[i], rest_ref[1], b_ref, y_ref, give_features)
    send(0, 0, count)

    for layer in (1, 0):
        hops = 2**layer
        kernel = rest_ref[2 * layer]
        for i in range(count):
            if layer == 1:
                gated = line_of(parts_ref, count, channels, 1, i).astype(F32) * s1_ref[i]
                gated = gated.astype(BF16)
                gz1_ref[i] = gated
            else:
                gated = gz0_ref[i]
            y_ref[i] = product(kernel, back_taps(gated, hops * share))
        for i in range(count):
            g = y_ref[i, channels : 2 * channels]
            g = g + y_ref[(i + hops) % count, :channels]
            g = g + y_ref[(i - hops) % count, 2 * channels :]
            g = g.astype(BF16)
            if layer == 1:
                gz0_ref[i] = (g.astype(F32) * s0_ref[i]).astype(BF16)
            else:
                put(1, i, g)
                send(1, i, 1)
    for started in copies:
        started.wait()


def sums_kernel(
    share, parts_ref, first_ref, b_ref, gz0_ref, gz1_ref, keep_ref, send_ref, rows_ref, h_ref, y_ref
):
    count, channels, _ = gz0_ref.shape
    high = 3 * channels

    def line(i):
        return line_of(parts_ref, count, channels, 0, i)

    def give_hidden(i, pre, sigma):
        h_ref[i] = (pre * sigma).astype(BF16)

    forward_layer(0, share, line, first_ref[...], b_ref, y_ref, give_hidden)
    biases = []
    for layer, gz_ref, lines in ((0, gz0_ref, line), (1, gz1_ref, lambda i: h_ref[i])):
        hops = 2**layer
        total, bias = 0.0, 0.0
        for i in range(count):
            gated = gz_ref[i]
            around = [lines((i + (a - 1) * hops) % count) for a in range(3)]
            term, bias_term = weight_product(gated, back_taps(gated, hops * share), around)
            total, bias = total + term, bias + bias_term
        rows_ref[layer * high : (layer + 1) * high, :] = total[:, : 2 * channels]
        rows_ref[2 * high : 3 * high, layer * channels : (layer + 1) * channels] = total[
            :, 2 * channels :
        ]
        biases.append(bias[:1])
    bias = jnp.concatenate(biases, axis=1)
    row = lax.broadcasted_iota(jnp.int32, (TAIL, 2 * channels), 0)
    rows_ref[3 * high :, :] = jnp.where(row == 0, bias, 0.0)
    half = keep_ref.shape[0]
    odd = lax.axis_index("lat") & 1
    keep_ref[...] = rows_ref[pl.ds(pl.multiple_of(odd * half, 16), half), :]
    send_ref[...] = rows_ref[pl.ds(pl.multiple_of((1 - odd) * half, 16), half), :].astype(BF16)


def assemble_kernel(scale, mine_ref, other_ref, out_ref, bias_ref, total_ref):
    channels = out_ref.shape[-1]
    half = mine_ref.shape[0]
    odd = lax.axis_index("lat") & 1
    for side, ref in ((odd, mine_ref), (1 - odd, other_ref)):
        total_ref[pl.ds(pl.multiple_of(side * half, 16), half), :] = ref[...].astype(F32) * scale
    high = 3 * channels
    for layer in range(2):
        for b in range(3):
            first = layer * high + b * channels
            pair = total_ref[first : first + channels, :]
            out_ref[layer, 0, b] = pair[:, :channels]
            out_ref[layer, 1, b] = pair[:, channels:]
            first = 2 * high + b * channels
            third = total_ref[first : first + channels, :]
            out_ref[layer, 2, b] = third[:, layer * channels : (layer + 1) * channels]
    bias = total_ref[3 * high : 3 * high + 1, :]
    bias_ref[0:1, :] = bias[:, :channels]
    bias_ref[1:2, :] = bias[:, channels:]


def partnered(block, devices, bit):
    return lax.ppermute(block, AXES, [(i, i ^ bit) for i in range(devices)])


def added(keep, send, devices):
    total = keep + partnered(send, devices, 1).astype(F32)
    for bit in [2 << k for k in range((devices // 2).bit_length() - 1)]:
        rounded = total.astype(BF16)
        total = rounded.astype(F32) + partnered(rounded, devices, bit).astype(F32)
    return total.astype(BF16)


def exchanged(parts):
    return lax.all_to_all(parts, AXES, 0, 0, tiled=True)


def local(inputs, weights, biases, cotangent):
    channels, cols, lat_rows = inputs.shape
    lons, lats = lax.axis_size("lon"), lax.axis_size("lat")
    devices = lons * lats
    share = cols * cols // devices
    width = lat_rows // cols * share
    span = lats * width
    scale = 1.0 / math.sqrt(cols * lons * lat_rows * lats)
    blocks = lats if width % LANES == 0 else 1
    shape = jax.ShapeDtypeStruct

    chunks = 2 * channels // min(channels, 256 // cols)
    fields_shape = (devices, 2 * channels, width)
    hbm = pl.BlockSpec(memory_space=pltpu.HBM)
    vmem = pl.BlockSpec(memory_space=pltpu.VMEM)

    packed = pl.pallas_call(
        functools.partial(pack_kernel, share),
        out_shape=shape(fields_shape, BF16),
        in_specs=[hbm, hbm],
        out_specs=hbm,
        scratch_shapes=[
            pltpu.VMEM((2,) + inputs.shape, BF16),
            pltpu.VMEM(fields_shape, BF16),
            pltpu.SemaphoreType.DMA((2,)),
            pltpu.SemaphoreType.DMA((2,)),
        ],
        compiler_params=WIDE,
    )(inputs, cotangent)
    packed, weights = lax.optimization_barrier((packed, weights))
    first, rest = pl.pallas_call(
        kernels_kernel,
        out_shape=[
            shape((3 * channels, 3 * channels), BF16),
            shape((3, 3 * channels, 3 * channels), BF16),
        ],
        compiler_params=PARAMS,
    )(weights)
    parts = exchanged(packed)
    if blocks == 1:
        parts = parts.reshape(lons, lats, 2 * channels, width).transpose(0, 2, 1, 3)
        parts = parts.reshape(lons, 2 * channels, span)

    cells = (lons, channels, span)
    column = biases[:, :, None]
    fields, gated0, gated1 = pl.pallas_call(
        functools.partial(stack_kernel, share),
        out_shape=[shape(parts.shape, BF16), shape(cells, BF16), shape(cells, BF16)],
        out_specs=[hbm, vmem, vmem],
        scratch_shapes=[
            pltpu.VMEM(cells, BF16),
            pltpu.VMEM(cells, F32),
            pltpu.VMEM(cells, F32),
            pltpu.VMEM((lons, 3 * channels, span), F32),
            pltpu.VMEM(parts.shape, BF16),
            pltpu.SemaphoreType.DMA((lons + 1,)),
        ],
        compiler_params=PARAMS,
    )(parts, first, rest, column)
    if blocks == 1:
        fields = fields.reshape(lons, 2 * channels, lats, width).transpose(0, 2, 1, 3)
        fields = fields.reshape(fields_shape)
    home = exchanged(fields)

    rows = 9 * channels + TAIL
    half_shape = (rows // 2, 2 * channels)
    flops = 9 * channels * parts.size
    keep, send = pl.pallas_call(
        functools.partial(sums_kernel, share),
        out_shape=[shape(half_shape, F32), shape(half_shape, BF16)],
        scratch_shapes=[
            pltpu.VMEM((rows, 2 * channels), F32),
            pltpu.VMEM(cells, BF16),
            pltpu.VMEM((lons, 3 * channels, span), F32),
        ],
        compiler_params=PARAMS,
        cost_estimate=pl.CostEstimate(flops=flops, bytes_accessed=3 * parts.size, transcendentals=0),
    )(parts, first, column, gated0, gated1)
    mine = added(keep, send, devices)
    home, mine = lax.optimization_barrier((home, mine))
    other = partnered(mine, devices, 1)
    features_out, grad_input = pl.pallas_call(
        functools.partial(unpack_kernel, share),
        out_shape=[shape(inputs.shape, BF16), shape(inputs.shape, BF16)],
        out_specs=[hbm, hbm],
        scratch_shapes=[
            pltpu.VMEM((2,) + inputs.shape, BF16),
            pltpu.SemaphoreType.DMA((chunks,)),
        ],
        compiler_params=PARAMS,
        cost_estimate=pl.CostEstimate(
            flops=4 * inputs.size * lat_rows, bytes_accessed=8 * inputs.size, transcendentals=0
        ),
    )(home)
    weight_grads, bias_grads = pl.pallas_call(
        functools.partial(assemble_kernel, scale),
        out_shape=[shape(weights.shape, F32), shape(biases.shape, F32)],
        scratch_shapes=[pltpu.VMEM((rows, 2 * channels), F32)],
        compiler_params=PARAMS,
    )(mine, other)
    return features_out, grad_input, weight_grads, bias_grads


def solution(mesh):
    in_specs = (P(None, "lon", "lat"), P(), P(), P(None, "lon", "lat"))
    out_specs = (P(None, "lon", "lat"), P(None, "lon", "lat"), P(), P())
    return jax.shard_map(local, mesh=mesh, in_specs=in_specs, out_specs=out_specs, check_vma=False)
```

```python
import functools
import math

import jax
import jax.numpy as jnp
from jax import lax
from jax.experimental import pallas as pl
from jax.experimental.pallas import tpu as pltpu
from jax.sharding import PartitionSpec as P


AXES = ("lon", "lat")
LANES = 128
TAIL = 32
BF16, F32 = jnp.bfloat16, jnp.float32
PARAMS = pltpu.CompilerParams(vmem_limit_bytes=24 * 2**20)
WIDE = pltpu.CompilerParams(vmem_limit_bytes=56 * 2**20)


def lane_order(cols, lat_rows, share, inverse):
    steps = lat_rows // cols
    place = lax.broadcasted_iota(jnp.int32, (lat_rows, lat_rows), 0 if inverse else 1)
    source = lax.broadcasted_iota(jnp.int32, (lat_rows, lat_rows), 1 if inverse else 0)
    group = lax.div(source & (cols - 1), share)
    wanted = (group * steps + lax.div(source, cols)) * share + (source & (share - 1))
    return (place == wanted).astype(F32).astype(BF16)


def row_order(outer, inner):
    rows = outer * inner
    place = lax.broadcasted_iota(jnp.int32, (rows, rows), 0)
    source = lax.broadcasted_iota(jnp.int32, (rows, rows), 1)
    wanted = (source & (inner - 1)) * outer + lax.div(source, inner)
    return (place == wanted).astype(F32).astype(BF16)


def product(left, right):
    return jnp.dot(left, right, preferred_element_type=F32)


def pack_kernel(share, x_ref, cot_ref, out_ref, buf, packed, in_sems, out_sems):
    _, channels, cols, lat_rows = buf.shape
    devices, _, width = packed.shape
    groups = devices // cols
    part = min(channels, 256 // cols)
    arrivals, departures = [], []
    for at, ref in enumerate((x_ref, cot_ref)):
        arrivals.append(pltpu.make_async_copy(ref, buf.at[at], in_sems.at[at]))
        rows = (slice(None), pl.ds(at * channels, channels), slice(None))
        departures.append(
            pltpu.make_async_copy(packed.at[rows], out_ref.at[rows], out_sems.at[at])
        )
        arrivals[at].start()
    lanes = lane_order(cols, lat_rows, share, False)
    order = row_order(part, cols)
    for at in range(2):
        arrivals[at].wait()
        for first in range(0, channels, part):
            rows = buf[at, first : first + part].reshape(part * cols, lat_rows)
            rows = product(order, rows).astype(BF16)
            rows = product(rows, lanes).astype(BF16)
            start = at * channels + first
            for col in range(cols):
                for group in range(groups):
                    packed[col * groups + group, start : start + part, :] = rows[
                        col * part : (col + 1) * part, group * width : (group + 1) * width
                    ]
        departures[at].start()
    for departure in departures:
        departure.wait()


def unpack_kernel(share, parts_ref, feat_ref, grad_ref, buf, sems):
    _, channels, cols, lat_rows = buf.shape
    devices, _, width = parts_ref.shape
    groups = devices // cols
    part = min(channels, 256 // cols)
    lanes = lane_order(cols, lat_rows, share, True)
    order = row_order(cols, part)
    departures = []
    for at, out_ref in enumerate((feat_ref, grad_ref)):
        for first in range(0, channels, part):
            start = at * channels + first
            rows = [
                jnp.concatenate(
                    [
                        parts_ref[col * groups + group, start : start + part, :]
                        for group in range(groups)
                    ],
                    axis=1,
                )
                for col in range(cols)
            ]
            rows = product(jnp.concatenate(rows, axis=0), lanes).astype(BF16)
            rows = product(order, rows).astype(BF16)
            buf[at, first : first + part] = rows.reshape(part, cols, lat_rows)
            rows = pl.ds(first, part)
            departures.append(
                pltpu.make_async_copy(buf.at[at, rows], out_ref.at[rows], sems.at[len(departures)])
            )
            departures[-1].start()
    for departure in departures:
        departure.wait()


def taps(row, shift):
    edge = jnp.zeros((row.shape[0], shift), row.dtype)
    before = jnp.concatenate([edge, row[:, :-shift]], axis=1)
    after = jnp.concatenate([row[:, shift:], edge], axis=1)
    return before, row, after


def kernels_kernel(w_ref, first_ref, rest_ref):
    for layer in range(2):
        for back in range(2):
            rows = []
            for a in range(3):
                row = [w_ref[layer, a, b] for b in range(3)]
                if back:
                    row = [tap.astype(F32).T.astype(BF16) for tap in row]
                rows.append(jnp.concatenate(row, axis=1))
            rows = jnp.concatenate(rows, axis=0)
            if layer or back:
                rest_ref[2 * layer + back - 1] = rows
            else:
                first_ref[...] = rows


def line_of(parts_ref, count, channels, field, i):
    blocks = parts_ref.shape[0] // count
    rows = slice(field * channels, (field + 1) * channels)
    return jnp.concatenate([parts_ref[i * blocks + k, rows, :] for k in range(blocks)], axis=1)


def weight_product(gated, stack, lines):
    ones = jnp.ones((16, gated.shape[1]), BF16)
    across = (((1,), (1,)), ((), ()))
    bias = lax.dot_general(ones, gated, across, preferred_element_type=F32)
    lines = jnp.concatenate(lines, axis=0)
    return lax.dot_general(stack, lines, across, preferred_element_type=F32), bias


def back_taps(gated, shift):
    before, here, after = taps(gated, shift)
    return jnp.concatenate([after, here, before], axis=0)


def forward_layer(layer, share, lines, kernel, b_ref, y_ref, give):
    count, channels = y_ref.shape[0], y_ref.shape[1] // 3
    hops = 2**layer
    for i in range(count):
        stack = jnp.concatenate(taps(lines(i), hops * share), axis=0)
        y_ref[i] = product(kernel, stack)
    bias = b_ref[layer]
    for i in range(count):
        pre = bias + y_ref[i, channels : 2 * channels]
        pre = pre + y_ref[(i - hops) % count, :channels]
        pre = pre + y_ref[(i + hops) % count, 2 * channels :]
        give(i, pre, 0.5 * jnp.tanh(0.5 * pre) + 0.5)


def stack_kernel(
    share,
    parts_ref,
    first_ref,
    rest_ref,
    b_ref,
    out_ref,
    gz0_ref,
    gz1_ref,
    h_ref,
    s0_ref,
    s1_ref,
    y_ref,
    fields_ref,
    sems,
):
    count, channels, _ = h_ref.shape
    devices, _, width = parts_ref.shape
    blocks = devices // count
    copies = []

    def put(field, i, line):
        rows = slice(field * channels, (field + 1) * channels)
        for k in range(blocks):
            fields_ref[i * blocks + k, rows, :] = line[:, k * width : (k + 1) * width]

    def send(field, i, lines):
        place = (pl.ds(i * blocks, lines * blocks), pl.ds(field * channels, channels))
        copies.append(
            pltpu.make_async_copy(fields_ref.at[place], out_ref.at[place], sems.at[len(copies)])
        )
        copies[-1].start()

    def give_hidden(i, pre, sigma):
        state = pre * sigma
        h_ref[i] = state.astype(BF16)
        s0_ref[i] = sigma + state * (1.0 - sigma)

    def give_features(i, pre, sigma):
        state = pre * sigma
        s1_ref[i] = sigma + state * (1.0 - sigma)
        put(0, i, state.astype(BF16))

    def line(i):
        return line_of(parts_ref, count, channels, 0, i)

    forward_layer(0, share, line, first_ref[...], b_ref, y_ref, give_hidden)
    forward_layer(1, share, lambda i: h_ref[i], rest_ref[1], b_ref, y_ref, give_features)
    send(0, 0, count)

    for layer in (1, 0):
        hops = 2**layer
        kernel = rest_ref[2 * layer]
        for i in range(count):
            if layer == 1:
                gated = line_of(parts_ref, count, channels, 1, i).astype(F32) * s1_ref[i]
                gated = gated.astype(BF16)
                gz1_ref[i] = gated
            else:
                gated = gz0_ref[i]
            y_ref[i] = product(kernel, back_taps(gated, hops * share))
        for i in range(count):
            g = y_ref[i, channels : 2 * channels]
            g = g + y_ref[(i + hops) % count, :channels]
            g = g + y_ref[(i - hops) % count, 2 * channels :]
            g = g.astype(BF16)
            if layer == 1:
                gz0_ref[i] = (g.astype(F32) * s0_ref[i]).astype(BF16)
            else:
                put(1, i, g)
                send(1, i, 1)
    for started in copies:
        started.wait()


def sums_kernel(
    share, parts_ref, first_ref, b_ref, gz0_ref, gz1_ref, keep_ref, send_ref, rows_ref, h_ref, y_ref
):
    count, channels, _ = gz0_ref.shape
    high = 3 * channels

    def line(i):
        return line_of(parts_ref, count, channels, 0, i)

    def give_hidden(i, pre, sigma):
        h_ref[i] = (pre * sigma).astype(BF16)

    forward_layer(0, share, line, first_ref[...], b_ref, y_ref, give_hidden)
    biases = []
    for layer, gz_ref, lines in ((0, gz0_ref, line), (1, gz1_ref, lambda i: h_ref[i])):
        hops = 2**layer
        total, bias = 0.0, 0.0
        for i in range(count):
            gated = gz_ref[i]
            around = [lines((i + (a - 1) * hops) % count) for a in range(3)]
            term, bias_term = weight_product(gated, back_taps(gated, hops * share), around)
            total, bias = total + term, bias + bias_term
        rows_ref[layer * high : (layer + 1) * high, :] = total[:, : 2 * channels]
        rows_ref[2 * high : 3 * high, layer * channels : (layer + 1) * channels] = total[
            :, 2 * channels :
        ]
        biases.append(bias[:1])
    bias = jnp.concatenate(biases, axis=1)
    row = lax.broadcasted_iota(jnp.int32, (TAIL, 2 * channels), 0)
    rows_ref[3 * high :, :] = jnp.where(row == 0, bias, 0.0)
    half = keep_ref.shape[0]
    odd = lax.axis_index("lat") & 1
    keep_ref[...] = rows_ref[pl.ds(pl.multiple_of(odd * half, 16), half), :]
    send_ref[...] = rows_ref[pl.ds(pl.multiple_of((1 - odd) * half, 16), half), :].astype(BF16)


def assemble_kernel(scale, mine_ref, other_ref, out_ref, bias_ref, total_ref):
    channels = out_ref.shape[-1]
    half = mine_ref.shape[0]
    odd = lax.axis_index("lat") & 1
    for side, ref in ((odd, mine_ref), (1 - odd, other_ref)):
        total_ref[pl.ds(pl.multiple_of(side * half, 16), half), :] = ref[...].astype(F32) * scale
    high = 3 * channels
    for layer in range(2):
        for b in range(3):
            first = layer * high + b * channels
            pair = total_ref[first : first + channels, :]
            out_ref[layer, 0, b] = pair[:, :channels]
            out_ref[layer, 1, b] = pair[:, channels:]
            first = 2 * high + b * channels
            third = total_ref[first : first + channels, :]
            out_ref[layer, 2, b] = third[:, layer * channels : (layer + 1) * channels]
    bias = total_ref[3 * high : 3 * high + 1, :]
    bias_ref[0:1, :] = bias[:, :channels]
    bias_ref[1:2, :] = bias[:, channels:]


def partnered(block, devices, bit):
    return lax.ppermute(block, AXES, [(i, i ^ bit) for i in range(devices)])


def added(keep, send, devices):
    total = keep + partnered(send, devices, 1).astype(F32)
    bit = 2
    while True:
        rounded = total.astype(BF16)
        came = partnered(rounded, devices, bit)
        bit *= 2
        if bit >= devices:
            return rounded, came
        total = rounded.astype(F32) + came.astype(F32)


def exchanged(parts):
    return lax.all_to_all(parts, AXES, 0, 0, tiled=True)


def local(inputs, weights, biases, cotangent):
    channels, cols, lat_rows = inputs.shape
    lons, lats = lax.axis_size("lon"), lax.axis_size("lat")
    devices = lons * lats
    share = cols * cols // devices
    width = lat_rows // cols * share
    span = lats * width
    scale = 1.0 / math.sqrt(cols * lons * lat_rows * lats)
    blocks = lats if width % LANES == 0 else 1
    shape = jax.ShapeDtypeStruct

    chunks = 2 * channels // min(channels, 256 // cols)
    fields_shape = (devices, 2 * channels, width)
    hbm = pl.BlockSpec(memory_space=pltpu.HBM)
    vmem = pl.BlockSpec(memory_space=pltpu.VMEM)

    packed = pl.pallas_call(
        functools.partial(pack_kernel, share),
        out_shape=shape(fields_shape, BF16),
        in_specs=[hbm, hbm],
        out_specs=hbm,
        scratch_shapes=[
            pltpu.VMEM((2,) + inputs.shape, BF16),
            pltpu.VMEM(fields_shape, BF16),
            pltpu.SemaphoreType.DMA((2,)),
            pltpu.SemaphoreType.DMA((2,)),
        ],
        compiler_params=WIDE,
    )(inputs, cotangent)
    packed, weights = lax.optimization_barrier((packed, weights))
    first, rest = pl.pallas_call(
        kernels_kernel,
        out_shape=[
            shape((3 * channels, 3 * channels), BF16),
            shape((3, 3 * channels, 3 * channels), BF16),
        ],
        compiler_params=PARAMS,
    )(weights)
    parts = exchanged(packed)
    if blocks == 1:
        parts = parts.reshape(lons, lats, 2 * channels, width).transpose(0, 2, 1, 3)
        parts = parts.reshape(lons, 2 * channels, span)

    cells = (lons, channels, span)
    column = biases[:, :, None]
    fields, gated0, gated1 = pl.pallas_call(
        functools.partial(stack_kernel, share),
        out_shape=[shape(parts.shape, BF16), shape(cells, BF16), shape(cells, BF16)],
        out_specs=[hbm, vmem, vmem],
        scratch_shapes=[
            pltpu.VMEM(cells, BF16),
            pltpu.VMEM(cells, F32),
            pltpu.VMEM(cells, F32),
            pltpu.VMEM((lons, 3 * channels, span), F32),
            pltpu.VMEM(parts.shape, BF16),
            pltpu.SemaphoreType.DMA((lons + 1,)),
        ],
        compiler_params=PARAMS,
    )(parts, first, rest, column)
    if blocks == 1:
        fields = fields.reshape(lons, 2 * channels, lats, width).transpose(0, 2, 1, 3)
        fields = fields.reshape(fields_shape)
    home = exchanged(fields)

    rows = 9 * channels + TAIL
    half_shape = (rows // 2, 2 * channels)
    flops = 9 * channels * parts.size
    keep, send = pl.pallas_call(
        functools.partial(sums_kernel, share),
        out_shape=[shape(half_shape, F32), shape(half_shape, BF16)],
        scratch_shapes=[
            pltpu.VMEM((rows, 2 * channels), F32),
            pltpu.VMEM(cells, BF16),
            pltpu.VMEM((lons, 3 * channels, span), F32),
        ],
        compiler_params=PARAMS,
        cost_estimate=pl.CostEstimate(flops=flops, bytes_accessed=3 * parts.size, transcendentals=0),
    )(parts, first, column, gated0, gated1)
    rounded, came = added(keep, send, devices)
    features_out, grad_input = pl.pallas_call(
        functools.partial(unpack_kernel, share),
        out_shape=[shape(inputs.shape, BF16), shape(inputs.shape, BF16)],
        out_specs=[hbm, hbm],
        scratch_shapes=[
            pltpu.VMEM((2,) + inputs.shape, BF16),
            pltpu.SemaphoreType.DMA((chunks,)),
        ],
        compiler_params=PARAMS,
        cost_estimate=pl.CostEstimate(
            flops=4 * inputs.size * lat_rows, bytes_accessed=8 * inputs.size, transcendentals=0
        ),
    )(home)
    came, grad_input = lax.optimization_barrier((came, grad_input))
    mine = (rounded.astype(F32) + came.astype(F32)).astype(BF16)
    other = partnered(mine, devices, 1)
    weight_grads, bias_grads = pl.pallas_call(
        functools.partial(assemble_kernel, scale),
        out_shape=[shape(weights.shape, F32), shape(biases.shape, F32)],
        scratch_shapes=[pltpu.VMEM((rows, 2 * channels), F32)],
        compiler_params=PARAMS,
    )(mine, other)
    return features_out, grad_input, weight_grads, bias_grads


def solution(mesh):
    in_specs = (P(None, "lon", "lat"), P(), P(), P(None, "lon", "lat"))
    out_specs = (P(None, "lon", "lat"), P(None, "lon", "lat"), P(), P())
    return jax.shard_map(local, mesh=mesh, in_specs=in_specs, out_specs=out_specs, check_vma=False)
```

```python
import functools
import math

import jax
import jax.numpy as jnp
from jax import lax
from jax.experimental import pallas as pl
from jax.experimental.pallas import tpu as pltpu
from jax.sharding import PartitionSpec as P


AXES = ("lon", "lat")
LANES = 128
TAIL = 32
BF16, F32 = jnp.bfloat16, jnp.float32
PARAMS = pltpu.CompilerParams(vmem_limit_bytes=24 * 2**20)
WIDE = pltpu.CompilerParams(vmem_limit_bytes=56 * 2**20)


def lane_order(cols, lat_rows, share, inverse):
    steps = lat_rows // cols
    place = lax.broadcasted_iota(jnp.int32, (lat_rows, lat_rows), 0 if inverse else 1)
    source = lax.broadcasted_iota(jnp.int32, (lat_rows, lat_rows), 1 if inverse else 0)
    group = lax.div(source & (cols - 1), share)
    wanted = (group * steps + lax.div(source, cols)) * share + (source & (share - 1))
    return (place == wanted).astype(F32).astype(BF16)


def row_order(outer, inner):
    rows = outer * inner
    place = lax.broadcasted_iota(jnp.int32, (rows, rows), 0)
    source = lax.broadcasted_iota(jnp.int32, (rows, rows), 1)
    wanted = (source & (inner - 1)) * outer + lax.div(source, inner)
    return (place == wanted).astype(F32).astype(BF16)


def product(left, right):
    return jnp.dot(left, right, preferred_element_type=F32)


def pack_kernel(share, x_ref, cot_ref, out_ref, buf, packed, in_sems, out_sems):
    _, channels, cols, lat_rows = buf.shape
    devices, _, width = packed.shape
    groups = devices // cols
    part = min(channels, 256 // cols)
    arrivals, departures = [], []
    for at, ref in enumerate((x_ref, cot_ref)):
        arrivals.append(pltpu.make_async_copy(ref, buf.at[at], in_sems.at[at]))
        rows = (slice(None), pl.ds(at * channels, channels), slice(None))
        departures.append(
            pltpu.make_async_copy(packed.at[rows], out_ref.at[rows], out_sems.at[at])
        )
        arrivals[at].start()
    lanes = lane_order(cols, lat_rows, share, False)
    order = row_order(part, cols)
    for at in range(2):
        arrivals[at].wait()
        for first in range(0, channels, part):
            rows = buf[at, first : first + part].reshape(part * cols, lat_rows)
            rows = product(order, rows).astype(BF16)
            rows = product(rows, lanes).astype(BF16)
            start = at * channels + first
            for col in range(cols):
                for group in range(groups):
                    packed[col * groups + group, start : start + part, :] = rows[
                        col * part : (col + 1) * part, group * width : (group + 1) * width
                    ]
        departures[at].start()
    for departure in departures:
        departure.wait()


def unpack_kernel(share, field, parts_ref, out_ref, buf, sems):
    channels, cols, lat_rows = buf.shape
    devices, _, width = parts_ref.shape
    groups = devices // cols
    part = min(channels, 256 // cols)
    lanes = lane_order(cols, lat_rows, share, True)
    order = row_order(cols, part)
    departures = []
    for first in range(0, channels, part):
        start = field * channels + first
        rows = [
            jnp.concatenate(
                [
                    parts_ref[col * groups + group, start : start + part, :]
                    for group in range(groups)
                ],
                axis=1,
            )
            for col in range(cols)
        ]
        rows = product(jnp.concatenate(rows, axis=0), lanes).astype(BF16)
        rows = product(order, rows).astype(BF16)
        buf[first : first + part] = rows.reshape(part, cols, lat_rows)
        rows = pl.ds(first, part)
        departures.append(
            pltpu.make_async_copy(buf.at[rows], out_ref.at[rows], sems.at[len(departures)])
        )
        departures[-1].start()
    for departure in departures:
        departure.wait()


def taps(row, shift):
    edge = jnp.zeros((row.shape[0], shift), row.dtype)
    before = jnp.concatenate([edge, row[:, :-shift]], axis=1)
    after = jnp.concatenate([row[:, shift:], edge], axis=1)
    return before, row, after


def kernels_kernel(w_ref, first_ref, rest_ref):
    for layer in range(2):
        for back in range(2):
            rows = []
            for a in range(3):
                row = [w_ref[layer, a, b] for b in range(3)]
                if back:
                    row = [tap.astype(F32).T.astype(BF16) for tap in row]
                rows.append(jnp.concatenate(row, axis=1))
            rows = jnp.concatenate(rows, axis=0)
            if layer or back:
                rest_ref[2 * layer + back - 1] = rows
            else:
                first_ref[...] = rows


def line_of(parts_ref, count, channels, field, i):
    blocks = parts_ref.shape[0] // count
    rows = slice(field * channels, (field + 1) * channels)
    return jnp.concatenate([parts_ref[i * blocks + k, rows, :] for k in range(blocks)], axis=1)


def weight_product(gated, stack, lines):
    ones = jnp.ones((16, gated.shape[1]), BF16)
    across = (((1,), (1,)), ((), ()))
    bias = lax.dot_general(ones, gated, across, preferred_element_type=F32)
    lines = jnp.concatenate(lines, axis=0)
    return lax.dot_general(stack, lines, across, preferred_element_type=F32), bias


def back_taps(gated, shift):
    before, here, after = taps(gated, shift)
    return jnp.concatenate([after, here, before], axis=0)


def forward_layer(layer, share, lines, kernel, b_ref, y_ref, give):
    count, channels = y_ref.shape[0], y_ref.shape[1] // 3
    hops = 2**layer
    for i in range(count):
        stack = jnp.concatenate(taps(lines(i), hops * share), axis=0)
        y_ref[i] = product(kernel, stack)
    bias = b_ref[layer]
    for i in range(count):
        pre = bias + y_ref[i, channels : 2 * channels]
        pre = pre + y_ref[(i - hops) % count, :channels]
        pre = pre + y_ref[(i + hops) % count, 2 * channels :]
        give(i, pre, 0.5 * jnp.tanh(0.5 * pre) + 0.5)


def stack_kernel(
    share,
    parts_ref,
    first_ref,
    rest_ref,
    b_ref,
    out_ref,
    gz0_ref,
    gz1_ref,
    h_ref,
    s0_ref,
    s1_ref,
    y_ref,
    fields_ref,
    sems,
):
    count, channels, _ = h_ref.shape
    devices, _, width = parts_ref.shape
    blocks = devices // count
    copies = []

    def put(field, i, line):
        rows = slice(field * channels, (field + 1) * channels)
        for k in range(blocks):
            fields_ref[i * blocks + k, rows, :] = line[:, k * width : (k + 1) * width]

    def send(field, i, lines):
        place = (pl.ds(i * blocks, lines * blocks), pl.ds(field * channels, channels))
        copies.append(
            pltpu.make_async_copy(fields_ref.at[place], out_ref.at[place], sems.at[len(copies)])
        )
        copies[-1].start()

    def give_hidden(i, pre, sigma):
        state = pre * sigma
        h_ref[i] = state.astype(BF16)
        s0_ref[i] = sigma + state * (1.0 - sigma)

    def give_features(i, pre, sigma):
        state = pre * sigma
        s1_ref[i] = sigma + state * (1.0 - sigma)
        put(0, i, state.astype(BF16))

    def line(i):
        return line_of(parts_ref, count, channels, 0, i)

    forward_layer(0, share, line, first_ref[...], b_ref, y_ref, give_hidden)
    forward_layer(1, share, lambda i: h_ref[i], rest_ref[1], b_ref, y_ref, give_features)
    send(0, 0, count)

    for layer in (1, 0):
        hops = 2**layer
        kernel = rest_ref[2 * layer]
        for i in range(count):
            if layer == 1:
                gated = line_of(parts_ref, count, channels, 1, i).astype(F32) * s1_ref[i]
                gated = gated.astype(BF16)
                gz1_ref[i] = gated
            else:
                gated = gz0_ref[i]
            y_ref[i] = product(kernel, back_taps(gated, hops * share))
        for i in range(count):
            g = y_ref[i, channels : 2 * channels]
            g = g + y_ref[(i + hops) % count, :channels]
            g = g + y_ref[(i - hops) % count, 2 * channels :]
            g = g.astype(BF16)
            if layer == 1:
                gz0_ref[i] = (g.astype(F32) * s0_ref[i]).astype(BF16)
            else:
                put(1, i, g)
                send(1, i, 1)
    for started in copies:
        started.wait()


def sums_kernel(
    share, parts_ref, first_ref, b_ref, gz0_ref, gz1_ref, keep_ref, send_ref, rows_ref, h_ref, y_ref
):
    count, channels, _ = gz0_ref.shape
    high = 3 * channels

    def line(i):
        return line_of(parts_ref, count, channels, 0, i)

    def give_hidden(i, pre, sigma):
        h_ref[i] = (pre * sigma).astype(BF16)

    forward_layer(0, share, line, first_ref[...], b_ref, y_ref, give_hidden)
    biases = []
    for layer, gz_ref, lines in ((0, gz0_ref, line), (1, gz1_ref, lambda i: h_ref[i])):
        hops = 2**layer
        total, bias = 0.0, 0.0
        for i in range(count):
            gated = gz_ref[i]
            around = [lines((i + (a - 1) * hops) % count) for a in range(3)]
            term, bias_term = weight_product(gated, back_taps(gated, hops * share), around)
            total, bias = total + term, bias + bias_term
        rows_ref[layer * high : (layer + 1) * high, :] = total[:, : 2 * channels]
        rows_ref[2 * high : 3 * high, layer * channels : (layer + 1) * channels] = total[
            :, 2 * channels :
        ]
        biases.append(bias[:1])
    bias = jnp.concatenate(biases, axis=1)
    row = lax.broadcasted_iota(jnp.int32, (TAIL, 2 * channels), 0)
    rows_ref[3 * high :, :] = jnp.where(row == 0, bias, 0.0)
    half = keep_ref.shape[0]
    odd = lax.axis_index("lat") & 1
    keep_ref[...] = rows_ref[pl.ds(pl.multiple_of(odd * half, 16), half), :]
    send_ref[...] = rows_ref[pl.ds(pl.multiple_of((1 - odd) * half, 16), half), :].astype(BF16)


def assemble_kernel(scale, mine_ref, other_ref, out_ref, bias_ref, total_ref):
    channels = out_ref.shape[-1]
    half = mine_ref.shape[0]
    odd = lax.axis_index("lat") & 1
    for side, ref in ((odd, mine_ref), (1 - odd, other_ref)):
        total_ref[pl.ds(pl.multiple_of(side * half, 16), half), :] = ref[...].astype(F32) * scale
    high = 3 * channels
    for layer in range(2):
        for b in range(3):
            first = layer * high + b * channels
            pair = total_ref[first : first + channels, :]
            out_ref[layer, 0, b] = pair[:, :channels]
            out_ref[layer, 1, b] = pair[:, channels:]
            first = 2 * high + b * channels
            third = total_ref[first : first + channels, :]
            out_ref[layer, 2, b] = third[:, layer * channels : (layer + 1) * channels]
    bias = total_ref[3 * high : 3 * high + 1, :]
    bias_ref[0:1, :] = bias[:, :channels]
    bias_ref[1:2, :] = bias[:, channels:]


def partnered(block, devices, bit):
    return lax.ppermute(block, AXES, [(i, i ^ bit) for i in range(devices)])


def added(keep, send, devices):
    total = keep + partnered(send, devices, 1).astype(F32)
    bit = 2
    while True:
        rounded = total.astype(BF16)
        came = partnered(rounded, devices, bit)
        bit *= 2
        if bit >= devices:
            return rounded, came
        total = rounded.astype(F32) + came.astype(F32)


def exchanged(parts):
    return lax.all_to_all(parts, AXES, 0, 0, tiled=True)


def local(inputs, weights, biases, cotangent):
    channels, cols, lat_rows = inputs.shape
    lons, lats = lax.axis_size("lon"), lax.axis_size("lat")
    devices = lons * lats
    share = cols * cols // devices
    width = lat_rows // cols * share
    span = lats * width
    scale = 1.0 / math.sqrt(cols * lons * lat_rows * lats)
    blocks = lats if width % LANES == 0 else 1
    shape = jax.ShapeDtypeStruct

    chunks = 2 * channels // min(channels, 256 // cols)
    fields_shape = (devices, 2 * channels, width)
    hbm = pl.BlockSpec(memory_space=pltpu.HBM)
    vmem = pl.BlockSpec(memory_space=pltpu.VMEM)

    packed = pl.pallas_call(
        functools.partial(pack_kernel, share),
        out_shape=shape(fields_shape, BF16),
        in_specs=[hbm, hbm],
        out_specs=hbm,
        scratch_shapes=[
            pltpu.VMEM((2,) + inputs.shape, BF16),
            pltpu.VMEM(fields_shape, BF16),
            pltpu.SemaphoreType.DMA((2,)),
            pltpu.SemaphoreType.DMA((2,)),
        ],
        compiler_params=WIDE,
    )(inputs, cotangent)
    packed, weights = lax.optimization_barrier((packed, weights))
    first, rest = pl.pallas_call(
        kernels_kernel,
        out_shape=[
            shape((3 * channels, 3 * channels), BF16),
            shape((3, 3 * channels, 3 * channels), BF16),
        ],
        compiler_params=PARAMS,
    )(weights)
    parts = exchanged(packed)
    if blocks == 1:
        parts = parts.reshape(lons, lats, 2 * channels, width).transpose(0, 2, 1, 3)
        parts = parts.reshape(lons, 2 * channels, span)

    cells = (lons, channels, span)
    column = biases[:, :, None]
    fields, gated0, gated1 = pl.pallas_call(
        functools.partial(stack_kernel, share),
        out_shape=[shape(parts.shape, BF16), shape(cells, BF16), shape(cells, BF16)],
        out_specs=[hbm, vmem, vmem],
        scratch_shapes=[
            pltpu.VMEM(cells, BF16),
            pltpu.VMEM(cells, F32),
            pltpu.VMEM(cells, F32),
            pltpu.VMEM((lons, 3 * channels, span), F32),
            pltpu.VMEM(parts.shape, BF16),
            pltpu.SemaphoreType.DMA((lons + 1,)),
        ],
        compiler_params=PARAMS,
    )(parts, first, rest, column)
    if blocks == 1:
        fields = fields.reshape(lons, 2 * channels, lats, width).transpose(0, 2, 1, 3)
        fields = fields.reshape(fields_shape)
    home = exchanged(fields)

    rows = 9 * channels + TAIL
    half_shape = (rows // 2, 2 * channels)
    flops = 9 * channels * parts.size
    keep, send = pl.pallas_call(
        functools.partial(sums_kernel, share),
        out_shape=[shape(half_shape, F32), shape(half_shape, BF16)],
        scratch_shapes=[
            pltpu.VMEM((rows, 2 * channels), F32),
            pltpu.VMEM(cells, BF16),
            pltpu.VMEM((lons, 3 * channels, span), F32),
        ],
        compiler_params=PARAMS,
        cost_estimate=pl.CostEstimate(flops=flops, bytes_accessed=3 * parts.size, transcendentals=0),
    )(parts, first, column, gated0, gated1)
    rounded, came = added(keep, send, devices)
    def unpacked(field, parts):
        return pl.pallas_call(
            functools.partial(unpack_kernel, share, field),
            out_shape=shape(inputs.shape, BF16),
            out_specs=hbm,
            scratch_shapes=[
                pltpu.VMEM(inputs.shape, BF16),
                pltpu.SemaphoreType.DMA((chunks // 2,)),
            ],
            compiler_params=PARAMS,
            cost_estimate=pl.CostEstimate(
                flops=2 * inputs.size * lat_rows, bytes_accessed=4 * inputs.size, transcendentals=0
            ),
        )(parts)

    features_out = unpacked(0, home)
    came, features_out, home = lax.optimization_barrier((came, features_out, home))
    grad_input = unpacked(1, home)
    mine = (rounded.astype(F32) + came.astype(F32)).astype(BF16)
    other = partnered(mine, devices, 1)
    weight_grads, bias_grads = pl.pallas_call(
        functools.partial(assemble_kernel, scale),
        out_shape=[shape(weights.shape, F32), shape(biases.shape, F32)],
        scratch_shapes=[pltpu.VMEM((rows, 2 * channels), F32)],
        compiler_params=PARAMS,
    )(mine, other)
    return features_out, grad_input, weight_grads, bias_grads


def solution(mesh):
    in_specs = (P(None, "lon", "lat"), P(), P(), P(None, "lon", "lat"))
    out_specs = (P(None, "lon", "lat"), P(None, "lon", "lat"), P(), P())
    return jax.shard_map(local, mesh=mesh, in_specs=in_specs, out_specs=out_specs, check_vma=False)
```

```python
import functools
import math

import jax
import jax.numpy as jnp
from jax import lax
from jax.experimental import pallas as pl
from jax.experimental.pallas import tpu as pltpu
from jax.sharding import PartitionSpec as P


AXES = ("lon", "lat")
LANES = 128
TAIL = 32
BF16, F32 = jnp.bfloat16, jnp.float32
PARAMS = pltpu.CompilerParams(vmem_limit_bytes=24 * 2**20)
WIDE = pltpu.CompilerParams(vmem_limit_bytes=56 * 2**20)


def lane_order(cols, lat_rows, share, inverse):
    steps = lat_rows // cols
    place = lax.broadcasted_iota(jnp.int32, (lat_rows, lat_rows), 0 if inverse else 1)
    source = lax.broadcasted_iota(jnp.int32, (lat_rows, lat_rows), 1 if inverse else 0)
    group = lax.div(source & (cols - 1), share)
    wanted = (group * steps + lax.div(source, cols)) * share + (source & (share - 1))
    return (place == wanted).astype(F32).astype(BF16)


def row_order(outer, inner):
    rows = outer * inner
    place = lax.broadcasted_iota(jnp.int32, (rows, rows), 0)
    source = lax.broadcasted_iota(jnp.int32, (rows, rows), 1)
    wanted = (source & (inner - 1)) * outer + lax.div(source, inner)
    return (place == wanted).astype(F32).astype(BF16)


def product(left, right):
    return jnp.dot(left, right, preferred_element_type=F32)


def pack_kernel(share, x_ref, cot_ref, out_ref, buf, packed, in_sems, out_sems):
    _, channels, cols, lat_rows = buf.shape
    devices, _, width = packed.shape
    groups = devices // cols
    part = min(channels, 256 // cols)
    arrivals, departures = [], []
    for at, ref in enumerate((x_ref, cot_ref)):
        arrivals.append(pltpu.make_async_copy(ref, buf.at[at], in_sems.at[at]))
        rows = (slice(None), pl.ds(at * channels, channels), slice(None))
        departures.append(
            pltpu.make_async_copy(packed.at[rows], out_ref.at[rows], out_sems.at[at])
        )
        arrivals[at].start()
    lanes = lane_order(cols, lat_rows, share, False)
    order = row_order(part, cols)
    for at in range(2):
        arrivals[at].wait()
        for first in range(0, channels, part):
            rows = buf[at, first : first + part].reshape(part * cols, lat_rows)
            rows = product(order, rows).astype(BF16)
            rows = product(rows, lanes).astype(BF16)
            start = at * channels + first
            for col in range(cols):
                for group in range(groups):
                    packed[col * groups + group, start : start + part, :] = rows[
                        col * part : (col + 1) * part, group * width : (group + 1) * width
                    ]
        departures[at].start()
    for departure in departures:
        departure.wait()


def unpack_kernel(share, field, parts_ref, out_ref, buf, sems):
    channels, cols, lat_rows = buf.shape
    devices, _, width = parts_ref.shape
    groups = devices // cols
    part = min(channels, 256 // cols)
    lanes = lane_order(cols, lat_rows, share, True)
    order = row_order(cols, part)
    departures = []
    for first in range(0, channels, part):
        start = field * channels + first
        rows = [
            jnp.concatenate(
                [
                    parts_ref[col * groups + group, start : start + part, :]
                    for group in range(groups)
                ],
                axis=1,
            )
            for col in range(cols)
        ]
        rows = product(jnp.concatenate(rows, axis=0), lanes).astype(BF16)
        rows = product(order, rows).astype(BF16)
        buf[first : first + part] = rows.reshape(part, cols, lat_rows)
        rows = pl.ds(first, part)
        departures.append(
            pltpu.make_async_copy(buf.at[rows], out_ref.at[rows], sems.at[len(departures)])
        )
        departures[-1].start()
    for departure in departures:
        departure.wait()


def taps(row, shift):
    edge = jnp.zeros((row.shape[0], shift), row.dtype)
    before = jnp.concatenate([edge, row[:, :-shift]], axis=1)
    after = jnp.concatenate([row[:, shift:], edge], axis=1)
    return before, row, after


def kernels_kernel(w_ref, first_ref, rest_ref):
    for layer in range(2):
        for back in range(2):
            rows = []
            for a in range(3):
                row = [w_ref[layer, a, b] for b in range(3)]
                if back:
                    row = [tap.astype(F32).T.astype(BF16) for tap in row]
                rows.append(jnp.concatenate(row, axis=1))
            rows = jnp.concatenate(rows, axis=0)
            if layer or back:
                rest_ref[2 * layer + back - 1] = rows
            else:
                first_ref[...] = rows


def line_of(parts_ref, count, channels, field, i):
    blocks = parts_ref.shape[0] // count
    rows = slice(field * channels, (field + 1) * channels)
    return jnp.concatenate([parts_ref[i * blocks + k, rows, :] for k in range(blocks)], axis=1)


def weight_product(gated, stack, lines):
    ones = jnp.ones((16, gated.shape[1]), BF16)
    across = (((1,), (1,)), ((), ()))
    bias = lax.dot_general(ones, gated, across, preferred_element_type=F32)
    lines = jnp.concatenate(lines, axis=0)
    return lax.dot_general(stack, lines, across, preferred_element_type=F32), bias


def back_taps(gated, shift):
    before, here, after = taps(gated, shift)
    return jnp.concatenate([after, here, before], axis=0)


def forward_layer(layer, share, lines, kernel, b_ref, y_ref, give):
    count, channels = y_ref.shape[0], y_ref.shape[1] // 3
    hops = 2**layer
    for i in range(count):
        stack = jnp.concatenate(taps(lines(i), hops * share), axis=0)
        y_ref[i] = product(kernel, stack)
    bias = b_ref[layer]
    for i in range(count):
        pre = bias + y_ref[i, channels : 2 * channels]
        pre = pre + y_ref[(i - hops) % count, :channels]
        pre = pre + y_ref[(i + hops) % count, 2 * channels :]
        give(i, pre, 0.5 * jnp.tanh(0.5 * pre) + 0.5)


def stack_kernel(
    share,
    parts_ref,
    first_ref,
    rest_ref,
    b_ref,
    out_ref,
    gz0_ref,
    gz1_ref,
    h_ref,
    s0_ref,
    s1_ref,
    y_ref,
    fields_ref,
    sems,
):
    count, channels, _ = h_ref.shape
    devices, _, width = parts_ref.shape
    blocks = devices // count
    copies = []

    def put(field, i, line):
        rows = slice(field * channels, (field + 1) * channels)
        for k in range(blocks):
            fields_ref[i * blocks + k, rows, :] = line[:, k * width : (k + 1) * width]

    def send(field, i, lines):
        place = (pl.ds(i * blocks, lines * blocks), pl.ds(field * channels, channels))
        copies.append(
            pltpu.make_async_copy(fields_ref.at[place], out_ref.at[place], sems.at[len(copies)])
        )
        copies[-1].start()

    def give_hidden(i, pre, sigma):
        state = pre * sigma
        h_ref[i] = state.astype(BF16)
        s0_ref[i] = sigma + state * (1.0 - sigma)

    def give_features(i, pre, sigma):
        state = pre * sigma
        s1_ref[i] = sigma + state * (1.0 - sigma)
        put(0, i, state.astype(BF16))

    def line(i):
        return line_of(parts_ref, count, channels, 0, i)

    forward_layer(0, share, line, first_ref[...], b_ref, y_ref, give_hidden)
    forward_layer(1, share, lambda i: h_ref[i], rest_ref[1], b_ref, y_ref, give_features)
    send(0, 0, count)

    for layer in (1, 0):
        hops = 2**layer
        kernel = rest_ref[2 * layer]
        for i in range(count):
            if layer == 1:
                gated = line_of(parts_ref, count, channels, 1, i).astype(F32) * s1_ref[i]
                gated = gated.astype(BF16)
                gz1_ref[i] = gated
            else:
                gated = gz0_ref[i]
            y_ref[i] = product(kernel, back_taps(gated, hops * share))
        for i in range(count):
            g = y_ref[i, channels : 2 * channels]
            g = g + y_ref[(i + hops) % count, :channels]
            g = g + y_ref[(i - hops) % count, 2 * channels :]
            g = g.astype(BF16)
            if layer == 1:
                gz0_ref[i] = (g.astype(F32) * s0_ref[i]).astype(BF16)
            else:
                put(1, i, g)
                if count % 2:
                    send(1, i, 1)
                elif i % 2:
                    send(1, i - 1, 2)
    for started in copies:
        started.wait()


def sums_kernel(
    share, parts_ref, first_ref, b_ref, gz0_ref, gz1_ref, keep_ref, send_ref, rows_ref, h_ref, y_ref
):
    count, channels, _ = gz0_ref.shape
    high = 3 * channels

    def line(i):
        return line_of(parts_ref, count, channels, 0, i)

    def give_hidden(i, pre, sigma):
        h_ref[i] = (pre * sigma).astype(BF16)

    forward_layer(0, share, line, first_ref[...], b_ref, y_ref, give_hidden)
    biases = []
    for layer, gz_ref, lines in ((0, gz0_ref, line), (1, gz1_ref, lambda i: h_ref[i])):
        hops = 2**layer
        total, bias = 0.0, 0.0
        for i in range(count):
            gated = gz_ref[i]
            around = [lines((i + (a - 1) * hops) % count) for a in range(3)]
            term, bias_term = weight_product(gated, back_taps(gated, hops * share), around)
            total, bias = total + term, bias + bias_term
        rows_ref[layer * high : (layer + 1) * high, :] = total[:, : 2 * channels]
        rows_ref[2 * high : 3 * high, layer * channels : (layer + 1) * channels] = total[
            :, 2 * channels :
        ]
        biases.append(bias[:1])
    bias = jnp.concatenate(biases, axis=1)
    row = lax.broadcasted_iota(jnp.int32, (TAIL, 2 * channels), 0)
    rows_ref[3 * high :, :] = jnp.where(row == 0, bias, 0.0)
    half = keep_ref.shape[0]
    odd = lax.axis_index("lat") & 1
    keep_ref[...] = rows_ref[pl.ds(pl.multiple_of(odd * half, 16), half), :]
    send_ref[...] = rows_ref[pl.ds(pl.multiple_of((1 - odd) * half, 16), half), :].astype(BF16)


def assemble_kernel(scale, mine_ref, other_ref, out_ref, bias_ref, total_ref):
    channels = out_ref.shape[-1]
    half = mine_ref.shape[0]
    odd = lax.axis_index("lat") & 1
    for side, ref in ((odd, mine_ref), (1 - odd, other_ref)):
        total_ref[pl.ds(pl.multiple_of(side * half, 16), half), :] = ref[...].astype(F32) * scale
    high = 3 * channels
    for layer in range(2):
        for b in range(3):
            first = layer * high + b * channels
            pair = total_ref[first : first + channels, :]
            out_ref[layer, 0, b] = pair[:, :channels]
            out_ref[layer, 1, b] = pair[:, channels:]
            first = 2 * high + b * channels
            third = total_ref[first : first + channels, :]
            out_ref[layer, 2, b] = third[:, layer * channels : (layer + 1) * channels]
    bias = total_ref[3 * high : 3 * high + 1, :]
    bias_ref[0:1, :] = bias[:, :channels]
    bias_ref[1:2, :] = bias[:, channels:]


def partnered(block, devices, bit):
    return lax.ppermute(block, AXES, [(i, i ^ bit) for i in range(devices)])


def added(keep, send, devices):
    total = keep + partnered(send, devices, 1).astype(F32)
    bit = 2
    while True:
        rounded = total.astype(BF16)
        came = partnered(rounded, devices, bit)
        bit *= 2
        if bit >= devices:
            return rounded, came
        total = rounded.astype(F32) + came.astype(F32)


def exchanged(parts):
    return lax.all_to_all(parts, AXES, 0, 0, tiled=True)


def local(inputs, weights, biases, cotangent):
    channels, cols, lat_rows = inputs.shape
    lons, lats = lax.axis_size("lon"), lax.axis_size("lat")
    devices = lons * lats
    share = cols * cols // devices
    width = lat_rows // cols * share
    span = lats * width
    scale = 1.0 / math.sqrt(cols * lons * lat_rows * lats)
    blocks = lats if width % LANES == 0 else 1
    shape = jax.ShapeDtypeStruct

    chunks = 2 * channels // min(channels, 256 // cols)
    fields_shape = (devices, 2 * channels, width)
    hbm = pl.BlockSpec(memory_space=pltpu.HBM)
    vmem = pl.BlockSpec(memory_space=pltpu.VMEM)

    packed = pl.pallas_call(
        functools.partial(pack_kernel, share),
        out_shape=shape(fields_shape, BF16),
        in_specs=[hbm, hbm],
        out_specs=hbm,
        scratch_shapes=[
            pltpu.VMEM((2,) + inputs.shape, BF16),
            pltpu.VMEM(fields_shape, BF16),
            pltpu.SemaphoreType.DMA((2,)),
            pltpu.SemaphoreType.DMA((2,)),
        ],
        compiler_params=WIDE,
    )(inputs, cotangent)
    packed, weights = lax.optimization_barrier((packed, weights))
    first, rest = pl.pallas_call(
        kernels_kernel,
        out_shape=[
            shape((3 * channels, 3 * channels), BF16),
            shape((3, 3 * channels, 3 * channels), BF16),
        ],
        compiler_params=PARAMS,
    )(weights)
    parts = exchanged(packed)
    if blocks == 1:
        parts = parts.reshape(lons, lats, 2 * channels, width).transpose(0, 2, 1, 3)
        parts = parts.reshape(lons, 2 * channels, span)

    cells = (lons, channels, span)
    column = biases[:, :, None]
    fields, gated0, gated1 = pl.pallas_call(
        functools.partial(stack_kernel, share),
        out_shape=[shape(parts.shape, BF16), shape(cells, BF16), shape(cells, BF16)],
        out_specs=[hbm, vmem, vmem],
        scratch_shapes=[
            pltpu.VMEM(cells, BF16),
            pltpu.VMEM(cells, F32),
            pltpu.VMEM(cells, F32),
            pltpu.VMEM((lons, 3 * channels, span), F32),
            pltpu.VMEM(parts.shape, BF16),
            pltpu.SemaphoreType.DMA((lons + 1,)),
        ],
        compiler_params=PARAMS,
    )(parts, first, rest, column)
    if blocks == 1:
        fields = fields.reshape(lons, 2 * channels, lats, width).transpose(0, 2, 1, 3)
        fields = fields.reshape(fields_shape)
    home = exchanged(fields)

    rows = 9 * channels + TAIL
    half_shape = (rows // 2, 2 * channels)
    flops = 9 * channels * parts.size
    keep, send = pl.pallas_call(
        functools.partial(sums_kernel, share),
        out_shape=[shape(half_shape, F32), shape(half_shape, BF16)],
        scratch_shapes=[
            pltpu.VMEM((rows, 2 * channels), F32),
            pltpu.VMEM(cells, BF16),
            pltpu.VMEM((lons, 3 * channels, span), F32),
        ],
        compiler_params=PARAMS,
        cost_estimate=pl.CostEstimate(flops=flops, bytes_accessed=3 * parts.size, transcendentals=0),
    )(parts, first, column, gated0, gated1)
    rounded, came = added(keep, send, devices)
    def unpacked(field, parts):
        return pl.pallas_call(
            functools.partial(unpack_kernel, share, field),
            out_shape=shape(inputs.shape, BF16),
            out_specs=hbm,
            scratch_shapes=[
                pltpu.VMEM(inputs.shape, BF16),
                pltpu.SemaphoreType.DMA((chunks // 2,)),
            ],
            compiler_params=PARAMS,
            cost_estimate=pl.CostEstimate(
                flops=2 * inputs.size * lat_rows, bytes_accessed=4 * inputs.size, transcendentals=0
            ),
        )(parts)

    features_out = unpacked(0, home)
    came, features_out, home = lax.optimization_barrier((came, features_out, home))
    grad_input = unpacked(1, home)
    mine = (rounded.astype(F32) + came.astype(F32)).astype(BF16)
    other = partnered(mine, devices, 1)
    weight_grads, bias_grads = pl.pallas_call(
        functools.partial(assemble_kernel, scale),
        out_shape=[shape(weights.shape, F32), shape(biases.shape, F32)],
        scratch_shapes=[pltpu.VMEM((rows, 2 * channels), F32)],
        compiler_params=PARAMS,
    )(mine, other)
    return features_out, grad_input, weight_grads, bias_grads


def solution(mesh):
    in_specs = (P(None, "lon", "lat"), P(), P(), P(None, "lon", "lat"))
    out_specs = (P(None, "lon", "lat"), P(None, "lon", "lat"), P(), P())
    return jax.shard_map(local, mesh=mesh, in_specs=in_specs, out_specs=out_specs, check_vma=False)
```
